32 devices in a mesh: section: 4 (over x, core), dp: 8 (over z, y).
Axes of the slice: x: 2, y: 2, z: 4, core: 2. Of those that a mesh axis runs over, the one named last changes fastest.
Arguments:
- inputs: float32 [65536, 256], P('dp'), may hold values from -6 to 6
- targets: float32 [4, 65536, 256], P('section', 'dp'), may hold values from -6 to 6
- lengths: int32 [65536], P('dp'), may hold values from 1 to 4, as said below
- lat_index: int32 [65536], P('dp'), may hold values from 0 to 127
- land: int32 [65536], P('dp'), may hold values from 0 to 1
- w_up: float32 [4, 2, 256, 256], P('section'), may hold values from -0.375 to 0.375
- w_down: float32 [4, 2, 256, 256], P('section'), may hold values from -0.375 to 0.375
- gains: float32 [4, 2, 256], P('section'), may hold values from 0.5 to 1.5
- m_up: float32 [4, 2, 256, 256], P('section'), may hold values from -7.6293945e-05 to 7.6293945e-05
- m_down: float32 [4, 2, 256, 256], P('section'), may hold values from -7.6293945e-05 to 7.6293945e-05
- m_gains: float32 [4, 2, 256], P('section'), may hold values from -0.00024414062 to 0.00024414062
- v_up: float32 [4, 2, 256, 256], P('section'), may hold values from 2.3795382e-12 to 9.518153e-12
- v_down: float32 [4, 2, 256, 256], P('section'), may hold values from 2.3795382e-12 to 9.518153e-12
- v_gains: float32 [4, 2, 256], P('section'), may hold values from 2.1415845e-11 to 8.566338e-11
Outputs:
- loss_sum: float32 [], replicated
- weight_sum: float32 [], replicated
- grad_norm: float32 [], replicated
- new_up: float32 [4, 2, 256, 256], P('section')
- new_down: float32 [4, 2, 256, 256], P('section')
- new_gains: float32 [4, 2, 256], P('section')
- new_m_up: float32 [4, 2, 256, 256], P('section')
- new_m_down: float32 [4, 2, 256, 256], P('section')
- new_m_gains: float32 [4, 2, 256], P('section')
- new_v_up: float32 [4, 2, 256, 256], P('section')
- new_v_down: float32 [4, 2, 256, 256], P('section')
- new_v_gains: float32 [4, 2, 256], P('section')
The draws below stay inside these ranges and needn't reach their ends.
Inputs may be any that keep to these rules, and one draw needn't show every extreme that they name: `lengths`: some column has length 4.
All inputs are finite; a program needn't handle non-finite values.
Results may differ from the reference program's by a relative error of at most 0.0035.
Values sent between devices are 32-bit elements; how exact they have to be, the bound alone decides.
A program may use at most 128 MiB of HBM per device.

```python
import math
import jax
import jax.numpy as jnp
from jax import lax

D = 256
H = 256
LAYERS = 2
NLAT = 128
STEP = 10
SECTIONS = 4
COLS = 65536
PARAMS = 1050624


def latitude_rows(key):
    rows = jax.random.randint(key, (COLS,), 0, NLAT)
    first = jax.random.randint(jax.random.fold_in(key, 1), (), 0, COLS)
    offset = jax.random.randint(jax.random.fold_in(key, 2), (), 1, COLS)
    rows = rows.at[first].set(0)
    rows = rows.at[(first + offset) % COLS].set(NLAT - 1)
    return rows.astype(jnp.int32)


def polar_flags(rows):
    band = NLAT // 16
    return (rows < band) | (rows >= NLAT - band)


def draw_lengths(key, part):
    key = jax.random.fold_in(key, 7)
    values = jax.random.randint(key, (COLS,), 1, SECTIONS + 1)
    picked = jax.random.randint(jax.random.fold_in(key, 1), (), 0, COLS)
    values = values.at[picked].set(SECTIONS)
    return values.astype(jnp.int32)


def draw_lat_index(key, part):
    return latitude_rows(key)


def draw_land(key, part):
    polar = polar_flags(latitude_rows(key))
    key = jax.random.fold_in(key, 11)
    coin = jax.random.randint(key, (COLS,), 0, 10)
    ones = (coin < 3).astype(jnp.int32)
    return jnp.where(polar, 1, ones).astype(jnp.int32)


def draw_targets(key, part):
    polar = polar_flags(latitude_rows(key))
    key = jax.random.fold_in(key, 13)
    spread = jnp.where(polar, 3.0, 1.0).astype(jnp.float32)[None, :, None]
    base = jax.random.normal(key, (SECTIONS, COLS, D), jnp.float32)
    return jnp.clip(base * spread, -6.0, 6.0).astype(jnp.float32)


def block_levels(stream_key, shape, shards, low, largest):
    def one(axis_at, parts):
        steps = jax.random.uniform(jax.random.fold_in(jax.random.fold_in(stream_key, 6), axis_at), (parts,), jnp.float32, low / len(shards), largest / len(shards))
        return jnp.repeat(jnp.exp(steps), shape[axis_at] // parts).reshape((-1,) + (1,) * (len(shape) - axis_at - 1))

    gain = one(*shards[0])
    for cut in shards[1:]:
        gain = gain * one(*cut)
    return gain


def normal_values(key, dims, scale, bound, pieces=(), kind=jnp.bfloat16):
    entries = scale * jax.random.normal(key, dims, jnp.float32)
    if pieces:
        entries = entries * block_levels(key, dims, pieces, -0.22, 0.18)
    return jnp.clip(entries, -bound, bound).astype(kind)


def setup_inputs(seed: int = 0) -> dict:
    key_of = jax.random.split(jax.random.key(seed), 15)
    return {
        "inputs": normal_values(key_of[0], (COLS, D), 1.0, 6.0, ((0, 8),), jnp.float32),
        "targets": draw_targets(jax.random.fold_in(key_of[14], 71), 0),
        "lengths": draw_lengths(jax.random.fold_in(key_of[14], 71), 0),
        "lat_index": draw_lat_index(jax.random.fold_in(key_of[14], 71), 0),
        "land": draw_land(jax.random.fold_in(key_of[14], 71), 0),
        "w_up": normal_values(key_of[5], (SECTIONS, LAYERS, D, H), D ** -0.5, 0.375, ((0, 4),), jnp.float32),
        "w_down": normal_values(key_of[6], (SECTIONS, LAYERS, H, D), H ** -0.5, 0.375, ((0, 4),), jnp.float32),
        "gains": jnp.clip(1.0 + 0.1 * jax.random.normal(key_of[7], (SECTIONS, LAYERS, D), jnp.float32), 0.5, 1.5),
        "m_up": normal_values(key_of[8], (SECTIONS, LAYERS, D, H), (0.0055 * PARAMS ** -0.5), 7.62939453125e-05, ((0, 4),), jnp.float32),
        "m_down": normal_values(key_of[9], (SECTIONS, LAYERS, H, D), (0.0055 * PARAMS ** -0.5), 7.62939453125e-05, ((0, 4),), jnp.float32),
        "m_gains": normal_values(key_of[10], (SECTIONS, LAYERS, D), (0.0165 * PARAMS ** -0.5), 0.00024414062, ((0, 4),), jnp.float32),
        "v_up": jnp.clip(jnp.exp(math.log(9.518152759013798e-12) - 1.3862944 * jax.random.uniform(key_of[11], (SECTIONS, LAYERS, D, H), jnp.float32) ** block_levels(key_of[11], (SECTIONS, LAYERS, D, H), ((0, 4),), -0.2, 0.2)), 2.3795381897534496e-12, 9.518152759013798e-12),
        "v_down": jnp.clip(jnp.exp(math.log(9.518152759013798e-12) - 1.3862944 * jax.random.uniform(key_of[12], (SECTIONS, LAYERS, H, D), jnp.float32) ** block_levels(key_of[12], (SECTIONS, LAYERS, H, D), ((0, 4),), -0.2, 0.2)), 2.3795381897534496e-12, 9.518152759013798e-12),
        "v_gains": jnp.clip(jnp.exp(math.log(8.566337916793287e-11) - 1.3862944 * jax.random.uniform(key_of[13], (SECTIONS, LAYERS, D), jnp.float32) ** block_levels(key_of[13], (SECTIONS, LAYERS, D), ((0, 4),), -0.2, 0.2)), 2.141584479198322e-11, 8.566337916793287e-11),
    }


@jax.custom_vjp
def low(v):
    return lax.optimization_barrier(v.astype(jnp.bfloat16)).astype(jnp.float32)

@jax.custom_vjp
def low_back(v):
    return v

def low_keep(v):
    return (low(v), None)

def low_pass(kept, grad):
    return (grad,)

def back_keep(v):
    return (v, None)

def back_low(kept, grad):
    return (low(grad),)
low.defvjp(low_keep, low_pass)
low_back.defvjp(back_keep, back_low)
norm_eps = 1e-06
clip_limit = 0.05
beta_one = 0.9
beta_two = 0.999
adam_eps = 1e-08
learn_rate = 0.1
weight_decay = 0.01

def area_weight(lat_index, land):
    latitude = (lat_index.astype(jnp.float32) + 0.5) * (math.pi / NLAT) - math.pi / 2
    return jnp.cos(latitude) * (1.0 + land.astype(jnp.float32))

def column_block(state, up_one, down_one, gain_one):
    scale_inv = lax.rsqrt(lax.optimization_barrier(jnp.mean(state * state, -1, keepdims=True)) + norm_eps)
    normed = low(state * scale_inv * gain_one)
    pre_act = low_back(jnp.dot(normed, low(up_one), precision=lax.Precision.HIGHEST))
    hidden = low(jax.nn.silu(pre_act))
    branch = low_back(jnp.dot(hidden, low(down_one), precision=lax.Precision.HIGHEST))
    return state + branch

def adam_step(weights_old, gradient, moment_one, moment_two, decay_rate):
    moment_one = beta_one * moment_one + (1.0 - beta_one) * gradient
    moment_two = beta_two * moment_two + (1.0 - beta_two) * gradient * gradient
    first_hat = moment_one / (1.0 - beta_one ** STEP)
    second_hat = moment_two / (1.0 - beta_two ** STEP)
    new_weights = weights_old - learn_rate * (first_hat / (jnp.sqrt(second_hat) + adam_eps) + decay_rate * weights_old)
    return (new_weights, moment_one, moment_two)

def reference(inputs, targets, lengths, lat_index, land, w_up, w_down, gains, m_up, m_down, m_gains, v_up, v_down, v_gains):
    area = area_weight(lat_index, land)
    section_ids = jnp.arange(SECTIONS, dtype=jnp.int32)
    live = (section_ids[:, None] < lengths[None, :]).astype(jnp.float32)
    loss_weight = live * area[None, :]
    weight_sum = jnp.sum(loss_weight)
    block_rows = min(4096, COLS)
    block_count = COLS // block_rows

    def total_loss(params):
        up_all, down_all, gain_all = params

        def one_block(block_id):
            start = (block_id * block_rows).astype(jnp.int32)
            state = lax.dynamic_slice_in_dim(inputs, start, block_rows, 0)
            accumulated = jnp.zeros((), jnp.float32)
            for section_id in range(SECTIONS):
                for layer_id in range(LAYERS):
                    state = column_block(state, up_all[section_id, layer_id], down_all[section_id, layer_id], gain_all[section_id, layer_id])
                target_rows = lax.dynamic_slice_in_dim(targets[section_id], start, block_rows, 0)
                weight_rows = lax.dynamic_slice_in_dim(loss_weight[section_id], start, block_rows, 0)
                diff = state - target_rows
                accumulated = accumulated + jnp.sum(weight_rows * lax.optimization_barrier(jnp.sum(diff * diff, -1)))
            return accumulated
        return jnp.sum(lax.map(jax.checkpoint(one_block), jnp.arange(block_count, dtype=jnp.int32)))
    loss_sum, pullback = jax.vjp(total_loss, (w_up, w_down, gains))
    grads = pullback(1.0 / weight_sum)[0]
    squares = sum((jnp.sum(g * g) for g in grads))
    grad_norm = jnp.sqrt(squares)
    clip_scale = jnp.minimum(1.0, clip_limit / grad_norm)
    g_up, g_down, g_gain = [g * clip_scale for g in grads]
    new_up, new_m_up, new_v_up = adam_step(w_up, g_up, m_up, v_up, weight_decay)
    new_down, new_m_down, new_v_down = adam_step(w_down, g_down, m_down, v_down, weight_decay)
    new_gains, new_m_gains, new_v_gains = adam_step(gains, g_gain, m_gains, v_gains, 0.0)
    return (loss_sum, weight_sum, grad_norm, new_up, new_down, new_gains, new_m_up, new_m_down, new_m_gains, new_v_up, new_v_down, new_v_gains)
```

```python
import functools
import math

import jax
import jax.numpy as jnp
from jax import lax
from jax.experimental import pallas as pl
from jax.experimental.pallas import tpu as pltpu
from jax.sharding import PartitionSpec as P

MICRO = 8
NLAT = 128
STEP = 10

norm_eps = 1e-06
clip_limit = 0.05
beta_one = 0.9
beta_two = 0.999
adam_eps = 1e-08
learn_rate = 0.1
weight_decay = 0.01

f32, bf16 = jnp.float32, jnp.bfloat16
MESH = pl.DeviceIdType.MESH
LANES = 128
ROWS = 512
WINDOW = 1536
RING = 11
QRING = 8


def dot(a, b):
    return jnp.dot(a, b, preferred_element_type=f32)


def dot_lhs_t(a, b):
    return lax.dot_general(a, b, (((0,), (0,)), ((), ())), preferred_element_type=f32)


def split_dot(product, onehot, values):
    high = values.astype(bf16)
    low = (values - high.astype(f32)).astype(bf16)
    return product(onehot, high) + product(onehot, low)


def rollout_kernel(
    sections,
    groups,
    inputs_ref,
    target_ref,
    len_ref,
    lat_ref,
    land_ref,
    up_ref,
    down_ref,
    gain_ref,
    dup_ref,
    ddown_ref,
    dgain_ref,
    stat_ref,
    xin,
    xout,
    cin,
    tgt,
    packed,
    save_x,
    save_h,
    save_d,
    qring,
    up_lo,
    up_t,
    down_lo,
    down_t,
    rank_ref,
    q_ref,
    scale_ref,
    loss_acc,
    gain_acc,
    wbuf,
    spread,
    in_sem,
    tgt_sem,
    st_send,
    st_recv,
    ct_send,
    ct_recv,
    w_send,
    w_recv,
):
    section = lax.axis_index("section")
    dp = lax.axis_index("dp")
    columns = xin.shape[0]
    feats = xin.shape[1]
    chunks = columns // ROWS
    live_rows = ROWS * (sections - 2) // sections
    prows = live_rows + 16
    total_packed = chunks * prows
    expand = live_rows + 512
    natural = section < 2
    last = sections - 1

    barrier = pltpu.get_barrier_semaphore()

    @pl.when(section > 0)
    def _():
        pl.semaphore_signal(barrier, inc=1, device_id=(section - 1, dp), device_id_type=MESH)

    @pl.when(section < last)
    def _():
        pl.semaphore_signal(barrier, inc=1, device_id=(section + 1, dp), device_id_type=MESH)

    for step in range(1, groups):
        pl.semaphore_signal(
            barrier, inc=1, device_id=(section, lax.rem(dp + step, groups)), device_id_type=MESH
        )

    def rows_at(index, size, align=16):
        return pl.ds(pl.multiple_of(index, align), size)

    def input_copy(i):
        rows = rows_at(i * ROWS, ROWS)
        return pltpu.make_async_copy(inputs_ref.at[rows], xin.at[rows], in_sem.at[i])

    def target_copy(i):
        rows = rows_at(i * ROWS, ROWS)
        return pltpu.make_async_copy(target_ref.at[rows], tgt.at[rows], tgt_sem.at[i])

    @pl.when(section == 0)
    def _():
        @pl.loop(0, chunks)
        def _(i):
            input_copy(i).start()

    @pl.loop(0, chunks)
    def _(i):
        target_copy(i).start()

    for layer in range(2):
        up = up_ref[layer]
        down = down_ref[layer]
        up_lo[layer] = (0.5 * up).astype(bf16)
        down_lo[layer] = down.astype(bf16)
        up_t[layer] = up.T.astype(bf16)
        down_t[layer] = (0.5 * down).T.astype(bf16)
        dup_ref[layer] = jnp.zeros((feats, feats), f32)
        ddown_ref[layer] = jnp.zeros((feats, feats), f32)
        gain_acc[layer] = jnp.zeros((8, feats), f32)
    loss_acc[...] = jnp.zeros_like(loss_acc)

    grid_rows = columns // LANES
    length = len_ref[...]
    latitude = (lat_ref[...].astype(f32) + 0.5) * (math.pi / NLAT) - math.pi / 2
    area = jnp.cos(latitude) * (1.0 + land_ref[...].astype(f32))
    q_ref[...] = area * (section < length).astype(f32)
    local_weight = jnp.sum(
        area * jnp.minimum(length, sections).astype(f32), axis=(0, 1), keepdims=True
    )
    beyond = length > 2
    flag = beyond.astype(bf16)
    lane_a = lax.broadcasted_iota(jnp.int32, (LANES, LANES), 0)
    lane_b = lax.broadcasted_iota(jnp.int32, (LANES, LANES), 1)
    within = dot(flag, (lane_a < lane_b).astype(bf16))
    row_total = jnp.sum(flag.astype(f32), axis=1, keepdims=True)
    row_a = lax.broadcasted_iota(jnp.int32, (grid_rows, grid_rows), 0)
    row_b = lax.broadcasted_iota(jnp.int32, (grid_rows, grid_rows), 1)
    before = dot(
        (row_b < row_a).astype(bf16), jnp.broadcast_to(row_total, (grid_rows, LANES)).astype(bf16)
    )
    rank = jnp.where(beyond, within + before, -1e6)
    rank_ref[...] = rank

    def window_start(j):
        first = (j * (prows * sections) // (sections - 2) - 448) // LANES * LANES
        return jnp.clip(first, 0, columns - WINDOW)

    def expand_start(k):
        return jnp.clip(live_rows * k - 256, 0, total_packed - expand)

    place = (
        lax.broadcasted_iota(jnp.int32, (grid_rows, LANES), 0) * LANES
        + lax.broadcasted_iota(jnp.int32, (grid_rows, LANES), 1)
    )
    rank_i = rank.astype(jnp.int32)
    missed = beyond & (rank_i >= total_packed)
    for j in range(chunks):
        start = min(
            max((j * (prows * sections) // (sections - 2) - 448) // LANES * LANES, 0),
            columns - WINDOW,
        )
        member = (rank_i >= j * prows) & (rank_i < (j + 1) * prows)
        missed |= member & ((place < start) | (place >= start + WINDOW))
    row_chunk = lax.broadcasted_iota(jnp.int32, (grid_rows, LANES), 0) // (ROWS // LANES)
    row_start = jnp.clip(live_rows * row_chunk - 256, 0, total_packed - expand)
    missed |= beyond & ((rank_i < row_start) | (rank_i >= row_start + expand))
    misses = jnp.sum(missed.astype(f32), axis=(0, 1), keepdims=True)
    tile_row = lax.broadcasted_iota(jnp.int32, (8, LANES), 0)
    wbuf[dp] = jnp.where(tile_row < 4, local_weight, misses)

    chain = jnp.where((section > 0) & (section < last), 2, 1)
    pl.semaphore_wait(barrier, groups - 1 + chain)

    def weight_copy(step):
        return pltpu.make_async_remote_copy(
            src_ref=wbuf.at[dp],
            dst_ref=wbuf.at[dp],
            send_sem=w_send.at[step],
            recv_sem=w_recv.at[step],
            device_id=(section, lax.rem(dp + step, groups)),
            device_id_type=MESH,
        )

    for step in range(1, groups):
        weight_copy(step).start()

    def finish_weights():
        for step in range(1, groups):
            weight_copy(step).wait_recv()
        total = wbuf[0]
        for peer in range(1, groups):
            total = total + wbuf[peer]
        stat_ref[...] = total
        scale_ref[...] = 2.0 / jnp.broadcast_to(total[0:1], (8, LANES))

    def pack_matrix(j):
        start = window_start(j)
        base = (j * prows).astype(f32)
        target_row = lax.broadcasted_iota(jnp.int32, (prows, LANES), 0).astype(f32)
        first = start // LANES
        hits = []
        for i in range(WINDOW // LANES):
            hits.append(target_row == rank_ref[pl.ds(first + i, 1), :] - base)
        return start, first, hits

    def as_onehot(hits):
        return jnp.concatenate([jnp.where(hit, 1.0, 0.0).astype(bf16) for hit in hits], axis=1)

    def unpack_rows(k):
        start = expand_start(k)
        base = start.astype(f32)
        source_row = lax.broadcasted_iota(jnp.int32, (expand, LANES), 0).astype(f32)
        hits = []
        for i in range(ROWS // LANES):
            hits.append(source_row == rank_ref[pl.ds(k * (ROWS // LANES) + i, 1), :] - base)
        return split_dot(dot_lhs_t, as_onehot(hits), cin[rows_at(start, expand), :])

    def forward(size, rows, saved):
        x = xin[rows, :]
        for layer in range(2):
            if layer == 1:
                save_x[saved, :] = x
            r = lax.rsqrt(jnp.mean(x * x, -1, keepdims=True) + norm_eps)
            normed = (x * r * gain_ref[layer : layer + 1]).astype(bf16)
            half = dot(normed, up_lo[layer])
            t = jnp.tanh(half)
            a = 1.0 + t
            h = half * a
            hidden = h.astype(bf16)
            save_h[layer, saved, :] = hidden
            save_d[layer, saved, :] = (a + h * (1.0 - t)).astype(bf16)
            x = x + dot(hidden, down_lo[layer])
        xout[rows, :] = x

    def loss_part(size, diff, weight):
        weighted = jnp.concatenate(
            [diff[:, :LANES] * weight, diff[:, LANES:] * weight], axis=1
        )
        loss_acc[...] += jnp.sum((weighted * diff).reshape(size // 8, 8, feats), 0)
        return weighted * scale_ref[0:1, 0:1]

    def backward(size, rows, saved, g):
        for layer in (1, 0):
            low = g.astype(bf16)
            ddown_ref[layer] += dot_lhs_t(save_h[layer, saved, :], low)
            pull = dot(low, down_t[layer])
            g_pre = (pull * save_d[layer, saved, :].astype(f32)).astype(bf16)
            x = save_x[saved, :] if layer == 1 else xin[rows, :]
            r = lax.rsqrt(jnp.mean(x * x, -1, keepdims=True) + norm_eps)
            gain = gain_ref[layer : layer + 1]
            xr = x * r
            normed = (xr * gain).astype(bf16)
            dup_ref[layer] += dot_lhs_t(normed, g_pre)
            g_normed = dot(g_pre, up_t[layer])
            prod = g_normed * xr
            gain_acc[layer] += jnp.sum(prod.reshape(size // 8, 8, feats), 0)
            mean = jnp.mean(prod * gain, -1, keepdims=True)
            g = g + r * (gain * g_normed - xr * mean)
        xin[rows, :] = g

    def state_copy(source, size, i):
        rows = rows_at(i * size, size)
        return pltpu.make_async_remote_copy(
            src_ref=source.at[rows],
            dst_ref=xin.at[rows],
            send_sem=st_send.at[i],
            recv_sem=st_recv.at[i],
            device_id=(jnp.minimum(section + 1, last), dp),
            device_id_type=MESH,
        )

    def cot_copy(size, i):
        rows = rows_at(i * size, size)
        return pltpu.make_async_remote_copy(
            src_ref=xin.at[rows],
            dst_ref=cin.at[rows],
            send_sem=ct_send.at[i],
            recv_sem=ct_recv.at[i],
            device_id=(jnp.maximum(section - 1, 0), dp),
            device_id_type=MESH,
        )

    @pl.when(natural)
    def _():
        lag = jnp.where(section == 0, RING - 1, RING - 3)

        @pl.loop(0, chunks + RING - 1)
        def _(t):
            @pl.when(t < chunks)
            def _():
                @pl.when(section == 0)
                def _():
                    input_copy(t).wait()

                @pl.when(section > 0)
                def _():
                    state_copy(xout, ROWS, t).wait_recv()

                rows = rows_at(t * ROWS, ROWS)
                saved = rows_at(lax.rem(t, RING) * ROWS, ROWS)
                forward(ROWS, rows, saved)

                @pl.when(section == 0)
                def _():
                    state_copy(xout, ROWS, t).start()

            @pl.when((section == 1) & (t >= 2) & (t < chunks + 2))
            def _():
                j = t - 2
                start, _, hits = pack_matrix(j)
                packed[rows_at(j * prows, prows), :] = split_dot(
                    dot, as_onehot(hits), xout[rows_at(start, WINDOW), :]
                )
                state_copy(packed, prows, j).start()

            k = t - lag

            @pl.when((k >= 0) & (k < chunks))
            def _():
                @pl.when(k == 0)
                def _():
                    finish_weights()

                @pl.when(section == 0)
                def _():
                    cot_copy(ROWS, k).wait_recv()

                @pl.when((section == 1) & (k == 0))
                def _():
                    cot_copy(prows, k).wait_recv()
                    cot_copy(prows, k + 1).wait_recv()
                    cot_copy(prows, k + 2).wait_recv()

                @pl.when((section == 1) & (k >= 2) & (k + 1 < chunks))
                def _():
                    cot_copy(prows, k + 1).wait_recv()

                target_copy(k).wait()
                rows = rows_at(k * ROWS, ROWS)
                saved = rows_at(lax.rem(k, RING) * ROWS, ROWS)

                @pl.when(section == 1)
                def _():
                    cin_rows = unpack_rows(k)
                    spread[...] = cin_rows

                @pl.when(section == 0)
                def _():
                    spread[...] = cin[rows, :]

                weight = jnp.concatenate(
                    [
                        jnp.broadcast_to(
                            q_ref[pl.ds(k * (ROWS // LANES) + i, 1), :], (LANES, LANES)
                        ).T
                        for i in range(ROWS // LANES)
                    ],
                    axis=0,
                )
                diff = xout[rows, :] - tgt[rows, :]
                g = loss_part(ROWS, diff, weight) + spread[...]
                backward(ROWS, rows, saved, g)

                @pl.when(section == 1)
                def _():
                    cot_copy(ROWS, k).start()

        @pl.when(section == 0)
        def _():
            @pl.loop(0, chunks)
            def _(i):
                state_copy(xout, ROWS, i).wait_send()

        @pl.when(section == 1)
        def _():
            @pl.loop(0, chunks)
            def _(i):
                state_copy(packed, prows, i).wait_send()
                cot_copy(ROWS, i).wait_send()

    @pl.when(jnp.logical_not(natural))
    def _():
        lag = last - section

        @pl.loop(0, chunks + lag)
        def _(t):
            @pl.when(t < chunks)
            def _():
                @pl.when(t == 0)
                def _():
                    target_copy(0).wait()
                    target_copy(1).wait()

                @pl.when(t + 2 < chunks)
                def _():
                    target_copy(t + 2).wait()

                start, first, hits = pack_matrix(t)
                rows = rows_at(t * prows, prows)
                packed[rows, :] = split_dot(dot, as_onehot(hits), tgt[rows_at(start, WINDOW), :])
                weight = jnp.zeros((prows, LANES), f32)
                for i, hit in enumerate(hits):
                    weight += jnp.where(hit, q_ref[pl.ds(first + i, 1), :], 0.0)
                qring[lax.rem(t, QRING)] = jnp.broadcast_to(
                    jnp.sum(weight, -1, keepdims=True), (prows, LANES)
                )
                state_copy(xout, prows, t).wait_recv()
                saved = rows_at(lax.rem(t, RING) * ROWS, prows)
                forward(prows, rows, saved)

                @pl.when(section < last)
                def _():
                    state_copy(xout, prows, t).start()

            k = t - lag

            @pl.when(k >= 0)
            def _():
                @pl.when(k == 0)
                def _():
                    finish_weights()

                rows = rows_at(k * prows, prows)
                saved = rows_at(lax.rem(k, RING) * ROWS, prows)
                diff = xout[rows, :] - packed[rows, :]
                spread[0:prows, :] = loss_part(prows, diff, qring[lax.rem(k, QRING)])

                @pl.when(section < last)
                def _():
                    cot_copy(prows, k).wait_recv()
                    spread[0:prows, :] += cin[rows, :]

                backward(prows, rows, saved, spread[0:prows, :])
                cot_copy(prows, k).start()

        @pl.loop(0, chunks)
        def _(i):
            cot_copy(prows, i).wait_send()

        @pl.when(section < last)
        def _():
            @pl.loop(0, chunks)
            def _(i):
                state_copy(xout, prows, i).wait_send()

    for step in range(1, groups):
        weight_copy(step).wait_send()
    for layer in range(2):
        dgain_ref[layer : layer + 1, :] = jnp.sum(gain_acc[layer], 0, keepdims=True)
    loss = jnp.sum(loss_acc[...], axis=(0, 1), keepdims=True)
    stat_ref[...] = jnp.where(tile_row < 2, loss, stat_ref[...])


def rollout(inputs, target, lengths, lat_index, land, w_up, w_down, gains, sections, groups):
    columns, feats = inputs.shape
    chunks = columns // ROWS
    prows = ROWS * (sections - 2) // sections + 16
    grid_rows = columns // LANES
    hbm = pl.BlockSpec(memory_space=pl.ANY)
    vmem = pl.BlockSpec(memory_space=pltpu.VMEM)
    square = jax.ShapeDtypeStruct((2, feats, feats), f32)
    dma = pltpu.SemaphoreType.DMA
    wide = pltpu.VMEM((columns, feats), f32)
    lows = pltpu.VMEM((2, feats, feats), bf16)
    flat = lambda array: array.reshape(grid_rows, LANES)
    return pl.pallas_call(
        functools.partial(rollout_kernel, sections, groups),
        out_shape=(
            square,
            square,
            jax.ShapeDtypeStruct((2, feats), f32),
            jax.ShapeDtypeStruct((8, LANES), f32),
        ),
        in_specs=[hbm, hbm] + [vmem] * 6,
        out_specs=(vmem,) * 4,
        scratch_shapes=[
            wide,
            wide,
            wide,
            wide,
            pltpu.VMEM((chunks * prows, feats), f32),
            pltpu.VMEM((RING * ROWS, feats), f32),
            pltpu.VMEM((2, RING * ROWS, feats), bf16),
            pltpu.VMEM((2, RING * ROWS, feats), bf16),
            pltpu.VMEM((QRING, prows, LANES), f32),
            lows,
            lows,
            lows,
            lows,
            pltpu.VMEM((grid_rows, LANES), f32),
            pltpu.VMEM((grid_rows, LANES), f32),
            pltpu.VMEM((8, LANES), f32),
            pltpu.VMEM((8, feats), f32),
            pltpu.VMEM((2, 8, feats), f32),
            pltpu.VMEM((groups, 8, LANES), f32),
            pltpu.VMEM((ROWS, feats), f32),
            dma((chunks,)),
            dma((chunks,)),
            dma((chunks,)),
            dma((chunks,)),
            dma((chunks,)),
            dma((chunks,)),
            dma((groups,)),
            dma((groups,)),
        ],
        compiler_params=pltpu.CompilerParams(
            collective_id=0, has_side_effects=True, vmem_limit_bytes=63 * 1024 * 1024
        ),
        name="rollout",
    )(
        inputs,
        target,
        flat(lengths),
        flat(lat_index),
        flat(land),
        w_up,
        w_down,
        gains,
    )


def shifted(shard, axis, by):
    size = lax.axis_size(axis)
    pairs = [(i, i + by) for i in range(size) if 0 <= i + by < size]
    return lax.ppermute(shard, axis, pairs)


def area_weight(lat_index, land):
    latitude = (lat_index.astype(jnp.float32) + 0.5) * (math.pi / NLAT) - math.pi / 2
    return jnp.cos(latitude) * (1.0 + land.astype(jnp.float32))


def norm_part(state, gain_one):
    scale_inv = lax.rsqrt(jnp.mean(state * state, -1, keepdims=True) + norm_eps)
    return state * scale_inv * gain_one


def block_forward(state, up_one, down_one, gain_one):
    normed = norm_part(state, gain_one).astype(jnp.bfloat16)
    pre_act = jnp.dot(normed, up_one, preferred_element_type=jnp.float32)
    hidden = jax.nn.silu(pre_act).astype(jnp.bfloat16)
    branch = jnp.dot(hidden, down_one, preferred_element_type=jnp.float32)
    return (state + branch, normed, pre_act, hidden)


def block_backward(state, normed, pre_act, hidden, up_one, down_one, gain_one, cotangent):
    grad_low = cotangent.astype(jnp.bfloat16)
    grad_down = jnp.dot(hidden.T, grad_low, preferred_element_type=jnp.float32)
    grad_hidden = jnp.dot(grad_low, down_one.T, preferred_element_type=jnp.float32)
    sigmoid_pre = jax.nn.sigmoid(pre_act)
    grad_pre = (grad_hidden * sigmoid_pre * (1.0 + pre_act * (1.0 - sigmoid_pre))).astype(
        jnp.bfloat16
    )
    grad_up = jnp.dot(normed.T, grad_pre, preferred_element_type=jnp.float32)
    grad_normed = jnp.dot(grad_pre, up_one.T, preferred_element_type=jnp.float32)
    unused, norm_pull = jax.vjp(norm_part, state, gain_one)
    grad_state, grad_gain = norm_pull(grad_normed)
    return (cotangent + grad_state, grad_up, grad_down, grad_gain)


def plain_gradients(inputs, target_all, loss_weight, weight_sum, up_low, down_low, gain_all):
    section_id = lax.axis_index("section")
    section_count = lax.axis_size("section")
    micro_rows = inputs.shape[0] // MICRO
    layer_count = up_low.shape[0]
    tick_count = MICRO + section_count - 1

    def take_rows(array, slot_id):
        return lax.dynamic_slice_in_dim(array, slot_id * micro_rows, micro_rows, 0)

    def forward_tick(time_step, state_carry):
        received, saved, accumulated = state_carry
        micro_id = time_step - section_id
        is_valid = (micro_id >= 0) & (micro_id < MICRO)
        slot_id = jnp.clip(micro_id, 0, MICRO - 1)
        state = jnp.where(section_id == 0, take_rows(inputs, slot_id), received)
        kept_in = jnp.where(is_valid, state, saved[slot_id])
        saved = lax.dynamic_update_index_in_dim(saved, kept_in, slot_id, 0)
        moved = state
        for layer_id in range(layer_count):
            moved = block_forward(moved, up_low[layer_id], down_low[layer_id], gain_all[layer_id])[
                0
            ]
        diff = moved - take_rows(target_all, slot_id)
        term = jnp.sum(take_rows(loss_weight, slot_id) * jnp.sum(diff * diff, -1))
        accumulated = accumulated + jnp.where(is_valid, term, 0.0)
        received = shifted(moved, "section", 1)
        return (received, saved, accumulated)

    start_carry = (
        jnp.zeros((micro_rows, inputs.shape[1]), jnp.float32),
        jnp.zeros((MICRO, micro_rows, inputs.shape[1]), jnp.float32),
        jnp.zeros((), jnp.float32),
    )
    received, saved, local_loss = lax.fori_loop(0, tick_count, forward_tick, start_carry)

    def backward_tick(time_step, state_carry):
        received, sum_up, sum_down, sum_gain = state_carry
        micro_id = time_step - (section_count - 1 - section_id)
        is_valid = (micro_id >= 0) & (micro_id < MICRO)
        slot_id = jnp.clip(micro_id, 0, MICRO - 1)
        state = saved[slot_id]
        kept_layers = []
        for layer_id in range(layer_count):
            next_state, normed, pre_act, hidden = block_forward(
                state, up_low[layer_id], down_low[layer_id], gain_all[layer_id]
            )
            kept_layers.append((state, normed, pre_act, hidden))
            state = next_state
        cotangent = (
            2.0
            * take_rows(loss_weight, slot_id)[:, None]
            * (state - take_rows(target_all, slot_id))
            / weight_sum
            + received
        )
        ups = [None] * layer_count
        downs = [None] * layer_count
        gains_list = [None] * layer_count
        for layer_id in reversed(range(layer_count)):
            layer_in, normed, pre_act, hidden = kept_layers[layer_id]
            cotangent, ups[layer_id], downs[layer_id], gains_list[layer_id] = block_backward(
                layer_in,
                normed,
                pre_act,
                hidden,
                up_low[layer_id],
                down_low[layer_id],
                gain_all[layer_id],
                cotangent,
            )
        cotangent, ups, downs, gains_here = (
            cotangent,
            jnp.stack(ups),
            jnp.stack(downs),
            jnp.stack(gains_list),
        )
        live_factor = is_valid.astype(jnp.float32)
        sum_up = sum_up + live_factor * ups
        sum_down = sum_down + live_factor * downs
        sum_gain = sum_gain + live_factor * gains_here
        received = shifted(cotangent, "section", -1)
        return (received, sum_up, sum_down, sum_gain)

    back_carry = (
        jnp.zeros((micro_rows, inputs.shape[1]), jnp.float32),
        jnp.zeros(up_low.shape, jnp.float32),
        jnp.zeros(down_low.shape, jnp.float32),
        jnp.zeros(gain_all.shape, jnp.float32),
    )
    unused, grad_up, grad_down, grad_gain = lax.fori_loop(0, tick_count, backward_tick, back_carry)
    return grad_up, grad_down, grad_gain, local_loss


def adam_step(weights_old, gradient, moment_one, moment_two, decay_rate):
    moment_one = beta_one * moment_one + (1.0 - beta_one) * gradient
    moment_two = beta_two * moment_two + (1.0 - beta_two) * gradient * gradient
    first_hat = moment_one / (1.0 - beta_one**STEP)
    second_hat = moment_two / (1.0 - beta_two**STEP)
    new_weights = weights_old - learn_rate * (
        first_hat / (jnp.sqrt(second_hat) + adam_eps) + decay_rate * weights_old
    )
    return (new_weights, moment_one, moment_two)


def per_device(
    inputs,
    targets,
    lengths,
    lat_index,
    land,
    w_up,
    w_down,
    gains,
    m_up,
    m_down,
    m_gains,
    v_up,
    v_down,
    v_gains,
):
    section_id = lax.axis_index("section")
    sections, groups = lax.axis_size("section"), lax.axis_size("dp")
    fast_up, fast_down, fast_gain, stats = rollout(
        inputs,
        targets[0],
        lengths,
        lat_index,
        land,
        w_up[0],
        w_down[0],
        gains[0],
        sections,
        groups,
    )
    weight_sum = stats[2, 0]

    def slow_path():
        loss_weight = area_weight(lat_index, land) * (section_id < lengths).astype(jnp.float32)
        return plain_gradients(
            inputs,
            targets[0],
            loss_weight,
            weight_sum,
            w_up[0].astype(bf16),
            w_down[0].astype(bf16),
            gains[0],
        )

    grad_up, grad_down, grad_gain, local_loss = lax.cond(
        stats[4, 0] > 0.0, slow_path, lambda: (fast_up, fast_down, fast_gain, stats[0, 0])
    )
    loss_sum = lax.psum(local_loss, ("section", "dp"))
    grad_up, grad_down, grad_gain = (grad_up[None], grad_down[None], grad_gain[None])
    grad_up, grad_down, grad_gain = lax.psum((grad_up, grad_down, grad_gain), "dp")
    local_squares = (
        jnp.sum(grad_up * grad_up) + jnp.sum(grad_down * grad_down) + jnp.sum(grad_gain * grad_gain)
    )
    grad_norm = jnp.sqrt(lax.psum(local_squares, "section"))
    clip_scale = jnp.minimum(1.0, clip_limit / grad_norm)
    new_up, new_m_up, new_v_up = adam_step(w_up, grad_up * clip_scale, m_up, v_up, weight_decay)
    new_down, new_m_down, new_v_down = adam_step(
        w_down, grad_down * clip_scale, m_down, v_down, weight_decay
    )
    new_gains, new_m_gains, new_v_gains = adam_step(
        gains, grad_gain * clip_scale, m_gains, v_gains, 0.0
    )
    return (
        loss_sum,
        weight_sum,
        grad_norm,
        new_up,
        new_down,
        new_gains,
        new_m_up,
        new_m_down,
        new_m_gains,
        new_v_up,
        new_v_down,
        new_v_gains,
    )


def solution(mesh):
    return jax.shard_map(
        per_device,
        mesh=mesh,
        in_specs=(
            P("dp", None),
            P("section", "dp", None),
            P("dp"),
            P("dp"),
            P("dp"),
            P("section", None, None, None),
            P("section", None, None, None),
            P("section", None, None),
            P("section", None, None, None),
            P("section", None, None, None),
            P("section", None, None),
            P("section", None, None, None),
            P("section", None, None, None),
            P("section", None, None),
        ),
        out_specs=(
            P(),
            P(),
            P(),
            P("section", None, None, None),
            P("section", None, None, None),
            P("section", None, None),
            P("section", None, None, None),
            P("section", None, None, None),
            P("section", None, None),
            P("section", None, None, None),
            P("section", None, None, None),
            P("section", None, None),
        ),
        check_vma=False,
    )
```

```python
import functools
import math

import jax
import jax.numpy as jnp
from jax import lax
from jax.experimental import pallas as pl
from jax.experimental.pallas import tpu as pltpu
from jax.sharding import PartitionSpec as P

NLAT = 128
STEP = 10

norm_eps = 1e-06
clip_limit = 0.05
beta_one = 0.9
beta_two = 0.999
adam_eps = 1e-08
learn_rate = 0.1
weight_decay = 0.01

f32, bf16 = jnp.float32, jnp.bfloat16
MESH = pl.DeviceIdType.MESH
LANES = 128
ROWS = 512
WINDOW = 1536
SAVE_BYTES = 21 * 1024 * 1024


def dot(a, b):
    return jnp.dot(a, b, preferred_element_type=f32)


def dot_lhs_t(a, b):
    return lax.dot_general(a, b, (((0,), (0,)), ((), ())), preferred_element_type=f32)


def split_dot(product, onehot, values):
    high = values.astype(bf16)
    low = (values - high.astype(f32)).astype(bf16)
    return product(onehot, high) + product(onehot, low)


def rollout_kernel(
    sections,
    groups,
    packing,
    inputs_ref,
    target_ref,
    len_ref,
    lat_ref,
    land_ref,
    up_ref,
    down_ref,
    gain_ref,
    grads_ref,
    dgain_ref,
    stat_ref,
    xin,
    xout,
    cin,
    tgt,
    packed,
    save_x,
    save_h,
    save_d,
    qring,
    up_lo,
    up_t,
    down_lo,
    down_t,
    rank_ref,
    q_ref,
    scale_ref,
    loss_acc,
    gain_acc,
    wbuf,
    spread,
    acc,
    final,
    ybuf,
    zbuf,
    small,
    tiny,
    in_sem,
    tgt_sem,
    st_send,
    st_recv,
    ct_send,
    ct_recv,
    w_send,
    w_recv,
    y_send,
    y_recv,
    z_send,
    z_recv,
    za_send,
    za_recv,
    ya_send,
    ya_recv,
    small_send,
    small_recv,
    tiny_send,
    tiny_recv,
    out_sem,
):
    section = lax.axis_index("section")
    dp = lax.axis_index("dp")
    columns = xin.shape[0]
    feats = xin.shape[1]
    chunks = columns // ROWS
    live_rows = ROWS * (sections - 2) // sections
    prows = live_rows + 16
    total_packed = chunks * prows
    expand = live_rows + 512
    last = sections - 1
    ring = save_x.shape[0] // ROWS
    natural = section < (2 if packing else sections)
    plain_next = (section == 0) if packing else (section < last)
    packs = (section == 1) if packing else (section < 0)

    def peer(step):
        return (section, lax.rem(dp + step, groups))

    barrier = pltpu.get_barrier_semaphore()
    for step in range(1, sections):
        other = lax.rem(section + step, sections)
        pl.semaphore_signal(barrier, inc=1, device_id=(other, dp), device_id_type=MESH)
    for step in range(1, groups):
        pl.semaphore_signal(barrier, inc=1, device_id=peer(step), device_id_type=MESH)

    def rows_at(index, size, align=16):
        return pl.ds(pl.multiple_of(index, align), size)

    def input_copy(i):
        rows = rows_at(i * ROWS, ROWS)
        return pltpu.make_async_copy(inputs_ref.at[rows], xin.at[rows], in_sem.at[i])

    def target_copy(i):
        rows = rows_at(i * ROWS, ROWS)
        return pltpu.make_async_copy(target_ref.at[rows], tgt.at[rows], tgt_sem.at[i])

    @pl.when(section == 0)
    def _():
        @pl.loop(0, chunks)
        def _(i):
            input_copy(i).start()

    @pl.loop(0, chunks)
    def _(i):
        target_copy(i).start()

    for layer in range(2):
        up_lo[layer] = (0.5 * up_ref[layer]).astype(bf16)
        down_lo[layer] = down_ref[layer].astype(bf16)

    def prepare_backward():
        for layer in range(2):
            up_t[layer] = up_ref[layer].T.astype(bf16)
            down_t[layer] = (0.5 * down_ref[layer]).T.astype(bf16)
            gain_acc[layer] = jnp.zeros((8, feats), f32)
        for i in range(4):
            acc[i] = jnp.zeros((feats, feats), f32)
        loss_acc[...] = jnp.zeros_like(loss_acc)

    grid_rows = columns // LANES
    tile_row = lax.broadcasted_iota(jnp.int32, (8, LANES), 0)

    def window_start(j):
        shift = jnp.where(j < 7, 0, jnp.where(j < 11, 256, 384))
        return jnp.clip(ROWS * (j - 1) + shift, 0, columns - WINDOW)

    def expand_start(k):
        return jnp.clip(live_rows * k - 256, 0, total_packed - expand)

    def weight_copy(step):
        return pltpu.make_async_remote_copy(
            src_ref=wbuf.at[dp],
            dst_ref=wbuf.at[dp],
            send_sem=w_send.at[step],
            recv_sem=w_recv.at[step],
            device_id=peer(step),
            device_id_type=MESH,
        )

    def prepare_columns():
        length = len_ref[...]
        latitude = (lat_ref[...].astype(f32) + 0.5) * (math.pi / NLAT) - math.pi / 2
        area = jnp.cos(latitude) * (1.0 + land_ref[...].astype(f32))
        q_ref[...] = area * (section < length).astype(f32)
        local_weight = jnp.sum(
            area * jnp.minimum(length, sections).astype(f32), axis=(0, 1), keepdims=True
        )
        misses = jnp.zeros((1, 1), f32)
        if packing:
            beyond = length > 2
            flag = beyond.astype(bf16)
            lane_a = lax.broadcasted_iota(jnp.int32, (LANES, LANES), 0)
            lane_b = lax.broadcasted_iota(jnp.int32, (LANES, LANES), 1)
            within = dot(flag, (lane_a < lane_b).astype(bf16))
            row_total = jnp.sum(flag.astype(f32), axis=1, keepdims=True)
            row_a = lax.broadcasted_iota(jnp.int32, (grid_rows, grid_rows), 0)
            row_b = lax.broadcasted_iota(jnp.int32, (grid_rows, grid_rows), 1)
            before = dot(
                (row_b < row_a).astype(bf16),
                jnp.broadcast_to(row_total, (grid_rows, LANES)).astype(bf16),
            )
            rank = jnp.where(beyond, within + before, -1e6)
            rank_ref[...] = rank
            place = (
                lax.broadcasted_iota(jnp.int32, (grid_rows, LANES), 0) * LANES
                + lax.broadcasted_iota(jnp.int32, (grid_rows, LANES), 1)
            )
            rank_i = rank.astype(jnp.int32)
            missed = beyond & (rank_i >= total_packed)
            for j in range(chunks):
                shift = 0 if j < 7 else 256 if j < 11 else 384
                start = min(max(ROWS * (j - 1) + shift, 0), columns - WINDOW)
                member = (rank_i >= j * prows) & (rank_i < (j + 1) * prows)
                ready = ROWS * (j + 2 if j < 7 else j + 3)
                missed |= member & ((place < start) | (place >= min(start + WINDOW, ready)))
            row_chunk = lax.broadcasted_iota(jnp.int32, (grid_rows, LANES), 0) // (ROWS // LANES)
            row_start = jnp.clip(live_rows * row_chunk - 256, 0, total_packed - expand)
            missed |= beyond & ((rank_i < row_start) | (rank_i >= row_start + expand))
            misses = jnp.sum(missed.astype(f32), axis=(0, 1), keepdims=True)
        wbuf[dp] = jnp.where(tile_row < 4, local_weight, misses)
        for step in range(1, groups):
            weight_copy(step).start()

    def finish_weights():
        for step in range(1, groups):
            weight_copy(step).wait_recv()
        total = wbuf[0]
        for other in range(1, groups):
            total = total + wbuf[other]
        stat_ref[...] = total
        scale_ref[...] = 2.0 / jnp.broadcast_to(total[0:1], (8, LANES))

    pl.semaphore_wait(barrier, sections - 1 + groups - 1)

    def pack_matrix(j):
        start = window_start(j)
        base = (j * prows).astype(f32)
        target_row = lax.broadcasted_iota(jnp.int32, (prows, LANES), 0).astype(f32)
        first = start // LANES
        hits = []
        for i in range(WINDOW // LANES):
            hits.append(target_row == rank_ref[pl.ds(first + i, 1), :] - base)
        return start, first, hits

    def as_onehot(hits):
        return jnp.concatenate([jnp.where(hit, 1.0, 0.0).astype(bf16) for hit in hits], axis=1)

    def unpack_rows(k):
        start = expand_start(k)
        base = start.astype(f32)
        source_row = lax.broadcasted_iota(jnp.int32, (expand, LANES), 0).astype(f32)
        hits = []
        for i in range(ROWS // LANES):
            hits.append(source_row == rank_ref[pl.ds(k * (ROWS // LANES) + i, 1), :] - base)
        return split_dot(dot_lhs_t, as_onehot(hits), cin[rows_at(start, expand), :])

    def forward(rows, saved):
        x = xin[rows, :]
        for layer in range(2):
            if layer == 1:
                save_x[saved, :] = x
            r = lax.rsqrt(jnp.mean(x * x, -1, keepdims=True) + norm_eps)
            normed = (x * r * gain_ref[layer : layer + 1]).astype(bf16)
            half = dot(normed, up_lo[layer])
            t = jnp.tanh(half)
            a = 1.0 + t
            h = half * a
            hidden = h.astype(bf16)
            save_h[layer, saved, :] = hidden
            save_d[layer, saved, :] = (a + h * (1.0 - t)).astype(bf16)
            x = x + dot(hidden, down_lo[layer])
        xout[rows, :] = x

    def loss_part(size, diff, weight):
        weighted = jnp.concatenate(
            [diff[:, :LANES] * weight, diff[:, LANES:] * weight], axis=1
        )
        loss_acc[...] += jnp.sum((weighted * diff).reshape(size // 8, 8, feats), 0)
        return weighted * scale_ref[0:1, 0:1]

    def backward(size, rows, saved, g):
        for layer in (1, 0):
            low = g.astype(bf16)
            acc[2 + layer] += dot_lhs_t(save_h[layer, saved, :], low)
            pull = dot(low, down_t[layer])
            g_pre = (pull * save_d[layer, saved, :].astype(f32)).astype(bf16)
            x = save_x[saved, :] if layer == 1 else xin[rows, :]
            r = lax.rsqrt(jnp.mean(x * x, -1, keepdims=True) + norm_eps)
            gain = gain_ref[layer : layer + 1]
            xr = x * r
            normed = (xr * gain).astype(bf16)
            acc[layer] += dot_lhs_t(normed, g_pre)
            g_normed = dot(g_pre, up_t[layer])
            prod = g_normed * xr
            gain_acc[layer] += jnp.sum(prod.reshape(size // 8, 8, feats), 0)
            mean = jnp.mean(prod * gain, -1, keepdims=True)
            g = g + r * (gain * g_normed - xr * mean)
        xin[rows, :] = g

    def state_copy(source, size, i):
        rows = rows_at(i * size, size)
        return pltpu.make_async_remote_copy(
            src_ref=source.at[rows],
            dst_ref=xin.at[rows],
            send_sem=st_send.at[i],
            recv_sem=st_recv.at[i],
            device_id=(lax.rem(section + 1, sections), dp),
            device_id_type=MESH,
        )

    def cot_copy(size, i):
        rows = rows_at(i * size, size)
        return pltpu.make_async_remote_copy(
            src_ref=xin.at[rows],
            dst_ref=cin.at[rows],
            send_sem=ct_send.at[i],
            recv_sem=ct_recv.at[i],
            device_id=(lax.rem(section + sections - 1, sections), dp),
            device_id_type=MESH,
        )

    @pl.when(natural)
    def _():
        if packing:
            lag = jnp.where(section == 0, ring - 1, ring - 3)
        else:
            lag = jnp.minimum(ring - 1, 3 * (last - section))

        @pl.when(section > 0)
        def _():
            prepare_columns()
            prepare_backward()
            if packing:
                xout[2 * ROWS : WINDOW, :] = jnp.zeros((WINDOW - 2 * ROWS, feats), f32)

        @pl.loop(0, chunks + lag)
        def _(t):
            @pl.when(t < chunks)
            def _():
                @pl.when(section == 0)
                def _():
                    input_copy(t).wait()

                @pl.when(section > 0)
                def _():
                    state_copy(xout, ROWS, t).wait_recv()

                rows = rows_at(t * ROWS, ROWS)
                saved = rows_at(lax.rem(t, ring) * ROWS, ROWS)
                forward(rows, saved)

                @pl.when(plain_next)
                def _():
                    state_copy(xout, ROWS, t).start()

            if packing:

                j = jnp.where(t < 8, t - 1, t - 2)

                @pl.when(packs & (t >= 1) & (t != 8) & (j < chunks))
                def _():
                    start, _, hits = pack_matrix(j)
                    packed[rows_at(j * prows, prows), :] = split_dot(
                        dot, as_onehot(hits), xout[rows_at(start, WINDOW), :]
                    )
                    state_copy(packed, prows, j).start()

            @pl.when((section == 0) & (t == 3))
            def _():
                prepare_columns()
                prepare_backward()

            k = t - lag

            @pl.when((k >= 0) & (k < chunks))
            def _():
                @pl.when(k == 0)
                def _():
                    finish_weights()

                target_copy(k).wait()
                rows = rows_at(k * ROWS, ROWS)
                saved = rows_at(lax.rem(k, ring) * ROWS, ROWS)

                @pl.when(plain_next)
                def _():
                    cot_copy(ROWS, k).wait_recv()
                    spread[...] = cin[rows, :]

                if packing:

                    @pl.when(packs)
                    def _():
                        @pl.when(k == 0)
                        def _():
                            for i in range(3):
                                cot_copy(prows, i).wait_recv()

                        @pl.when((k >= 2) & (k + 1 < chunks))
                        def _():
                            cot_copy(prows, k + 1).wait_recv()

                        spread[...] = unpack_rows(k)

                else:

                    @pl.when(section == last)
                    def _():
                        spread[...] = jnp.zeros_like(spread)

                weight = jnp.concatenate(
                    [
                        jnp.broadcast_to(
                            q_ref[pl.ds(k * (ROWS // LANES) + i, 1), :], (LANES, LANES)
                        ).T
                        for i in range(ROWS // LANES)
                    ],
                    axis=0,
                )
                diff = xout[rows, :] - tgt[rows, :]
                g = loss_part(ROWS, diff, weight) + spread[...]
                backward(ROWS, rows, saved, g)

                @pl.when(section > 0)
                def _():
                    cot_copy(ROWS, k).start()

        @pl.loop(0, chunks)
        def _(i):
            @pl.when(plain_next)
            def _():
                state_copy(xout, ROWS, i).wait_send()

            if packing:

                @pl.when(packs)
                def _():
                    state_copy(packed, prows, i).wait_send()

            @pl.when(section > 0)
            def _():
                cot_copy(ROWS, i).wait_send()

    if packing:

        @pl.when(jnp.logical_not(natural))
        def _():
            lag = last - section
            prepare_columns()
            prepare_backward()

            @pl.loop(0, chunks + lag)
            def _(t):
                @pl.when(t < chunks)
                def _():
                    @pl.when(t == 0)
                    def _():
                        target_copy(0).wait()
                        target_copy(1).wait()

                    @pl.when(t + 2 < chunks)
                    def _():
                        target_copy(t + 2).wait()

                    start, first, hits = pack_matrix(t)
                    rows = rows_at(t * prows, prows)
                    packed[rows, :] = split_dot(
                        dot, as_onehot(hits), tgt[rows_at(start, WINDOW), :]
                    )
                    weight = jnp.zeros((prows, LANES), f32)
                    for i, hit in enumerate(hits):
                        weight += jnp.where(hit, q_ref[pl.ds(first + i, 1), :], 0.0)
                    qring[lax.rem(t, sections)] = jnp.broadcast_to(
                        jnp.sum(weight, -1, keepdims=True), (prows, LANES)
                    )
                    state_copy(xout, prows, t).wait_recv()
                    saved = rows_at(lax.rem(t, ring) * ROWS, prows)
                    forward(rows, saved)

                    @pl.when(section < last)
                    def _():
                        state_copy(xout, prows, t).start()

                k = t - lag

                @pl.when(k >= 0)
                def _():
                    @pl.when(k == 0)
                    def _():
                        finish_weights()

                    rows = rows_at(k * prows, prows)
                    saved = rows_at(lax.rem(k, ring) * ROWS, prows)
                    diff = xout[rows, :] - packed[rows, :]
                    spread[0:prows, :] = loss_part(prows, diff, qring[lax.rem(k, sections)])

                    @pl.when(section < last)
                    def _():
                        cot_copy(prows, k).wait_recv()
                        spread[0:prows, :] += cin[rows, :]

                    backward(prows, rows, saved, spread[0:prows, :])
                    cot_copy(prows, k).start()

            @pl.loop(0, chunks)
            def _(i):
                cot_copy(prows, i).wait_send()

                @pl.when(section < last)
                def _():
                    state_copy(xout, prows, i).wait_send()

    depth = min(4, groups)
    width = groups // depth
    y, z = lax.rem(dp, width), dp // width
    ypart, zpart = feats // width, feats // groups
    order = (3, 1, 2, 0)
    ysum = save_x

    def y_copy(p, step):
        to = lax.rem(y + step, width)
        i = p * width + step
        return pltpu.make_async_remote_copy(
            src_ref=acc.at[order[p], rows_at(to * ypart, ypart)],
            dst_ref=ybuf.at[p * (width - 1) + step - 1],
            send_sem=y_send.at[i],
            recv_sem=y_recv.at[i],
            device_id=(section, z * width + to),
            device_id_type=MESH,
        )

    def z_copy(p, step):
        to = lax.rem(z + step, depth)
        i = p * depth + step
        return pltpu.make_async_remote_copy(
            src_ref=ysum.at[rows_at(p * ypart + to * zpart, zpart)],
            dst_ref=zbuf.at[p * (depth - 1) + step - 1],
            send_sem=z_send.at[i],
            recv_sem=z_recv.at[i],
            device_id=(section, to * width + y),
            device_id_type=MESH,
        )

    def z_back(p, step):
        to = lax.rem(z + step, depth)
        i = p * depth + step
        rows = rows_at(y * ypart + z * zpart, zpart)
        return pltpu.make_async_remote_copy(
            src_ref=final.at[order[p], rows],
            dst_ref=final.at[order[p], rows],
            send_sem=za_send.at[i],
            recv_sem=za_recv.at[i],
            device_id=(section, to * width + y),
            device_id_type=MESH,
        )

    def y_back(p, step):
        to = lax.rem(y + step, width)
        i = p * width + step
        rows = rows_at(y * ypart, ypart)
        return pltpu.make_async_remote_copy(
            src_ref=final.at[order[p], rows],
            dst_ref=final.at[order[p], rows],
            send_sem=ya_send.at[i],
            recv_sem=ya_recv.at[i],
            device_id=(section, z * width + to),
            device_id_type=MESH,
        )

    def small_copy(step):
        return pltpu.make_async_remote_copy(
            src_ref=small.at[dp],
            dst_ref=small.at[dp],
            send_sem=small_send.at[step],
            recv_sem=small_recv.at[step],
            device_id=peer(step),
            device_id_type=MESH,
        )

    def tiny_copy(step):
        return pltpu.make_async_remote_copy(
            src_ref=tiny.at[section],
            dst_ref=tiny.at[section],
            send_sem=tiny_send.at[step],
            recv_sem=tiny_recv.at[step],
            device_id=(lax.rem(section + step, sections), dp),
            device_id_type=MESH,
        )

    def out_copy(p):
        return pltpu.make_async_copy(final.at[order[p]], grads_ref.at[order[p]], out_sem.at[p])

    pieces = range(4)
    for p in pieces:
        for step in range(1, width):
            y_copy(p, step).start()
    for p in pieces:
        own = acc[order[p], rows_at(y * ypart, ypart), :]
        for step in range(1, width):
            y_copy(p, step).wait_recv()
            own = own + ybuf[p * (width - 1) + step - 1]
        ysum[p * ypart : (p + 1) * ypart, :] = own
        for step in range(1, depth):
            z_copy(p, step).start()
    squares = jnp.zeros((1, 1), f32)
    for p in pieces:
        own = ysum[rows_at(p * ypart + z * zpart, zpart), :]
        for step in range(1, depth):
            z_copy(p, step).wait_recv()
            own = own + zbuf[p * (depth - 1) + step - 1]
        final[order[p], rows_at(y * ypart + z * zpart, zpart), :] = own
        squares = squares + jnp.sum(own * own, axis=(0, 1), keepdims=True)
        for step in range(1, depth):
            z_back(p, step).start()
    loss = jnp.sum(loss_acc[...], axis=(0, 1), keepdims=True)
    wide_row = lax.broadcasted_iota(jnp.int32, (8, feats), 0)
    small[dp] = jnp.where(
        wide_row == 0,
        jnp.sum(gain_acc[0], 0, keepdims=True),
        jnp.where(
            wide_row == 1,
            jnp.sum(gain_acc[1], 0, keepdims=True),
            jnp.where(wide_row < 4, loss, squares),
        ),
    )
    for step in range(1, groups):
        small_copy(step).start()
    for p in pieces:
        for step in range(1, depth):
            z_back(p, step).wait_recv()
        for step in range(1, width):
            y_back(p, step).start()
    for step in range(1, groups):
        small_copy(step).wait_recv()
    total = small[0]
    for other in range(1, groups):
        total = total + small[other]
    dgain_ref[...] = total[0:2]
    gain_squares = jnp.sum(total[0:2] * total[0:2], axis=(0, 1), keepdims=True)
    tiny[section] = jnp.where(tile_row < 4, total[2:3, 0:1], total[4:5, 0:1] + gain_squares)
    for step in range(1, sections):
        tiny_copy(step).start()
    for p in pieces:
        for step in range(1, width):
            y_back(p, step).wait_recv()
        out_copy(p).start()
    for step in range(1, sections):
        tiny_copy(step).wait_recv()
    whole = tiny[0]
    for other in range(1, sections):
        whole = whole + tiny[other]
    norm = jnp.sqrt(whole[4:5])
    scale = jnp.minimum(1.0, clip_limit / norm)
    stats = stat_ref[...]
    stat_ref[...] = jnp.where(
        tile_row == 0,
        whole[0:1],
        jnp.where(tile_row == 1, norm, jnp.where(tile_row == 2, scale, stats)),
    )

    for step in range(1, groups):
        weight_copy(step).wait_send()
        small_copy(step).wait_send()
    for step in range(1, sections):
        tiny_copy(step).wait_send()
    for p in pieces:
        out_copy(p).wait()
        for step in range(1, width):
            y_copy(p, step).wait_send()
            y_back(p, step).wait_send()
        for step in range(1, depth):
            z_copy(p, step).wait_send()
            z_back(p, step).wait_send()


def rollout(packing, sections, groups, inputs, target, lengths, lat_index, land, w_up, w_down, gains):
    columns, feats = inputs.shape
    chunks = columns // ROWS
    prows = ROWS * (sections - 2) // sections + 16
    grid_rows = columns // LANES
    packed_bytes = 4 * chunks * prows * feats
    ring = (SAVE_BYTES - packed_bytes) // (12 * ROWS * feats)
    depth = min(4, groups)
    width = groups // depth
    hbm = pl.BlockSpec(memory_space=pl.ANY)
    vmem = pl.BlockSpec(memory_space=pltpu.VMEM)
    dma = pltpu.SemaphoreType.DMA
    wide = pltpu.VMEM((columns, feats), f32)
    lows = pltpu.VMEM((2, feats, feats), bf16)
    grads = pltpu.VMEM((4, feats, feats), f32)
    flat = lambda array: array.reshape(grid_rows, LANES)
    return pl.pallas_call(
        functools.partial(rollout_kernel, sections, groups, packing),
        out_shape=(
            jax.ShapeDtypeStruct((4, feats, feats), f32),
            jax.ShapeDtypeStruct((2, feats), f32),
            jax.ShapeDtypeStruct((8, LANES), f32),
        ),
        in_specs=[hbm, hbm] + [vmem] * 6,
        out_specs=(hbm, vmem, vmem),
        scratch_shapes=[
            wide,
            wide,
            wide,
            wide,
            pltpu.VMEM((chunks * prows if packing else 8, feats), f32),
            pltpu.VMEM((ring * ROWS, feats), f32),
            pltpu.VMEM((2, ring * ROWS, feats), bf16),
            pltpu.VMEM((2, ring * ROWS, feats), bf16),
            pltpu.VMEM((sections, prows, LANES), f32),
            lows,
            lows,
            lows,
            lows,
            pltpu.VMEM((grid_rows, LANES), f32),
            pltpu.VMEM((grid_rows, LANES), f32),
            pltpu.VMEM((8, LANES), f32),
            pltpu.VMEM((8, feats), f32),
            pltpu.VMEM((2, 8, feats), f32),
            pltpu.VMEM((groups, 8, LANES), f32),
            pltpu.VMEM((ROWS, feats), f32),
            grads,
            grads,
            pltpu.VMEM((max(4 * (width - 1), 1), feats // width, feats), f32),
            pltpu.VMEM((4 * (depth - 1), feats // groups, feats), f32),
            pltpu.VMEM((groups, 8, feats), f32),
            pltpu.VMEM((sections, 8, LANES), f32),
            dma((chunks,)),
            dma((chunks,)),
            dma((chunks,)),
            dma((chunks,)),
            dma((chunks,)),
            dma((chunks,)),
            dma((groups,)),
            dma((groups,)),
            dma((4 * width,)),
            dma((4 * width,)),
            dma((4 * depth,)),
            dma((4 * depth,)),
            dma((4 * depth,)),
            dma((4 * depth,)),
            dma((4 * width,)),
            dma((4 * width,)),
            dma((groups,)),
            dma((groups,)),
            dma((sections,)),
            dma((sections,)),
            dma((4,)),
        ],
        compiler_params=pltpu.CompilerParams(
            collective_id=0 if packing else 1,
            has_side_effects=True,
            vmem_limit_bytes=63 * 1024 * 1024,
        ),
        name="rollout_packed" if packing else "rollout_all",
    )(
        inputs,
        target,
        flat(lengths),
        flat(lat_index),
        flat(land),
        w_up,
        w_down,
        gains,
    )


def adam_step(weights_old, gradient, moment_one, moment_two, decay_rate):
    moment_one = beta_one * moment_one + (1.0 - beta_one) * gradient
    moment_two = beta_two * moment_two + (1.0 - beta_two) * gradient * gradient
    first_hat = moment_one / (1.0 - beta_one**STEP)
    second_hat = moment_two / (1.0 - beta_two**STEP)
    new_weights = weights_old - learn_rate * (
        first_hat / (jnp.sqrt(second_hat) + adam_eps) + decay_rate * weights_old
    )
    return (new_weights, moment_one, moment_two)


def per_device(
    inputs,
    targets,
    lengths,
    lat_index,
    land,
    w_up,
    w_down,
    gains,
    m_up,
    m_down,
    m_gains,
    v_up,
    v_down,
    v_gains,
):
    sections, groups = lax.axis_size("section"), lax.axis_size("dp")
    operands = (inputs, targets[0], lengths, lat_index, land, w_up[0], w_down[0], gains[0])
    packed = rollout(True, sections, groups, *operands)

    grads, grad_gain, stats = lax.cond(
        packed[2][4, 0] > 0.0,
        lambda: rollout(False, sections, groups, *operands),
        lambda: packed,
    )
    loss_sum, grad_norm, clip_scale, weight_sum = (stats[i, 0] for i in range(4))
    grad_up, grad_down, grad_gain = grads[None, 0:2], grads[None, 2:4], grad_gain[None]
    new_up, new_m_up, new_v_up = adam_step(w_up, grad_up * clip_scale, m_up, v_up, weight_decay)
    new_down, new_m_down, new_v_down = adam_step(
        w_down, grad_down * clip_scale, m_down, v_down, weight_decay
    )
    new_gains, new_m_gains, new_v_gains = adam_step(
        gains, grad_gain * clip_scale, m_gains, v_gains, 0.0
    )
    return (
        loss_sum,
        weight_sum,
        grad_norm,
        new_up,
        new_down,
        new_gains,
        new_m_up,
        new_m_down,
        new_m_gains,
        new_v_up,
        new_v_down,
        new_v_gains,
    )


def solution(mesh):
    return jax.shard_map(
        per_device,
        mesh=mesh,
        in_specs=(
            P("dp", None),
            P("section", "dp", None),
            P("dp"),
            P("dp"),
            P("dp"),
            P("section", None, None, None),
            P("section", None, None, None),
            P("section", None, None),
            P("section", None, None, None),
            P("section", None, None, None),
            P("section", None, None),
            P("section", None, None, None),
            P("section", None, None, None),
            P("section", None, None),
        ),
        out_specs=(
            P(),
            P(),
            P(),
            P("section", None, None, None),
            P("section", None, None, None),
            P("section", None, None),
            P("section", None, None, None),
            P("section", None, None, None),
            P("section", None, None),
            P("section", None, None, None),
            P("section", None, None, None),
            P("section", None, None),
        ),
        check_vma=False,
    )
```

```python
import functools
import math

import jax
import jax.numpy as jnp
from jax import lax
from jax.experimental import pallas as pl
from jax.experimental.pallas import tpu as pltpu
from jax.sharding import PartitionSpec as P

NLAT = 128
STEP = 10

norm_eps = 1e-06
clip_limit = 0.05
beta_one = 0.9
beta_two = 0.999
adam_eps = 1e-08
learn_rate = 0.1
weight_decay = 0.01

f32, bf16 = jnp.float32, jnp.bfloat16
MESH = pl.DeviceIdType.MESH
LANES = 128
PIECE = 128
ROWS = 512
SPARE = 80
WINDOW = 1536
SAVE_BYTES = 21 * 1024 * 1024


def dot(a, b):
    return jnp.dot(a, b, preferred_element_type=f32)


def dot_lhs_t(a, b):
    return lax.dot_general(a, b, (((0,), (0,)), ((), ())), preferred_element_type=f32)


def split_dot(product, onehot, values):
    high = values.astype(bf16)
    low = (values - high.astype(f32)).astype(bf16)
    return product(onehot, high) + product(onehot, low)


def rollout_kernel(
    sections,
    groups,
    packing,
    inputs_ref,
    target_ref,
    len_ref,
    lat_ref,
    land_ref,
    up_hbm,
    down_hbm,
    gain_ref,
    grads_ref,
    dgain_ref,
    stat_ref,
    xin,
    xout,
    cin,
    tgt,
    packed,
    save_x,
    save_h,
    save_d,
    qring,
    up_lo,
    up_t,
    down_lo,
    down_t,
    rank_ref,
    q_ref,
    scale_ref,
    loss_acc,
    gain_acc,
    wbuf,
    spread,
    up_ref,
    down_ref,
    acc,
    final,
    ybuf,
    zbuf,
    small,
    tiny,
    in_sem,
    tgt_sem,
    st_send,
    st_recv,
    ct_send,
    ct_recv,
    w_send,
    w_recv,
    y_send,
    y_recv,
    z_send,
    z_recv,
    za_send,
    za_recv,
    ya_send,
    ya_recv,
    small_send,
    small_recv,
    tiny_send,
    tiny_recv,
    out_sem,
    weight_sem,
):
    section = lax.axis_index("section")
    dp = lax.axis_index("dp")
    columns = xin.shape[0]
    feats = xin.shape[1]
    chunks = columns // ROWS
    live_rows = ROWS * (sections - 2) // sections
    prows = live_rows + 16
    total_packed = chunks * prows
    expand = live_rows + 512
    last = sections - 1
    ring = save_x.shape[0] // ROWS
    natural = section < (2 if packing else sections)
    plain_next = (section == 0) if packing else (section < last)
    packs = (section == 1) if packing else (section < 0)

    def peer(step):
        return (section, lax.rem(dp + step, groups))

    up_copy = pltpu.make_async_copy(up_hbm, up_ref, weight_sem.at[0])
    down_copy = pltpu.make_async_copy(down_hbm, down_ref, weight_sem.at[1])
    up_copy.start()
    down_copy.start()

    barrier = pltpu.get_barrier_semaphore()
    for step in range(1, sections):
        other = lax.rem(section + step, sections)
        pl.semaphore_signal(barrier, inc=1, device_id=(other, dp), device_id_type=MESH)
    for step in range(1, groups):
        pl.semaphore_signal(barrier, inc=1, device_id=peer(step), device_id_type=MESH)

    def rows_at(index, size, align=16):
        return pl.ds(pl.multiple_of(index, align), size)

    def input_copy(i):
        rows = rows_at(i * ROWS, ROWS)
        return pltpu.make_async_copy(inputs_ref.at[rows], xin.at[rows], in_sem.at[i])

    def target_copy(i):
        rows = rows_at(i * ROWS, ROWS)
        return pltpu.make_async_copy(target_ref.at[rows], tgt.at[rows], tgt_sem.at[i])

    @pl.when(section == 0)
    def _():
        @pl.loop(0, chunks)
        def _(i):
            input_copy(i).start()

    @pl.loop(0, chunks)
    def _(i):
        target_copy(i).start()

    def prepare_backward():
        for layer in range(2):
            up_t[layer] = up_ref[layer].T.astype(bf16)
            down_t[layer] = (0.5 * down_ref[layer]).T.astype(bf16)
            gain_acc[layer] = jnp.zeros((8, feats), f32)
        for i in range(4):
            acc[i] = jnp.zeros((feats, feats), f32)
        loss_acc[...] = jnp.zeros_like(loss_acc)

    grid_rows = columns // LANES
    tile_row = lax.broadcasted_iota(jnp.int32, (8, LANES), 0)

    def window_start(j):
        shift = jnp.where(j < 7, 0, jnp.where(j < 11, 256, 384))
        return jnp.clip(ROWS * (j - 1) + shift, 0, columns - WINDOW)

    def expand_start(k):
        return jnp.clip(live_rows * k - 272, 0, total_packed - expand)

    def chunks_for(k):
        return (expand_start(k) + expand - 1) // prows

    def weight_copy(step):
        return pltpu.make_async_remote_copy(
            src_ref=wbuf.at[dp],
            dst_ref=wbuf.at[dp],
            send_sem=w_send.at[step],
            recv_sem=w_recv.at[step],
            device_id=peer(step),
            device_id_type=MESH,
        )

    def prepare_columns():
        length = len_ref[...]
        latitude = (lat_ref[...].astype(f32) + 0.5) * (math.pi / NLAT) - math.pi / 2
        area = jnp.cos(latitude) * (1.0 + land_ref[...].astype(f32))
        q_ref[...] = area * (section < length).astype(f32)
        local_weight = jnp.sum(
            area * jnp.minimum(length, sections).astype(f32), axis=(0, 1), keepdims=True
        )
        misses = jnp.zeros((1, 1), f32)
        if packing:
            beyond = length > 2
            flag = beyond.astype(bf16)
            lane_a = lax.broadcasted_iota(jnp.int32, (LANES, LANES), 0)
            lane_b = lax.broadcasted_iota(jnp.int32, (LANES, LANES), 1)
            within = dot(flag, (lane_a < lane_b).astype(bf16))
            row_total = jnp.sum(flag.astype(f32), axis=1, keepdims=True)
            row_a = lax.broadcasted_iota(jnp.int32, (grid_rows, grid_rows), 0)
            row_b = lax.broadcasted_iota(jnp.int32, (grid_rows, grid_rows), 1)
            before = dot(
                (row_b < row_a).astype(bf16),
                jnp.broadcast_to(row_total, (grid_rows, LANES)).astype(bf16),
            )
            rank = jnp.where(beyond, within + before, -1e6)
            rank_ref[...] = rank
            place = (
                lax.broadcasted_iota(jnp.int32, (grid_rows, LANES), 0) * LANES
                + lax.broadcasted_iota(jnp.int32, (grid_rows, LANES), 1)
            )
            rank_i = rank.astype(jnp.int32)
            missed = beyond & (rank_i >= total_packed - SPARE)
            for j in range(chunks):
                shift = 0 if j < 7 else 256 if j < 11 else 384
                start = min(max(ROWS * (j - 1) + shift, 0), columns - WINDOW)
                member = (rank_i >= j * prows) & (rank_i < (j + 1) * prows)
                ready = ROWS * (j + 2 if j < 7 else j + 3)
                missed |= member & ((place < start) | (place >= min(start + WINDOW, ready)))
            row_chunk = lax.broadcasted_iota(jnp.int32, (grid_rows, LANES), 0) // (ROWS // LANES)
            row_start = jnp.clip(live_rows * row_chunk - 272, 0, total_packed - expand)
            missed |= beyond & ((rank_i < row_start) | (rank_i >= row_start + expand))
            misses = jnp.sum(missed.astype(f32), axis=(0, 1), keepdims=True)
        wbuf[dp] = jnp.where(tile_row < 4, local_weight, misses)
        for step in range(1, groups):
            weight_copy(step).start()

    def finish_weights():
        for step in range(1, groups):
            weight_copy(step).wait_recv()
        total = wbuf[0]
        for other in range(1, groups):
            total = total + wbuf[other]
        stat_ref[...] = total
        scale_ref[...] = 2.0 / jnp.broadcast_to(total[0:1], (8, LANES))

    up_copy.wait()
    down_copy.wait()
    for layer in range(2):
        up_lo[layer] = (0.5 * up_ref[layer]).astype(bf16)
        down_lo[layer] = down_ref[layer].astype(bf16)
    pl.semaphore_wait(barrier, sections - 1 + groups - 1)

    def pack_matrix(j):
        start = window_start(j)
        base = (j * prows).astype(f32)
        target_row = lax.broadcasted_iota(jnp.int32, (prows, LANES), 0).astype(f32)
        first = start // LANES
        hits = []
        for i in range(WINDOW // LANES):
            hits.append(target_row == rank_ref[pl.ds(first + i, 1), :] - base)
        return start, first, hits

    def as_onehot(hits):
        return jnp.concatenate([jnp.where(hit, 1.0, 0.0).astype(bf16) for hit in hits], axis=1)

    def unpack_rows(k):
        start = expand_start(k)
        base = start.astype(f32)
        source_row = lax.broadcasted_iota(jnp.int32, (expand, LANES), 0).astype(f32)
        hits = []
        for i in range(ROWS // LANES):
            hits.append(source_row == rank_ref[pl.ds(k * (ROWS // LANES) + i, 1), :] - base)
        return dot_lhs_t(as_onehot(hits), cin[rows_at(start, expand), :].astype(bf16))

    def forward(rows, saved):
        x = xin[rows, :]
        for layer in range(2):
            if layer == 1:
                save_x[saved, :] = x
            r = lax.rsqrt(jnp.mean(x * x, -1, keepdims=True) + norm_eps)
            normed = (x * r * gain_ref[layer : layer + 1]).astype(bf16)
            half = dot(normed, up_lo[layer])
            t = jnp.tanh(half)
            a = 1.0 + t
            h = half * a
            hidden = h.astype(bf16)
            save_h[layer, saved, :] = hidden
            save_d[layer, saved, :] = (a + h * (1.0 - t)).astype(bf16)
            x = x + dot(hidden, down_lo[layer])
        xout[rows, :] = x

    def loss_part(size, diff, weight):
        weighted = jnp.concatenate(
            [diff[:, :LANES] * weight, diff[:, LANES:] * weight], axis=1
        )
        loss_acc[...] += jnp.sum((weighted * diff).reshape(size // 8, 8, feats), 0)
        return weighted * scale_ref[0:1, 0:1]

    def backward(size, rows, saved, g):
        for layer in (1, 0):
            low = g.astype(bf16)
            acc[2 + layer] += dot_lhs_t(save_h[layer, saved, :], low)
            pull = dot(low, down_t[layer])
            g_pre = (pull * save_d[layer, saved, :].astype(f32)).astype(bf16)
            x = save_x[saved, :] if layer == 1 else xin[rows, :]
            r = lax.rsqrt(jnp.mean(x * x, -1, keepdims=True) + norm_eps)
            gain = gain_ref[layer : layer + 1]
            xr = x * r
            normed = (xr * gain).astype(bf16)
            acc[layer] += dot_lhs_t(normed, g_pre)
            g_normed = dot(g_pre, up_t[layer])
            prod = g_normed * xr
            gain_acc[layer] += jnp.sum(prod.reshape(size // 8, 8, feats), 0)
            mean = jnp.mean(prod * gain, -1, keepdims=True)
            g = g + r * (gain * g_normed - xr * mean)
        xin[rows, :] = g

    def state_copy(source, size, i, count=None):
        rows = rows_at(i * size, size if count is None else count)
        return pltpu.make_async_remote_copy(
            src_ref=source.at[rows],
            dst_ref=xin.at[rows],
            send_sem=st_send.at[i],
            recv_sem=st_recv.at[i],
            device_id=(lax.rem(section + 1, sections), dp),
            device_id_type=MESH,
        )

    def cot_copy(size, i, count=None):
        rows = rows_at(i * size, size if count is None else count)
        return pltpu.make_async_remote_copy(
            src_ref=xin.at[rows],
            dst_ref=cin.at[rows],
            send_sem=ct_send.at[i],
            recv_sem=ct_recv.at[i],
            device_id=(lax.rem(section + sections - 1, sections), dp),
            device_id_type=MESH,
        )

    def shorter(copy, size, i, action):
        @pl.when(i < chunks - 1)
        def _():
            action(copy(size, i, size))

        @pl.when(i == chunks - 1)
        def _():
            action(copy(size, i, size - SPARE))

    def packed_state(size, i, count):
        return state_copy(packed, size, i, count)

    def packed_receive(size, i):
        @pl.when(section == 2)
        def _():
            shorter(packed_state, size, i, lambda copy: copy.wait_recv())

        @pl.when(section > 2)
        def _():
            state_copy(xout, size, i).wait_recv()

    def cot_part(size, i, count):
        return cot_copy(size, i, count)

    def cot_wait(size, i):
        shorter(cot_part, size, i, lambda copy: copy.wait_recv())

    def cot_do(size, i, action):
        @pl.when(section == 2)
        def _():
            shorter(cot_part, size, i, action)

        @pl.when(section > 2)
        def _():
            action(cot_copy(size, i))

    @pl.when(natural)
    def _():
        if packing:
            lag = jnp.where(section == 0, ring - 1, ring - 3)
        else:
            lag = jnp.minimum(ring - 1, 3 * (last - section))

        @pl.when(section > 0)
        def _():
            prepare_columns()
            prepare_backward()
            if packing:
                xout[2 * ROWS : WINDOW, :] = jnp.zeros((WINDOW - 2 * ROWS, feats), f32)
                cin[total_packed - SPARE : total_packed, :] = jnp.zeros((SPARE, feats), f32)

        @pl.loop(0, chunks + lag)
        def _(t):
            @pl.when(t < chunks)
            def _():
                @pl.when(section == 0)
                def _():
                    input_copy(t).wait()

                @pl.when(section > 0)
                def _():
                    state_copy(xout, ROWS, t).wait_recv()

                rows = rows_at(t * ROWS, ROWS)
                saved = rows_at(lax.rem(t, ring) * ROWS, ROWS)
                forward(rows, saved)

                @pl.when(plain_next)
                def _():
                    state_copy(xout, ROWS, t).start()

            if packing:

                j = jnp.where(t < 8, t - 1, t - 2)

                @pl.when(packs & (t >= 1) & (t != 8) & (j < chunks))
                def _():
                    start, _, hits = pack_matrix(j)
                    packed[rows_at(j * prows, prows), :] = split_dot(
                        dot, as_onehot(hits), xout[rows_at(start, WINDOW), :]
                    )
                    shorter(packed_state, prows, j, lambda copy: copy.start())

            @pl.when((section == 0) & (t == 3))
            def _():
                prepare_columns()
                prepare_backward()

            k = t - lag

            @pl.when((k >= 0) & (k < chunks))
            def _():
                @pl.when(k == 0)
                def _():
                    finish_weights()

                target_copy(k).wait()
                rows = rows_at(k * ROWS, ROWS)
                saved = rows_at(lax.rem(k, ring) * ROWS, ROWS)

                @pl.when(plain_next)
                def _():
                    cot_copy(ROWS, k).wait_recv()
                    spread[...] = cin[rows, :]

                if packing:

                    @pl.when(packs)
                    def _():
                        had = jnp.where(k == 0, -1, chunks_for(jnp.maximum(k - 1, 0)))
                        for i in range(3):

                            @pl.when(had + 1 + i <= chunks_for(k))
                            def _():
                                cot_wait(prows, had + 1 + i)

                        spread[...] = unpack_rows(k)

                else:

                    @pl.when(section == last)
                    def _():
                        spread[...] = jnp.zeros_like(spread)

                weight = jnp.concatenate(
                    [
                        jnp.broadcast_to(
                            q_ref[pl.ds(k * (ROWS // LANES) + i, 1), :], (LANES, LANES)
                        ).T
                        for i in range(ROWS // LANES)
                    ],
                    axis=0,
                )
                diff = xout[rows, :] - tgt[rows, :]
                g = loss_part(ROWS, diff, weight) + spread[...]
                backward(ROWS, rows, saved, g)

                @pl.when(section > 0)
                def _():
                    cot_copy(ROWS, k).start()

        @pl.loop(0, chunks)
        def _(i):
            @pl.when(plain_next)
            def _():
                state_copy(xout, ROWS, i).wait_send()

            if packing:

                @pl.when(packs)
                def _():
                    shorter(packed_state, prows, i, lambda copy: copy.wait_send())

            @pl.when(section > 0)
            def _():
                cot_copy(ROWS, i).wait_send()

    if packing:

        @pl.when(jnp.logical_not(natural))
        def _():
            lag = last - section
            prepare_columns()
            prepare_backward()

            @pl.when(section == 2)
            def _():
                xin[total_packed - SPARE : total_packed, :] = jnp.zeros((SPARE, feats), f32)


            @pl.loop(0, chunks + lag)
            def _(t):
                @pl.when(t < chunks)
                def _():
                    @pl.when(t == 0)
                    def _():
                        target_copy(0).wait()
                        target_copy(1).wait()

                    @pl.when(t + 2 < chunks)
                    def _():
                        target_copy(t + 2).wait()

                    start, first, hits = pack_matrix(t)
                    rows = rows_at(t * prows, prows)
                    packed[rows, :] = split_dot(
                        dot, as_onehot(hits), tgt[rows_at(start, WINDOW), :]
                    )
                    weight = jnp.zeros((prows, LANES), f32)
                    for i, hit in enumerate(hits):
                        weight += jnp.where(hit, q_ref[pl.ds(first + i, 1), :], 0.0)
                    qring[lax.rem(t, sections)] = jnp.broadcast_to(
                        jnp.sum(weight, -1, keepdims=True), (prows, LANES)
                    )
                    packed_receive(prows, t)
                    saved = rows_at(lax.rem(t, ring) * ROWS, prows)
                    forward(rows, saved)

                    @pl.when(section < last)
                    def _():
                        state_copy(xout, prows, t).start()

                k = t - lag

                @pl.when(k >= 0)
                def _():
                    @pl.when(k == 0)
                    def _():
                        finish_weights()

                    rows = rows_at(k * prows, prows)
                    saved = rows_at(lax.rem(k, ring) * ROWS, prows)
                    diff = xout[rows, :] - packed[rows, :]
                    spread[0:prows, :] = loss_part(prows, diff, qring[lax.rem(k, sections)])

                    @pl.when(section < last)
                    def _():
                        cot_copy(prows, k).wait_recv()
                        spread[0:prows, :] += cin[rows, :]

                    backward(prows, rows, saved, spread[0:prows, :])
                    cot_do(prows, k, lambda copy: copy.start())

            @pl.loop(0, chunks)
            def _(i):
                cot_do(prows, i, lambda copy: copy.wait_send())

                @pl.when(section < last)
                def _():
                    state_copy(xout, prows, i).wait_send()

    depth = min(4, groups)
    width = groups // depth
    y, z = lax.rem(dp, width), dp // width
    ypart, zpart = PIECE // width, PIECE // groups
    halves = feats // PIECE
    pieces = range(4 * halves)
    matrix = [m for m in (3, 1, 2, 0) for _ in range(halves)]
    first = [PIECE * (p % halves) for p in pieces]
    ysum = save_x

    def y_copy(p, step):
        to = lax.rem(y + step, width)
        i = p * width + step
        return pltpu.make_async_remote_copy(
            src_ref=acc.at[matrix[p], rows_at(first[p] + to * ypart, ypart)],
            dst_ref=ybuf.at[p * (width - 1) + step - 1],
            send_sem=y_send.at[i],
            recv_sem=y_recv.at[i],
            device_id=(section, z * width + to),
            device_id_type=MESH,
        )

    def z_copy(p, step):
        to = lax.rem(z + step, depth)
        i = p * depth + step
        return pltpu.make_async_remote_copy(
            src_ref=ysum.at[rows_at(p * ypart + to * zpart, zpart)],
            dst_ref=zbuf.at[p * (depth - 1) + step - 1],
            send_sem=z_send.at[i],
            recv_sem=z_recv.at[i],
            device_id=(section, to * width + y),
            device_id_type=MESH,
        )

    def z_back(p, step):
        to = lax.rem(z + step, depth)
        i = p * depth + step
        rows = rows_at(first[p] + y * ypart + z * zpart, zpart)
        return pltpu.make_async_remote_copy(
            src_ref=final.at[matrix[p], rows],
            dst_ref=final.at[matrix[p], rows],
            send_sem=za_send.at[i],
            recv_sem=za_recv.at[i],
            device_id=(section, to * width + y),
            device_id_type=MESH,
        )

    def y_back(p, step):
        to = lax.rem(y + step, width)
        i = p * width + step
        rows = rows_at(first[p] + y * ypart, ypart)
        return pltpu.make_async_remote_copy(
            src_ref=final.at[matrix[p], rows],
            dst_ref=final.at[matrix[p], rows],
            send_sem=ya_send.at[i],
            recv_sem=ya_recv.at[i],
            device_id=(section, z * width + to),
            device_id_type=MESH,
        )

    def small_copy(step):
        return pltpu.make_async_remote_copy(
            src_ref=small.at[dp],
            dst_ref=small.at[dp],
            send_sem=small_send.at[step],
            recv_sem=small_recv.at[step],
            device_id=peer(step),
            device_id_type=MESH,
        )

    def tiny_copy(step):
        return pltpu.make_async_remote_copy(
            src_ref=tiny.at[section],
            dst_ref=tiny.at[section],
            send_sem=tiny_send.at[step],
            recv_sem=tiny_recv.at[step],
            device_id=(lax.rem(section + step, sections), dp),
            device_id_type=MESH,
        )

    def out_copy(p):
        rows = pl.ds(first[p], PIECE)
        return pltpu.make_async_copy(
            final.at[matrix[p], rows], grads_ref.at[matrix[p], rows], out_sem.at[p]
        )

    for p in pieces:
        for step in range(1, width):
            y_copy(p, step).start()
    for p in pieces:
        own = acc[matrix[p], rows_at(first[p] + y * ypart, ypart), :]
        for step in range(1, width):
            y_copy(p, step).wait_recv()
            own = own + ybuf[p * (width - 1) + step - 1]
        ysum[p * ypart : (p + 1) * ypart, :] = own
        for step in range(1, depth):
            z_copy(p, step).start()
    squares = jnp.zeros((1, 1), f32)
    for p in pieces:
        own = ysum[rows_at(p * ypart + z * zpart, zpart), :]
        for step in range(1, depth):
            z_copy(p, step).wait_recv()
            own = own + zbuf[p * (depth - 1) + step - 1]
        final[matrix[p], rows_at(first[p] + y * ypart + z * zpart, zpart), :] = own
        squares = squares + jnp.sum(own * own, axis=(0, 1), keepdims=True)
        for step in range(1, depth):
            z_back(p, step).start()
    loss = jnp.sum(loss_acc[...], axis=(0, 1), keepdims=True)
    wide_row = lax.broadcasted_iota(jnp.int32, (8, feats), 0)
    small[dp] = jnp.where(
        wide_row == 0,
        jnp.sum(gain_acc[0], 0, keepdims=True),
        jnp.where(
            wide_row == 1,
            jnp.sum(gain_acc[1], 0, keepdims=True),
            jnp.where(wide_row < 4, loss, squares),
        ),
    )
    for step in range(1, groups):
        small_copy(step).start()
    for p in pieces:
        for step in range(1, depth):
            z_back(p, step).wait_recv()
        for step in range(1, width):
            y_back(p, step).start()
    for step in range(1, groups):
        small_copy(step).wait_recv()
    total = small[0]
    for other in range(1, groups):
        total = total + small[other]
    dgain_ref[...] = total[0:2]
    gain_squares = jnp.sum(total[0:2] * total[0:2], axis=(0, 1), keepdims=True)
    tiny[section] = jnp.where(tile_row < 4, total[2:3, 0:1], total[4:5, 0:1] + gain_squares)
    for step in range(1, sections):
        tiny_copy(step).start()
    for p in pieces:
        for step in range(1, width):
            y_back(p, step).wait_recv()
        out_copy(p).start()
    for step in range(1, sections):
        tiny_copy(step).wait_recv()
    whole = tiny[0]
    for other in range(1, sections):
        whole = whole + tiny[other]
    norm = jnp.sqrt(whole[4:5])
    scale = jnp.minimum(1.0, clip_limit / norm)
    stats = stat_ref[...]
    stat_ref[...] = jnp.where(
        tile_row == 0,
        whole[0:1],
        jnp.where(tile_row == 1, norm, jnp.where(tile_row == 2, scale, stats)),
    )

    for step in range(1, groups):
        weight_copy(step).wait_send()
        small_copy(step).wait_send()
    for step in range(1, sections):
        tiny_copy(step).wait_send()
    for p in pieces:
        out_copy(p).wait()
        for step in range(1, width):
            y_copy(p, step).wait_send()
            y_back(p, step).wait_send()
        for step in range(1, depth):
            z_copy(p, step).wait_send()
            z_back(p, step).wait_send()


def rollout(packing, sections, groups, inputs, target, lengths, lat_index, land, w_up, w_down, gains):
    columns, feats = inputs.shape
    chunks = columns // ROWS
    prows = ROWS * (sections - 2) // sections + 16
    grid_rows = columns // LANES
    packed_bytes = 4 * chunks * prows * feats
    ring = (SAVE_BYTES - packed_bytes) // (12 * ROWS * feats)
    depth = min(4, groups)
    width = groups // depth
    pieces = 4 * feats // PIECE
    hbm = pl.BlockSpec(memory_space=pl.ANY)
    vmem = pl.BlockSpec(memory_space=pltpu.VMEM)
    dma = pltpu.SemaphoreType.DMA
    wide = pltpu.VMEM((columns, feats), f32)
    lows = pltpu.VMEM((2, feats, feats), bf16)
    grads = pltpu.VMEM((4, feats, feats), f32)
    square = pltpu.VMEM((2, feats, feats), f32)
    flat = lambda array: array.reshape(grid_rows, LANES)
    return pl.pallas_call(
        functools.partial(rollout_kernel, sections, groups, packing),
        out_shape=(
            jax.ShapeDtypeStruct((4, feats, feats), f32),
            jax.ShapeDtypeStruct((2, feats), f32),
            jax.ShapeDtypeStruct((8, LANES), f32),
        ),
        in_specs=[hbm, hbm, vmem, vmem, vmem, hbm, hbm, vmem],
        out_specs=(hbm, vmem, vmem),
        scratch_shapes=[
            wide,
            wide,
            wide,
            wide,
            pltpu.VMEM((chunks * prows if packing else 8, feats), f32),
            pltpu.VMEM((ring * ROWS, feats), f32),
            pltpu.VMEM((2, ring * ROWS, feats), bf16),
            pltpu.VMEM((2, ring * ROWS, feats), bf16),
            pltpu.VMEM((sections, prows, LANES), f32),
            lows,
            lows,
            lows,
            lows,
            pltpu.VMEM((grid_rows, LANES), f32),
            pltpu.VMEM((grid_rows, LANES), f32),
            pltpu.VMEM((8, LANES), f32),
            pltpu.VMEM((8, feats), f32),
            pltpu.VMEM((2, 8, feats), f32),
            pltpu.VMEM((groups, 8, LANES), f32),
            pltpu.VMEM((ROWS, feats), f32),
            square,
            square,
            grads,
            grads,
            pltpu.VMEM((max(pieces * (width - 1), 1), PIECE // width, feats), f32),
            pltpu.VMEM((pieces * (depth - 1), PIECE // groups, feats), f32),
            pltpu.VMEM((groups, 8, feats), f32),
            pltpu.VMEM((sections, 8, LANES), f32),
            dma((chunks,)),
            dma((chunks,)),
            dma((chunks,)),
            dma((chunks,)),
            dma((chunks,)),
            dma((chunks,)),
            dma((groups,)),
            dma((groups,)),
            dma((pieces * width,)),
            dma((pieces * width,)),
            dma((pieces * depth,)),
            dma((pieces * depth,)),
            dma((pieces * depth,)),
            dma((pieces * depth,)),
            dma((pieces * width,)),
            dma((pieces * width,)),
            dma((groups,)),
            dma((groups,)),
            dma((sections,)),
            dma((sections,)),
            dma((pieces,)),
            dma((2,)),
        ],
        compiler_params=pltpu.CompilerParams(
            collective_id=0 if packing else 1,
            has_side_effects=True,
            vmem_limit_bytes=63 * 1024 * 1024,
        ),
        name="rollout_packed" if packing else "rollout_all",
    )(
        inputs,
        target,
        flat(lengths),
        flat(lat_index),
        flat(land),
        w_up,
        w_down,
        gains,
    )


def adam_step(weights_old, gradient, moment_one, moment_two, decay_rate):
    moment_one = beta_one * moment_one + (1.0 - beta_one) * gradient
    moment_two = beta_two * moment_two + (1.0 - beta_two) * gradient * gradient
    first_hat = moment_one / (1.0 - beta_one**STEP)
    second_hat = moment_two / (1.0 - beta_two**STEP)
    new_weights = weights_old - learn_rate * (
        first_hat / (jnp.sqrt(second_hat) + adam_eps) + decay_rate * weights_old
    )
    return (new_weights, moment_one, moment_two)


def update_kernel(
    grads_ref,
    dgain_ref,
    stat_ref,
    w_up,
    w_down,
    gains,
    m_up,
    m_down,
    m_gains,
    v_up,
    v_down,
    v_gains,
    *outs,
):
    clip = stat_ref[2:3, 0:1]
    matrices = ((0, w_up, m_up, v_up), (1, w_down, m_down, v_down))
    for i, weight, one, two in matrices:
        new = adam_step(weight[0], grads_ref[i, 0] * clip, one[0], two[0], weight_decay)
        for part in range(3):
            outs[3 * part + i][0] = new[part]

    @pl.when(pl.program_id(0) == 0)
    def _():
        new = adam_step(gains[...], dgain_ref[...] * clip, m_gains[...], v_gains[...], 0.0)
        for part in range(3):
            outs[3 * part + 2][...] = new[part]


def update(grads, grad_gain, stats, *state):
    layers, feats = grad_gain.shape
    halves = 2
    rows = feats // halves
    grads = grads.reshape(2, layers, feats, feats)
    matrix = pl.BlockSpec((1, rows, feats), lambda i: (i // halves, i % halves, 0))
    small = pl.BlockSpec((layers, feats), lambda i: (0, 0))
    specs = [matrix, matrix, small] * 3
    shapes = [jax.ShapeDtypeStruct(a.shape[1:], f32) for a in state]
    new = pl.pallas_call(
        update_kernel,
        grid=(layers * halves,),
        in_specs=[
            pl.BlockSpec((2, 1, rows, feats), lambda i: (0, i // halves, i % halves, 0)),
            small,
            pl.BlockSpec((8, LANES), lambda i: (0, 0)),
        ]
        + specs,
        out_specs=specs,
        out_shape=shapes,
        compiler_params=pltpu.CompilerParams(vmem_limit_bytes=32 * 1024 * 1024),
        name="update",
    )(grads, grad_gain, stats, *(a[0] for a in state))
    return tuple(a[None] for a in new)


def per_device(
    inputs,
    targets,
    lengths,
    lat_index,
    land,
    w_up,
    w_down,
    gains,
    m_up,
    m_down,
    m_gains,
    v_up,
    v_down,
    v_gains,
):
    sections, groups = lax.axis_size("section"), lax.axis_size("dp")
    operands = (inputs, targets[0], lengths, lat_index, land, w_up[0], w_down[0], gains[0])
    packed = rollout(True, sections, groups, *operands)

    grads, grad_gain, stats = lax.cond(
        packed[2][4, 0] > 0.0,
        lambda: rollout(False, sections, groups, *operands),
        lambda: packed,
    )
    new = update(
        grads,
        grad_gain,
        stats,
        w_up,
        w_down,
        gains,
        m_up,
        m_down,
        m_gains,
        v_up,
        v_down,
        v_gains,
    )
    return (stats[0, 0], stats[3, 0], stats[1, 0]) + new


def solution(mesh):
    return jax.shard_map(
        per_device,
        mesh=mesh,
        in_specs=(
            P("dp", None),
            P("section", "dp", None),
            P("dp"),
            P("dp"),
            P("dp"),
            P("section", None, None, None),
            P("section", None, None, None),
            P("section", None, None),
            P("section", None, None, None),
            P("section", None, None, None),
            P("section", None, None),
            P("section", None, None, None),
            P("section", None, None, None),
            P("section", None, None),
        ),
        out_specs=(
            P(),
            P(),
            P(),
            P("section", None, None, None),
            P("section", None, None, None),
            P("section", None, None),
            P("section", None, None, None),
            P("section", None, None, None),
            P("section", None, None),
            P("section", None, None, None),
            P("section", None, None, None),
            P("section", None, None),
        ),
        check_vma=False,
    )
```

```python
import functools
import math

import jax
import jax.numpy as jnp
from jax import lax
from jax.experimental import pallas as pl
from jax.experimental.pallas import tpu as pltpu
from jax.sharding import PartitionSpec as P

NLAT = 128
STEP = 10

norm_eps = 1e-06
clip_limit = 0.05
beta_one = 0.9
beta_two = 0.999
adam_eps = 1e-08
learn_rate = 0.1
weight_decay = 0.01

f32, bf16 = jnp.float32, jnp.bfloat16
MESH = pl.DeviceIdType.MESH
LANES = 128
PIECE = 128
ROWS = 512
SPARE = 80
WINDOW = 1536
SAVE_BYTES = 21 * 1024 * 1024


def dot(a, b):
    return jnp.dot(a, b, preferred_element_type=f32)


def dot_lhs_t(a, b):
    return lax.dot_general(a, b, (((0,), (0,)), ((), ())), preferred_element_type=f32)


def split_dot(product, onehot, values):
    high = values.astype(bf16)
    low = (values - high.astype(f32)).astype(bf16)
    return product(onehot, high) + product(onehot, low)


def rollout_kernel(
    sections,
    groups,
    packing,
    inputs_ref,
    target_ref,
    len_hbm,
    lat_hbm,
    land_hbm,
    up_hbm,
    down_hbm,
    gain_hbm,
    grads_ref,
    stat_ref,
    miss_ref,
    xin,
    xout,
    cin,
    tgt,
    packed,
    save_x,
    save_h,
    save_d,
    qring,
    up_lo,
    up_t,
    down_lo,
    down_t,
    rank_ref,
    q_ref,
    scale_ref,
    weight_ref,
    loss_acc,
    gain_acc,
    wbuf,
    spread,
    len_ref,
    lat_ref,
    land_ref,
    gain_ref,
    up_ref,
    down_ref,
    acc,
    final,
    ybuf,
    zbuf,
    small,
    tiny,
    in_sem,
    tgt_sem,
    st_send,
    st_recv,
    ct_send,
    ct_recv,
    w_send,
    w_recv,
    y_send,
    y_recv,
    z_send,
    z_recv,
    za_send,
    za_recv,
    ya_send,
    ya_recv,
    small_send,
    small_recv,
    tiny_send,
    tiny_recv,
    out_sem,
    weight_sem,
):
    section = lax.axis_index("section")
    dp = lax.axis_index("dp")
    columns = xin.shape[0]
    feats = xin.shape[1]
    chunks = columns // ROWS
    live_rows = ROWS * (sections - 2) // sections
    prows = live_rows + 16
    total_packed = chunks * prows
    expand = live_rows + 512
    last = sections - 1
    ring = save_x.shape[0] // ROWS
    natural = section < (2 if packing else sections)
    plain_next = (section == 0) if packing else (section < last)
    packs = (section == 1) if packing else (section < 0)

    def peer(step):
        return (section, lax.rem(dp + step, groups))

    sources = (up_hbm, down_hbm, gain_hbm, len_hbm, lat_hbm, land_hbm)
    places = (up_ref, down_ref, gain_ref, len_ref, lat_ref, land_ref)
    fetches = [
        pltpu.make_async_copy(source, place, weight_sem.at[i])
        for i, (source, place) in enumerate(zip(sources, places))
    ]
    for fetch in fetches:
        fetch.start()

    barrier = pltpu.get_barrier_semaphore()
    for step in range(1, sections):
        other = lax.rem(section + step, sections)
        pl.semaphore_signal(barrier, inc=1, device_id=(other, dp), device_id_type=MESH)
    for step in range(1, groups):
        pl.semaphore_signal(barrier, inc=1, device_id=peer(step), device_id_type=MESH)

    def rows_at(index, size, align=16):
        return pl.ds(pl.multiple_of(index, align), size)

    def input_copy(i):
        rows = rows_at(i * ROWS, ROWS)
        return pltpu.make_async_copy(inputs_ref.at[rows], xin.at[rows], in_sem.at[i])

    def target_copy(i):
        rows = rows_at(i * ROWS, ROWS)
        return pltpu.make_async_copy(target_ref.at[rows], tgt.at[rows], tgt_sem.at[i])

    @pl.when(section == 0)
    def _():
        @pl.loop(0, chunks)
        def _(i):
            input_copy(i).start()

    @pl.loop(0, chunks)
    def _(i):
        target_copy(i).start()

    def prepare_backward():
        for layer in range(2):
            up_t[layer] = up_ref[layer].T.astype(bf16)
            down_t[layer] = (0.5 * down_ref[layer]).T.astype(bf16)
            gain_acc[layer] = jnp.zeros((8, feats), f32)
        for i in range(4):
            acc[i] = jnp.zeros((feats, feats), f32)
        loss_acc[...] = jnp.zeros_like(loss_acc)

    grid_rows = columns // LANES
    tile_row = lax.broadcasted_iota(jnp.int32, (8, LANES), 0)

    def window_start(j):
        shift = jnp.where(j < 7, 0, jnp.where(j < 11, 256, 384))
        return jnp.clip(ROWS * (j - 1) + shift, 0, columns - WINDOW)

    def expand_start(k):
        return jnp.clip(live_rows * k - 272, 0, total_packed - expand)

    def chunks_for(k):
        return (expand_start(k) + expand - 1) // prows

    def weight_copy(step):
        return pltpu.make_async_remote_copy(
            src_ref=wbuf.at[dp],
            dst_ref=wbuf.at[dp],
            send_sem=w_send.at[step],
            recv_sem=w_recv.at[step],
            device_id=peer(step),
            device_id_type=MESH,
        )

    def prepare_columns():
        length = len_ref[...]
        latitude = (lat_ref[...].astype(f32) + 0.5) * (math.pi / NLAT) - math.pi / 2
        area = jnp.cos(latitude) * (1.0 + land_ref[...].astype(f32))
        q_ref[...] = area * (section < length).astype(f32)
        local_weight = jnp.sum(
            area * jnp.minimum(length, sections).astype(f32), axis=(0, 1), keepdims=True
        )
        misses = jnp.zeros((1, 1), f32)
        if packing:
            beyond = length > 2
            flag = beyond.astype(bf16)
            lane_a = lax.broadcasted_iota(jnp.int32, (LANES, LANES), 0)
            lane_b = lax.broadcasted_iota(jnp.int32, (LANES, LANES), 1)
            within = dot(flag, (lane_a < lane_b).astype(bf16))
            row_total = jnp.sum(flag.astype(f32), axis=1, keepdims=True)
            row_a = lax.broadcasted_iota(jnp.int32, (grid_rows, grid_rows), 0)
            row_b = lax.broadcasted_iota(jnp.int32, (grid_rows, grid_rows), 1)
            before = dot(
                (row_b < row_a).astype(bf16),
                jnp.broadcast_to(row_total, (grid_rows, LANES)).astype(bf16),
            )
            rank = jnp.where(beyond, within + before, -1e6)
            rank_ref[...] = rank
            place = (
                lax.broadcasted_iota(jnp.int32, (grid_rows, LANES), 0) * LANES
                + lax.broadcasted_iota(jnp.int32, (grid_rows, LANES), 1)
            )
            rank_i = rank.astype(jnp.int32)
            missed = beyond & (rank_i >= total_packed - SPARE)
            for j in range(chunks):
                shift = 0 if j < 7 else 256 if j < 11 else 384
                start = min(max(ROWS * (j - 1) + shift, 0), columns - WINDOW)
                member = (rank_i >= j * prows) & (rank_i < (j + 1) * prows)
                ready = ROWS * (j + 2 if j < 7 else j + 3)
                missed |= member & ((place < start) | (place >= min(start + WINDOW, ready)))
            row_chunk = lax.broadcasted_iota(jnp.int32, (grid_rows, LANES), 0) // (ROWS // LANES)
            row_start = jnp.clip(live_rows * row_chunk - 272, 0, total_packed - expand)
            missed |= beyond & ((rank_i < row_start) | (rank_i >= row_start + expand))
            misses = jnp.sum(missed.astype(f32), axis=(0, 1), keepdims=True)
        wbuf[dp] = jnp.where(tile_row < 4, local_weight, misses)
        for step in range(1, groups):
            weight_copy(step).start()

    def finish_weights():
        for step in range(1, groups):
            weight_copy(step).wait_recv()
        total = wbuf[0]
        for other in range(1, groups):
            total = total + wbuf[other]
        weight_ref[...] = total
        miss_ref[...] = (total[4:5, 0:1] > 0.0).astype(jnp.int32)
        scale_ref[...] = 2.0 / jnp.broadcast_to(total[0:1], (8, LANES))

    for fetch in fetches:
        fetch.wait()
    for layer in range(2):
        up_lo[layer] = (0.5 * up_ref[layer]).astype(bf16)
        down_lo[layer] = down_ref[layer].astype(bf16)
    pl.semaphore_wait(barrier, sections - 1 + groups - 1)

    def pack_matrix(j):
        start = window_start(j)
        base = (j * prows).astype(f32)
        target_row = lax.broadcasted_iota(jnp.int32, (prows, LANES), 0).astype(f32)
        first = start // LANES
        hits = []
        for i in range(WINDOW // LANES):
            hits.append(target_row == rank_ref[pl.ds(first + i, 1), :] - base)
        return start, first, hits

    def as_onehot(hits):
        return jnp.concatenate([jnp.where(hit, 1.0, 0.0).astype(bf16) for hit in hits], axis=1)

    def unpack_rows(k):
        start = expand_start(k)
        base = start.astype(f32)
        source_row = lax.broadcasted_iota(jnp.int32, (expand, LANES), 0).astype(f32)
        hits = []
        for i in range(ROWS // LANES):
            hits.append(source_row == rank_ref[pl.ds(k * (ROWS // LANES) + i, 1), :] - base)
        return dot_lhs_t(as_onehot(hits), cin[rows_at(start, expand), :].astype(bf16))

    def forward(rows, saved):
        x = xin[rows, :]
        for layer in range(2):
            if layer == 1:
                save_x[saved, :] = x
            r = lax.rsqrt(jnp.mean(x * x, -1, keepdims=True) + norm_eps)
            normed = (x * r * gain_ref[layer : layer + 1]).astype(bf16)
            half = dot(normed, up_lo[layer])
            t = jnp.tanh(half)
            a = 1.0 + t
            h = half * a
            hidden = h.astype(bf16)
            save_h[layer, saved, :] = hidden
            save_d[layer, saved, :] = (a + h * (1.0 - t)).astype(bf16)
            x = x + dot(hidden, down_lo[layer])
        xout[rows, :] = x

    def loss_part(size, diff, weight):
        weighted = jnp.concatenate(
            [diff[:, :LANES] * weight, diff[:, LANES:] * weight], axis=1
        )
        loss_acc[...] += jnp.sum((weighted * diff).reshape(size // 8, 8, feats), 0)
        return weighted * scale_ref[0:1, 0:1]

    def backward(size, rows, saved, g):
        for layer in (1, 0):
            low = g.astype(bf16)
            acc[2 + layer] += dot_lhs_t(save_h[layer, saved, :], low)
            pull = dot(low, down_t[layer])
            g_pre = (pull * save_d[layer, saved, :].astype(f32)).astype(bf16)
            x = save_x[saved, :] if layer == 1 else xin[rows, :]
            r = lax.rsqrt(jnp.mean(x * x, -1, keepdims=True) + norm_eps)
            gain = gain_ref[layer : layer + 1]
            xr = x * r
            normed = (xr * gain).astype(bf16)
            acc[layer] += dot_lhs_t(normed, g_pre)
            g_normed = dot(g_pre, up_t[layer])
            prod = g_normed * xr
            gain_acc[layer] += jnp.sum(prod.reshape(size // 8, 8, feats), 0)
            mean = jnp.mean(prod * gain, -1, keepdims=True)
            g = g + r * (gain * g_normed - xr * mean)
        xin[rows, :] = g

    def state_copy(source, size, i, count=None):
        rows = rows_at(i * size, size if count is None else count)
        return pltpu.make_async_remote_copy(
            src_ref=source.at[rows],
            dst_ref=xin.at[rows],
            send_sem=st_send.at[i],
            recv_sem=st_recv.at[i],
            device_id=(lax.rem(section + 1, sections), dp),
            device_id_type=MESH,
        )

    def cot_copy(size, i, count=None):
        rows = rows_at(i * size, size if count is None else count)
        return pltpu.make_async_remote_copy(
            src_ref=xin.at[rows],
            dst_ref=cin.at[rows],
            send_sem=ct_send.at[i],
            recv_sem=ct_recv.at[i],
            device_id=(lax.rem(section + sections - 1, sections), dp),
            device_id_type=MESH,
        )

    def shorter(copy, size, i, action):
        @pl.when(i < chunks - 1)
        def _():
            action(copy(size, i, size))

        @pl.when(i == chunks - 1)
        def _():
            action(copy(size, i, size - SPARE))

    def packed_state(size, i, count):
        return state_copy(packed, size, i, count)

    def packed_receive(size, i):
        @pl.when(section == 2)
        def _():
            shorter(packed_state, size, i, lambda copy: copy.wait_recv())

        @pl.when(section > 2)
        def _():
            state_copy(xout, size, i).wait_recv()

    def cot_part(size, i, count):
        return cot_copy(size, i, count)

    def cot_wait(size, i):
        shorter(cot_part, size, i, lambda copy: copy.wait_recv())

    def cot_do(size, i, action):
        @pl.when(section == 2)
        def _():
            shorter(cot_part, size, i, action)

        @pl.when(section > 2)
        def _():
            action(cot_copy(size, i))

    @pl.when(natural)
    def _():
        if packing:
            lag = jnp.where(section == 0, ring - 1, ring - 3)
        else:
            lag = jnp.minimum(ring - 1, 3 * (last - section))

        @pl.when(section > 0)
        def _():
            prepare_columns()
            prepare_backward()
            if packing:
                xout[2 * ROWS : WINDOW, :] = jnp.zeros((WINDOW - 2 * ROWS, feats), f32)
                cin[total_packed - SPARE : total_packed, :] = jnp.zeros((SPARE, feats), f32)

        @pl.loop(0, chunks + lag)
        def _(t):
            @pl.when(t < chunks)
            def _():
                @pl.when(section == 0)
                def _():
                    input_copy(t).wait()

                @pl.when(section > 0)
                def _():
                    state_copy(xout, ROWS, t).wait_recv()

                rows = rows_at(t * ROWS, ROWS)
                saved = rows_at(lax.rem(t, ring) * ROWS, ROWS)
                forward(rows, saved)

                @pl.when(plain_next)
                def _():
                    state_copy(xout, ROWS, t).start()

            if packing:

                j = jnp.where(t < 8, t - 1, t - 2)

                @pl.when(packs & (t >= 1) & (t != 8) & (j < chunks))
                def _():
                    start, _, hits = pack_matrix(j)
                    packed[rows_at(j * prows, prows), :] = split_dot(
                        dot, as_onehot(hits), xout[rows_at(start, WINDOW), :]
                    )
                    shorter(packed_state, prows, j, lambda copy: copy.start())

            @pl.when((section == 0) & (t == 3))
            def _():
                prepare_columns()
                prepare_backward()

            k = t - lag

            @pl.when((k >= 0) & (k < chunks))
            def _():
                @pl.when(k == 0)
                def _():
                    finish_weights()

                target_copy(k).wait()
                rows = rows_at(k * ROWS, ROWS)
                saved = rows_at(lax.rem(k, ring) * ROWS, ROWS)

                @pl.when(plain_next)
                def _():
                    cot_copy(ROWS, k).wait_recv()
                    spread[...] = cin[rows, :]

                if packing:

                    @pl.when(packs)
                    def _():
                        had = jnp.where(k == 0, -1, chunks_for(jnp.maximum(k - 1, 0)))
                        for i in range(3):

                            @pl.when(had + 1 + i <= chunks_for(k))
                            def _():
                                cot_wait(prows, had + 1 + i)

                        spread[...] = unpack_rows(k)

                else:

                    @pl.when(section == last)
                    def _():
                        spread[...] = jnp.zeros_like(spread)

                weight = jnp.concatenate(
                    [
                        jnp.broadcast_to(
                            q_ref[pl.ds(k * (ROWS // LANES) + i, 1), :], (LANES, LANES)
                        ).T
                        for i in range(ROWS // LANES)
                    ],
                    axis=0,
                )
                diff = xout[rows, :] - tgt[rows, :]
                g = loss_part(ROWS, diff, weight) + spread[...]
                backward(ROWS, rows, saved, g)

                @pl.when(section > 0)
                def _():
                    cot_copy(ROWS, k).start()

        @pl.loop(0, chunks)
        def _(i):
            @pl.when(plain_next)
            def _():
                state_copy(xout, ROWS, i).wait_send()

            if packing:

                @pl.when(packs)
                def _():
                    shorter(packed_state, prows, i, lambda copy: copy.wait_send())

            @pl.when(section > 0)
            def _():
                cot_copy(ROWS, i).wait_send()

    if packing:

        @pl.when(jnp.logical_not(natural))
        def _():
            lag = last - section
            prepare_columns()
            prepare_backward()

            @pl.when(section == 2)
            def _():
                xin[total_packed - SPARE : total_packed, :] = jnp.zeros((SPARE, feats), f32)


            @pl.loop(0, chunks + lag)
            def _(t):
                @pl.when(t < chunks)
                def _():
                    @pl.when(t == 0)
                    def _():
                        target_copy(0).wait()
                        target_copy(1).wait()

                    @pl.when(t + 2 < chunks)
                    def _():
                        target_copy(t + 2).wait()

                    start, first, hits = pack_matrix(t)
                    rows = rows_at(t * prows, prows)
                    packed[rows, :] = split_dot(
                        dot, as_onehot(hits), tgt[rows_at(start, WINDOW), :]
                    )
                    weight = jnp.zeros((prows, LANES), f32)
                    for i, hit in enumerate(hits):
                        weight += jnp.where(hit, q_ref[pl.ds(first + i, 1), :], 0.0)
                    qring[lax.rem(t, sections)] = jnp.broadcast_to(
                        jnp.sum(weight, -1, keepdims=True), (prows, LANES)
                    )
                    packed_receive(prows, t)
                    saved = rows_at(lax.rem(t, ring) * ROWS, prows)
                    forward(rows, saved)

                    @pl.when(section < last)
                    def _():
                        state_copy(xout, prows, t).start()

                k = t - lag

                @pl.when(k >= 0)
                def _():
                    @pl.when(k == 0)
                    def _():
                        finish_weights()

                    rows = rows_at(k * prows, prows)
                    saved = rows_at(lax.rem(k, ring) * ROWS, prows)
                    diff = xout[rows, :] - packed[rows, :]
                    spread[0:prows, :] = loss_part(prows, diff, qring[lax.rem(k, sections)])

                    @pl.when(section < last)
                    def _():
                        cot_copy(prows, k).wait_recv()
                        spread[0:prows, :] += cin[rows, :]

                    backward(prows, rows, saved, spread[0:prows, :])
                    cot_do(prows, k, lambda copy: copy.start())

            @pl.loop(0, chunks)
            def _(i):
                cot_do(prows, i, lambda copy: copy.wait_send())

                @pl.when(section < last)
                def _():
                    state_copy(xout, prows, i).wait_send()

    depth = min(4, groups)
    width = groups // depth
    y, z = lax.rem(dp, width), dp // width
    ypart, zpart = PIECE // width, PIECE // groups
    halves = feats // PIECE
    pieces = range(4 * halves)
    matrix = [m for m in (3, 1, 2, 0) for _ in range(halves)]
    first = [PIECE * (p % halves) for p in pieces]
    ysum = save_x

    def y_copy(p, step):
        to = lax.rem(y + step, width)
        i = p * width + step
        return pltpu.make_async_remote_copy(
            src_ref=acc.at[matrix[p], rows_at(first[p] + to * ypart, ypart)],
            dst_ref=ybuf.at[p * (width - 1) + step - 1],
            send_sem=y_send.at[i],
            recv_sem=y_recv.at[i],
            device_id=(section, z * width + to),
            device_id_type=MESH,
        )

    def z_copy(p, step):
        to = lax.rem(z + step, depth)
        i = p * depth + step
        return pltpu.make_async_remote_copy(
            src_ref=ysum.at[rows_at(p * ypart + to * zpart, zpart)],
            dst_ref=zbuf.at[p * (depth - 1) + step - 1],
            send_sem=z_send.at[i],
            recv_sem=z_recv.at[i],
            device_id=(section, to * width + y),
            device_id_type=MESH,
        )

    def z_back(p, step):
        to = lax.rem(z + step, depth)
        i = p * depth + step
        rows = rows_at(first[p] + y * ypart + z * zpart, zpart)
        return pltpu.make_async_remote_copy(
            src_ref=final.at[matrix[p], rows],
            dst_ref=final.at[matrix[p], rows],
            send_sem=za_send.at[i],
            recv_sem=za_recv.at[i],
            device_id=(section, to * width + y),
            device_id_type=MESH,
        )

    def y_back(p, step):
        to = lax.rem(y + step, width)
        i = p * width + step
        rows = rows_at(first[p] + y * ypart, ypart)
        return pltpu.make_async_remote_copy(
            src_ref=final.at[matrix[p], rows],
            dst_ref=final.at[matrix[p], rows],
            send_sem=ya_send.at[i],
            recv_sem=ya_recv.at[i],
            device_id=(section, z * width + to),
            device_id_type=MESH,
        )

    def small_copy(step):
        return pltpu.make_async_remote_copy(
            src_ref=small.at[dp],
            dst_ref=small.at[dp],
            send_sem=small_send.at[step],
            recv_sem=small_recv.at[step],
            device_id=peer(step),
            device_id_type=MESH,
        )

    def tiny_copy(step):
        return pltpu.make_async_remote_copy(
            src_ref=tiny.at[section],
            dst_ref=tiny.at[section],
            send_sem=tiny_send.at[step],
            recv_sem=tiny_recv.at[step],
            device_id=(lax.rem(section + step, sections), dp),
            device_id_type=MESH,
        )

    def out_copy(p):
        rows = pl.ds(first[p], PIECE)
        return pltpu.make_async_copy(
            final.at[matrix[p], rows], grads_ref.at[matrix[p], rows], out_sem.at[p]
        )

    for p in pieces:
        for step in range(1, width):
            y_copy(p, step).start()
    for p in pieces:
        own = acc[matrix[p], rows_at(first[p] + y * ypart, ypart), :]
        for step in range(1, width):
            y_copy(p, step).wait_recv()
            own = own + ybuf[p * (width - 1) + step - 1]
        ysum[p * ypart : (p + 1) * ypart, :] = own
        for step in range(1, depth):
            z_copy(p, step).start()
    squares = jnp.zeros((1, 1), f32)
    for p in pieces:
        own = ysum[rows_at(p * ypart + z * zpart, zpart), :]
        for step in range(1, depth):
            z_copy(p, step).wait_recv()
            own = own + zbuf[p * (depth - 1) + step - 1]
        final[matrix[p], rows_at(first[p] + y * ypart + z * zpart, zpart), :] = own
        squares = squares + jnp.sum(own * own, axis=(0, 1), keepdims=True)
        for step in range(1, depth):
            z_back(p, step).start()
    loss = jnp.sum(loss_acc[...], axis=(0, 1), keepdims=True)
    wide_row = lax.broadcasted_iota(jnp.int32, (8, feats), 0)
    small[dp] = jnp.where(
        wide_row == 0,
        jnp.sum(gain_acc[0], 0, keepdims=True),
        jnp.where(
            wide_row == 1,
            jnp.sum(gain_acc[1], 0, keepdims=True),
            jnp.where(wide_row < 4, loss, squares),
        ),
    )
    for step in range(1, groups):
        small_copy(step).start()
    for p in pieces:
        for step in range(1, depth):
            z_back(p, step).wait_recv()
        for step in range(1, width):
            y_back(p, step).start()
    for step in range(1, groups):
        small_copy(step).wait_recv()
    total = small[0]
    for other in range(1, groups):
        total = total + small[other]
    gain_squares = jnp.sum(total[0:2] * total[0:2], axis=(0, 1), keepdims=True)
    tiny[section] = jnp.where(tile_row < 4, total[2:3, 0:1], total[4:5, 0:1] + gain_squares)
    for step in range(1, sections):
        tiny_copy(step).start()
    for p in pieces:
        for step in range(1, width):
            y_back(p, step).wait_recv()
        out_copy(p).start()
    for step in range(1, sections):
        tiny_copy(step).wait_recv()
    whole = tiny[0]
    for other in range(1, sections):
        whole = whole + tiny[other]
    norm = jnp.sqrt(whole[4:5, 0:1])
    clip = jnp.minimum(1.0, clip_limit / norm)
    stats = total
    for row, number in ((2, clip), (3, whole[0:1, 0:1]), (4, weight_ref[0:1, 0:1]), (5, norm)):
        stats = jnp.where(wide_row == row, number, stats)
    stat_ref[...] = stats

    for step in range(1, groups):
        weight_copy(step).wait_send()
        small_copy(step).wait_send()
    for step in range(1, sections):
        tiny_copy(step).wait_send()
    for p in pieces:
        out_copy(p).wait()
        for step in range(1, width):
            y_copy(p, step).wait_send()
            y_back(p, step).wait_send()
        for step in range(1, depth):
            z_copy(p, step).wait_send()
            z_back(p, step).wait_send()


def rollout(packing, sections, groups, inputs, target, lengths, lat_index, land, w_up, w_down, gains):
    columns, feats = inputs.shape
    chunks = columns // ROWS
    prows = ROWS * (sections - 2) // sections + 16
    grid_rows = columns // LANES
    packed_bytes = 4 * chunks * prows * feats
    ring = (SAVE_BYTES - packed_bytes) // (12 * ROWS * feats)
    depth = min(4, groups)
    width = groups // depth
    pieces = 4 * feats // PIECE
    hbm = pl.BlockSpec(memory_space=pl.ANY)
    vmem = pl.BlockSpec(memory_space=pltpu.VMEM)
    dma = pltpu.SemaphoreType.DMA
    wide = pltpu.VMEM((columns, feats), f32)
    lows = pltpu.VMEM((2, feats, feats), bf16)
    grads = pltpu.VMEM((4, feats, feats), f32)
    square = pltpu.VMEM((2, feats, feats), f32)
    flat = lambda array: array.reshape(grid_rows, LANES)
    return pl.pallas_call(
        functools.partial(rollout_kernel, sections, groups, packing),
        out_shape=(
            jax.ShapeDtypeStruct((4, feats, feats), f32),
            jax.ShapeDtypeStruct((8, feats), f32),
            jax.ShapeDtypeStruct((1, 1), jnp.int32),
        ),
        in_specs=[hbm] * 8,
        out_specs=(hbm, vmem, vmem),
        scratch_shapes=[
            wide,
            wide,
            wide,
            wide,
            pltpu.VMEM((chunks * prows if packing else 8, feats), f32),
            pltpu.VMEM((ring * ROWS, feats), f32),
            pltpu.VMEM((2, ring * ROWS, feats), bf16),
            pltpu.VMEM((2, ring * ROWS, feats), bf16),
            pltpu.VMEM((sections, prows, LANES), f32),
            lows,
            lows,
            lows,
            lows,
            pltpu.VMEM((grid_rows, LANES), f32),
            pltpu.VMEM((grid_rows, LANES), f32),
            pltpu.VMEM((8, LANES), f32),
            pltpu.VMEM((8, LANES), f32),
            pltpu.VMEM((8, feats), f32),
            pltpu.VMEM((2, 8, feats), f32),
            pltpu.VMEM((groups, 8, LANES), f32),
            pltpu.VMEM((ROWS, feats), f32),
            pltpu.VMEM((grid_rows, LANES), jnp.int32),
            pltpu.VMEM((grid_rows, LANES), jnp.int32),
            pltpu.VMEM((grid_rows, LANES), jnp.int32),
            pltpu.VMEM((2, feats), f32),
            square,
            square,
            grads,
            grads,
            pltpu.VMEM((max(pieces * (width - 1), 1), PIECE // width, feats), f32),
            pltpu.VMEM((pieces * (depth - 1), PIECE // groups, feats), f32),
            pltpu.VMEM((groups, 8, feats), f32),
            pltpu.VMEM((sections, 8, LANES), f32),
            dma((chunks,)),
            dma((chunks,)),
            dma((chunks,)),
            dma((chunks,)),
            dma((chunks,)),
            dma((chunks,)),
            dma((groups,)),
            dma((groups,)),
            dma((pieces * width,)),
            dma((pieces * width,)),
            dma((pieces * depth,)),
            dma((pieces * depth,)),
            dma((pieces * depth,)),
            dma((pieces * depth,)),
            dma((pieces * width,)),
            dma((pieces * width,)),
            dma((groups,)),
            dma((groups,)),
            dma((sections,)),
            dma((sections,)),
            dma((pieces,)),
            dma((6,)),
        ],
        compiler_params=pltpu.CompilerParams(
            collective_id=0 if packing else 1,
            has_side_effects=True,
            vmem_limit_bytes=63 * 1024 * 1024,
        ),
        name="rollout_packed" if packing else "rollout_all",
    )(
        inputs,
        target,
        flat(lengths),
        flat(lat_index),
        flat(land),
        w_up,
        w_down,
        gains,
    )


def adam_step(weights_old, gradient, moment_one, moment_two, decay_rate):
    moment_one = beta_one * moment_one + (1.0 - beta_one) * gradient
    moment_two = beta_two * moment_two + (1.0 - beta_two) * gradient * gradient
    second_hat = moment_two * (1.0 / (1.0 - beta_two**STEP))
    root = second_hat * lax.rsqrt(second_hat)
    pace = moment_one * (learn_rate / (1.0 - beta_one**STEP))
    step = pace * pl.reciprocal(root + adam_eps)
    new_weights = weights_old * (1.0 - learn_rate * decay_rate) - step
    return (new_weights, moment_one, moment_two)


def update_kernel(
    grads_ref,
    stat_hbm,
    w_up,
    w_down,
    gains,
    m_up,
    m_down,
    m_gains,
    v_up,
    v_down,
    v_gains,
    loss_out,
    total_out,
    norm_out,
    new_up,
    new_down,
    new_gains,
    new_m_up,
    new_m_down,
    new_m_gains,
    new_v_up,
    new_v_down,
    new_v_gains,
    held,
    stat_ref,
    gain_ref,
    in_sem,
    out_sem,
    small_in,
    small_out,
):
    old = ((grads_ref, grads_ref), (w_up, w_down), (m_up, m_down), (v_up, v_down))
    new = ((new_up, new_down), (new_m_up, new_m_down), (new_v_up, new_v_down))

    def fetch(i, part):
        source = old[part][i // 2].at[i if part == 0 else i % 2]
        return pltpu.make_async_copy(source, held.at[part, i], in_sem.at[part, i])

    def store(i, part):
        return pltpu.make_async_copy(
            held.at[part + 1, i], new[part][i // 2].at[i % 2], out_sem.at[part, i]
        )

    small_fetch = [pltpu.make_async_copy(stat_hbm, stat_ref, small_in.at[3])]
    small_store = []
    for part, (source, out) in enumerate(
        ((gains, new_gains), (m_gains, new_m_gains), (v_gains, new_v_gains))
    ):
        small_fetch.append(pltpu.make_async_copy(source, gain_ref.at[part], small_in.at[part]))
        small_store.append(pltpu.make_async_copy(gain_ref.at[part], out, small_out.at[part]))
    for copy in small_fetch:
        copy.start()
    for i in range(4):
        for part in range(4):
            fetch(i, part).start()
    for copy in small_fetch:
        copy.wait()
    clip = stat_ref[2:3, 0:1]
    for row, out in ((3, loss_out), (4, total_out), (5, norm_out)):
        out[...] = stat_ref[row : row + 1, 0:1]
    fresh = adam_step(gain_ref[0], stat_ref[0:2] * clip, gain_ref[1], gain_ref[2], 0.0)
    for part in range(3):
        gain_ref[part] = fresh[part]
        small_store[part].start()
    for i in range(4):
        for part in range(4):
            fetch(i, part).wait()
        fresh = adam_step(held[1, i], held[0, i] * clip, held[2, i], held[3, i], weight_decay)
        for part in range(3):
            held[part + 1, i] = fresh[part]
            store(i, part).start()
    for i in range(4):
        for part in range(3):
            store(i, part).wait()
    for copy in small_store:
        copy.wait()


def update(grads, stats, *state):
    hbm = pl.BlockSpec(memory_space=pl.ANY)
    vmem = pl.BlockSpec(memory_space=pltpu.VMEM)
    return pl.pallas_call(
        update_kernel,
        in_specs=[hbm] * 11,
        out_specs=(vmem,) * 3 + (hbm,) * 9,
        out_shape=(jax.ShapeDtypeStruct((1, 1), f32),) * 3
        + tuple(jax.ShapeDtypeStruct(a.shape, f32) for a in state),
        scratch_shapes=[
            pltpu.VMEM((4,) + grads.shape, f32),
            pltpu.VMEM(stats.shape, f32),
            pltpu.VMEM((3,) + state[2].shape, f32),
            pltpu.SemaphoreType.DMA((4, 4)),
            pltpu.SemaphoreType.DMA((3, 4)),
            pltpu.SemaphoreType.DMA((4,)),
            pltpu.SemaphoreType.DMA((3,)),
        ],
        compiler_params=pltpu.CompilerParams(vmem_limit_bytes=63 * 1024 * 1024),
        name="update",
    )(grads, stats, *state)


def per_device(
    inputs,
    targets,
    lengths,
    lat_index,
    land,
    w_up,
    w_down,
    gains,
    m_up,
    m_down,
    m_gains,
    v_up,
    v_down,
    v_gains,
):
    sections, groups = lax.axis_size("section"), lax.axis_size("dp")
    state = tuple(
        a[0] for a in (w_up, w_down, gains, m_up, m_down, m_gains, v_up, v_down, v_gains)
    )
    operands = (inputs, targets[0], lengths, lat_index, land) + state[:3]
    packed = rollout(True, sections, groups, *operands)

    grads, stats, unused = lax.cond(
        packed[2].reshape(()) > 0,
        lambda: rollout(False, sections, groups, *operands),
        lambda: packed,
    )
    new = update(grads, stats, *state)
    return tuple(a.reshape(()) for a in new[:3]) + tuple(a[None] for a in new[3:])


def solution(mesh):
    return jax.shard_map(
        per_device,
        mesh=mesh,
        in_specs=(
            P("dp", None),
            P("section", "dp", None),
            P("dp"),
            P("dp"),
            P("dp"),
            P("section", None, None, None),
            P("section", None, None, None),
            P("section", None, None),
            P("section", None, None, None),
            P("section", None, None, None),
            P("section", None, None),
            P("section", None, None, None),
            P("section", None, None, None),
            P("section", None, None),
        ),
        out_specs=(
            P(),
            P(),
            P(),
            P("section", None, None, None),
            P("section", None, None, None),
            P("section", None, None),
            P("section", None, None, None),
            P("section", None, None, None),
            P("section", None, None),
            P("section", None, None, None),
            P("section", None, None, None),
            P("section", None, None),
        ),
        check_vma=False,
    )
```

```python
import functools
import math

import jax
import jax.numpy as jnp
from jax import lax
from jax.experimental import pallas as pl
from jax.experimental.pallas import tpu as pltpu
from jax.sharding import PartitionSpec as P

NLAT = 128
STEP = 10

norm_eps = 1e-06
clip_limit = 0.05
beta_one = 0.9
beta_two = 0.999
adam_eps = 1e-08
learn_rate = 0.1
weight_decay = 0.01

f32, bf16 = jnp.float32, jnp.bfloat16
MESH = pl.DeviceIdType.MESH
LANES = 128
PIECE = 128
ROWS = 512
SPARE = 80
WINDOW = 1536
SAVE_BYTES = 19 * 1024 * 1024
NEAR = 4


def dot(a, b):
    return jnp.dot(a, b, preferred_element_type=f32)


def dot_lhs_t(a, b):
    return lax.dot_general(a, b, (((0,), (0,)), ((), ())), preferred_element_type=f32)


def split_dot(product, onehot, values):
    high = values.astype(bf16)
    low = (values - high.astype(f32)).astype(bf16)
    return product(onehot, high) + product(onehot, low)


def rollout_kernel(
    sections,
    groups,
    packing,
    inputs_ref,
    target_ref,
    len_hbm,
    lat_hbm,
    land_hbm,
    up_hbm,
    down_hbm,
    gain_hbm,
    grads_ref,
    stat_ref,
    miss_ref,
    xin,
    xout,
    cin,
    tgt,
    packed,
    near,
    save_h,
    save_d,
    qring,
    up_lo,
    up_t,
    down_lo,
    down_t,
    rank_ref,
    q_ref,
    scale_ref,
    weight_ref,
    loss_acc,
    gain_acc,
    wbuf,
    spread,
    len_ref,
    lat_ref,
    land_ref,
    gain_ref,
    up_ref,
    down_ref,
    acc,
    final,
    ybuf,
    zbuf,
    small,
    tiny,
    in_sem,
    tgt_sem,
    st_send,
    st_recv,
    ct_send,
    ct_recv,
    w_send,
    w_recv,
    y_send,
    y_recv,
    z_send,
    z_recv,
    za_send,
    za_recv,
    ya_send,
    ya_recv,
    small_send,
    small_recv,
    tiny_send,
    tiny_recv,
    out_sem,
    weight_sem,
):
    section = lax.axis_index("section")
    dp = lax.axis_index("dp")
    columns = xin.shape[0]
    feats = xin.shape[1]
    chunks = columns // ROWS
    live_rows = ROWS * (sections - 2) // sections
    prows = live_rows + 16
    total_packed = chunks * prows
    expand = live_rows + 512
    last = sections - 1
    ring = save_h.shape[1] // ROWS
    ring_packed = near.shape[0] // prows
    natural = section < (2 if packing else sections)
    plain_next = (section == 0) if packing else (section < last)
    packs = (section == 1) if packing else (section < 0)

    def peer(step):
        return (section, lax.rem(dp + step, groups))

    sources = (up_hbm, down_hbm, gain_hbm, len_hbm, lat_hbm, land_hbm)
    places = (up_ref, down_ref, gain_ref, len_ref, lat_ref, land_ref)
    fetches = [
        pltpu.make_async_copy(source, place, weight_sem.at[i])
        for i, (source, place) in enumerate(zip(sources, places))
    ]
    for fetch in fetches:
        fetch.start()

    barrier = pltpu.get_barrier_semaphore()
    for step in range(1, sections):
        other = lax.rem(section + step, sections)
        pl.semaphore_signal(barrier, inc=1, device_id=(other, dp), device_id_type=MESH)
    for step in range(1, groups):
        pl.semaphore_signal(barrier, inc=1, device_id=peer(step), device_id_type=MESH)

    def rows_at(index, size, align=16):
        return pl.ds(pl.multiple_of(index, align), size)

    def input_copy(i):
        rows = rows_at(i * ROWS, ROWS)
        return pltpu.make_async_copy(inputs_ref.at[rows], xin.at[rows], in_sem.at[i])

    def target_copy(i):
        rows = rows_at(i * ROWS, ROWS)
        return pltpu.make_async_copy(target_ref.at[rows], tgt.at[rows], tgt_sem.at[i])

    def near_copy(i):
        place = rows_at(lax.rem(i, NEAR) * ROWS, ROWS)
        return pltpu.make_async_copy(
            target_ref.at[rows_at(i * ROWS, ROWS)], near.at[place], tgt_sem.at[i]
        )

    @pl.when(section == 0)
    def _():
        @pl.loop(0, chunks)
        def _(i):
            input_copy(i).start()

    @pl.when(natural)
    def _():
        @pl.loop(0, NEAR)
        def _(i):
            near_copy(i).start()

    @pl.when(jnp.logical_not(natural))
    def _():
        @pl.loop(0, chunks)
        def _(i):
            target_copy(i).start()

    def prepare_backward():
        for layer in range(2):
            up_t[layer] = up_ref[layer].T.astype(bf16)
            down_t[layer] = (0.5 * down_ref[layer]).T.astype(bf16)
            gain_acc[layer] = jnp.zeros((8, feats), f32)
        for i in range(4):
            acc[i] = jnp.zeros((feats, feats), f32)
        loss_acc[...] = jnp.zeros_like(loss_acc)

    grid_rows = columns // LANES
    tile_row = lax.broadcasted_iota(jnp.int32, (8, LANES), 0)

    def window_start(j):
        shift = jnp.where(j < 7, 0, jnp.where(j < 11, 256, 384))
        return jnp.clip(ROWS * (j - 1) + shift, 0, columns - WINDOW)

    def expand_start(k):
        return jnp.clip(live_rows * k - 272, 0, total_packed - expand)

    def chunks_for(k):
        return (expand_start(k) + expand - 1) // prows

    def weight_copy(step):
        return pltpu.make_async_remote_copy(
            src_ref=wbuf.at[dp],
            dst_ref=wbuf.at[dp],
            send_sem=w_send.at[step],
            recv_sem=w_recv.at[step],
            device_id=peer(step),
            device_id_type=MESH,
        )

    def prepare_columns():
        length = len_ref[...]
        latitude = (lat_ref[...].astype(f32) + 0.5) * (math.pi / NLAT) - math.pi / 2
        area = jnp.cos(latitude) * (1.0 + land_ref[...].astype(f32))
        q_ref[...] = area * (section < length).astype(f32)
        local_weight = jnp.sum(
            area * jnp.minimum(length, sections).astype(f32), axis=(0, 1), keepdims=True
        )
        misses = jnp.zeros((1, 1), f32)
        if packing:
            beyond = length > 2
            flag = beyond.astype(bf16)
            lane_a = lax.broadcasted_iota(jnp.int32, (LANES, LANES), 0)
            lane_b = lax.broadcasted_iota(jnp.int32, (LANES, LANES), 1)
            within = dot(flag, (lane_a < lane_b).astype(bf16))
            row_total = jnp.sum(flag.astype(f32), axis=1, keepdims=True)
            row_a = lax.broadcasted_iota(jnp.int32, (grid_rows, grid_rows), 0)
            row_b = lax.broadcasted_iota(jnp.int32, (grid_rows, grid_rows), 1)
            before = dot(
                (row_b < row_a).astype(bf16),
                jnp.broadcast_to(row_total, (grid_rows, LANES)).astype(bf16),
            )
            rank = jnp.where(beyond, within + before, -1e6)
            rank_ref[...] = rank
            place = (
                lax.broadcasted_iota(jnp.int32, (grid_rows, LANES), 0) * LANES
                + lax.broadcasted_iota(jnp.int32, (grid_rows, LANES), 1)
            )
            rank_i = rank.astype(jnp.int32)
            missed = beyond & (rank_i >= total_packed - SPARE)
            for j in range(chunks):
                shift = 0 if j < 7 else 256 if j < 11 else 384
                start = min(max(ROWS * (j - 1) + shift, 0), columns - WINDOW)
                member = (rank_i >= j * prows) & (rank_i < (j + 1) * prows)
                ready = ROWS * (j + 2 if j < 7 else j + 3)
                missed |= member & ((place < start) | (place >= min(start + WINDOW, ready)))
            row_chunk = lax.broadcasted_iota(jnp.int32, (grid_rows, LANES), 0) // (ROWS // LANES)
            row_start = jnp.clip(live_rows * row_chunk - 272, 0, total_packed - expand)
            missed |= beyond & ((rank_i < row_start) | (rank_i >= row_start + expand))
            misses = jnp.sum(missed.astype(f32), axis=(0, 1), keepdims=True)
        wbuf[dp] = jnp.where(tile_row < 4, local_weight, misses)
        for step in range(1, groups):
            weight_copy(step).start()

    def finish_weights():
        for step in range(1, groups):
            weight_copy(step).wait_recv()
        total = wbuf[0]
        for other in range(1, groups):
            total = total + wbuf[other]
        weight_ref[...] = total
        miss_ref[...] = (total[4:5, 0:1] > 0.0).astype(jnp.int32)
        scale_ref[...] = 2.0 / jnp.broadcast_to(total[0:1], (8, LANES))

    for fetch in fetches:
        fetch.wait()
    for layer in range(2):
        up_lo[layer] = (0.5 * up_ref[layer]).astype(bf16)
        down_lo[layer] = down_ref[layer].astype(bf16)
    pl.semaphore_wait(barrier, sections - 1 + groups - 1)

    def pack_matrix(j):
        start = window_start(j)
        base = (j * prows).astype(f32)
        target_row = lax.broadcasted_iota(jnp.int32, (prows, LANES), 0).astype(f32)
        first = start // LANES
        hits = []
        for i in range(WINDOW // LANES):
            hits.append(target_row == rank_ref[pl.ds(first + i, 1), :] - base)
        return start, first, hits

    def as_onehot(hits):
        return jnp.concatenate([jnp.where(hit, 1.0, 0.0).astype(bf16) for hit in hits], axis=1)

    def unpack_rows(k):
        start = expand_start(k)
        base = start.astype(f32)
        source_row = lax.broadcasted_iota(jnp.int32, (expand, LANES), 0).astype(f32)
        hits = []
        for i in range(ROWS // LANES):
            hits.append(source_row == rank_ref[pl.ds(k * (ROWS // LANES) + i, 1), :] - base)
        return dot_lhs_t(as_onehot(hits), cin[rows_at(start, expand), :].astype(bf16))

    def forward(rows, saved, keep):
        x = xin[rows, :]
        for layer in range(2):
            if layer == 1:
                keep[...] = x
            r = lax.rsqrt(jnp.mean(x * x, -1, keepdims=True) + norm_eps)
            normed = (x * r * gain_ref[layer : layer + 1]).astype(bf16)
            half = dot(normed, up_lo[layer])
            t = jnp.tanh(half)
            a = 1.0 + t
            h = half * a
            hidden = h.astype(bf16)
            save_h[layer, saved, :] = hidden
            save_d[layer, saved, :] = (a + h * (1.0 - t)).astype(bf16)
            x = x + dot(hidden, down_lo[layer])
        xout[rows, :] = x

    def loss_part(size, diff, weight):
        weighted = jnp.concatenate(
            [diff[:, :LANES] * weight, diff[:, LANES:] * weight], axis=1
        )
        loss_acc[...] += jnp.sum((weighted * diff).reshape(size // 8, 8, feats), 0)
        return weighted * scale_ref[0:1, 0:1]

    def backward(size, rows, saved, keep, g):
        for layer in (1, 0):
            low = g.astype(bf16)
            acc[2 + layer] += dot_lhs_t(save_h[layer, saved, :], low)
            pull = dot(low, down_t[layer])
            g_pre = (pull * save_d[layer, saved, :].astype(f32)).astype(bf16)
            x = keep[...] if layer == 1 else xin[rows, :]
            r = lax.rsqrt(jnp.mean(x * x, -1, keepdims=True) + norm_eps)
            gain = gain_ref[layer : layer + 1]
            xr = x * r
            normed = (xr * gain).astype(bf16)
            acc[layer] += dot_lhs_t(normed, g_pre)
            g_normed = dot(g_pre, up_t[layer])
            prod = g_normed * xr
            gain_acc[layer] += jnp.sum(prod.reshape(size // 8, 8, feats), 0)
            mean = jnp.mean(prod * gain, -1, keepdims=True)
            g = g + r * (gain * g_normed - xr * mean)
        xin[rows, :] = g

    def state_copy(source, size, i, count=None):
        rows = rows_at(i * size, size if count is None else count)
        return pltpu.make_async_remote_copy(
            src_ref=source.at[rows],
            dst_ref=xin.at[rows],
            send_sem=st_send.at[i],
            recv_sem=st_recv.at[i],
            device_id=(lax.rem(section + 1, sections), dp),
            device_id_type=MESH,
        )

    def cot_copy(size, i, count=None):
        rows = rows_at(i * size, size if count is None else count)
        return pltpu.make_async_remote_copy(
            src_ref=xin.at[rows],
            dst_ref=cin.at[rows],
            send_sem=ct_send.at[i],
            recv_sem=ct_recv.at[i],
            device_id=(lax.rem(section + sections - 1, sections), dp),
            device_id_type=MESH,
        )

    def shorter(copy, size, i, action):
        @pl.when(i < chunks - 1)
        def _():
            action(copy(size, i, size))

        @pl.when(i == chunks - 1)
        def _():
            action(copy(size, i, size - SPARE))

    def packed_state(size, i, count):
        return state_copy(packed, size, i, count)

    def packed_receive(size, i):
        @pl.when(section == 2)
        def _():
            shorter(packed_state, size, i, lambda copy: copy.wait_recv())

        @pl.when(section > 2)
        def _():
            state_copy(xout, size, i).wait_recv()

    def cot_part(size, i, count):
        return cot_copy(size, i, count)

    def cot_wait(size, i):
        shorter(cot_part, size, i, lambda copy: copy.wait_recv())

    def cot_do(size, i, action):
        @pl.when(section == 2)
        def _():
            shorter(cot_part, size, i, action)

        @pl.when(section > 2)
        def _():
            action(cot_copy(size, i))

    @pl.when(natural)
    def _():
        if packing:
            lag = jnp.where(section == 0, ring - 1, ring - 3)
        else:
            lag = jnp.minimum(ring - 1, 3 * (last - section))

        @pl.when(section > 0)
        def _():
            prepare_columns()
            prepare_backward()
            if packing:
                xout[2 * ROWS : WINDOW, :] = jnp.zeros((WINDOW - 2 * ROWS, feats), f32)
                cin[total_packed - SPARE : total_packed, :] = jnp.zeros((SPARE, feats), f32)

        @pl.loop(0, chunks + lag)
        def _(t):
            @pl.when(t < chunks)
            def _():
                @pl.when(section == 0)
                def _():
                    input_copy(t).wait()

                @pl.when(section > 0)
                def _():
                    state_copy(xout, ROWS, t).wait_recv()

                rows = rows_at(t * ROWS, ROWS)
                saved = rows_at(lax.rem(t, ring) * ROWS, ROWS)
                forward(rows, saved, tgt.at[saved])

                @pl.when(plain_next)
                def _():
                    state_copy(xout, ROWS, t).start()

            if packing:

                j = jnp.where(t < 8, t - 1, t - 2)

                @pl.when(packs & (t >= 1) & (t != 8) & (j < chunks))
                def _():
                    start, _, hits = pack_matrix(j)
                    packed[rows_at(j * prows, prows), :] = split_dot(
                        dot, as_onehot(hits), xout[rows_at(start, WINDOW), :]
                    )
                    shorter(packed_state, prows, j, lambda copy: copy.start())

            @pl.when((section == 0) & (t == 3))
            def _():
                prepare_columns()
                prepare_backward()

            k = t - lag

            @pl.when((k >= 0) & (k < chunks))
            def _():
                @pl.when(k == 0)
                def _():
                    finish_weights()

                near_copy(k).wait()
                rows = rows_at(k * ROWS, ROWS)
                place = rows_at(lax.rem(k, NEAR) * ROWS, ROWS)
                saved = rows_at(lax.rem(k, ring) * ROWS, ROWS)

                @pl.when(plain_next)
                def _():
                    cot_copy(ROWS, k).wait_recv()
                    spread[...] = cin[rows, :]

                if packing:

                    @pl.when(packs)
                    def _():
                        had = jnp.where(k == 0, -1, chunks_for(jnp.maximum(k - 1, 0)))
                        for i in range(3):

                            @pl.when(had + 1 + i <= chunks_for(k))
                            def _():
                                cot_wait(prows, had + 1 + i)

                        spread[...] = unpack_rows(k)

                else:

                    @pl.when(section == last)
                    def _():
                        spread[...] = jnp.zeros_like(spread)

                weight = jnp.concatenate(
                    [
                        jnp.broadcast_to(
                            q_ref[pl.ds(k * (ROWS // LANES) + i, 1), :], (LANES, LANES)
                        ).T
                        for i in range(ROWS // LANES)
                    ],
                    axis=0,
                )
                diff = xout[rows, :] - near[place, :]
                spread[...] += loss_part(ROWS, diff, weight)

                @pl.when(k + NEAR < chunks)
                def _():
                    near_copy(k + NEAR).start()

                backward(ROWS, rows, saved, tgt.at[saved], spread[...])

                @pl.when(section > 0)
                def _():
                    cot_copy(ROWS, k).start()

        @pl.loop(0, chunks)
        def _(i):
            @pl.when(plain_next)
            def _():
                state_copy(xout, ROWS, i).wait_send()

            if packing:

                @pl.when(packs)
                def _():
                    shorter(packed_state, prows, i, lambda copy: copy.wait_send())

            @pl.when(section > 0)
            def _():
                cot_copy(ROWS, i).wait_send()

    if packing:

        @pl.when(jnp.logical_not(natural))
        def _():
            lag = jnp.minimum(2 * (last - section), min(ring_packed, qring.shape[0]) - 1)
            prepare_columns()
            prepare_backward()

            @pl.when(section == 2)
            def _():
                xin[total_packed - SPARE : total_packed, :] = jnp.zeros((SPARE, feats), f32)


            @pl.loop(0, chunks + lag)
            def _(t):
                @pl.when(t < chunks)
                def _():
                    @pl.when(t == 0)
                    def _():
                        target_copy(0).wait()
                        target_copy(1).wait()

                    @pl.when(t + 2 < chunks)
                    def _():
                        target_copy(t + 2).wait()

                    start, first, hits = pack_matrix(t)
                    rows = rows_at(t * prows, prows)
                    packed[rows, :] = split_dot(
                        dot, as_onehot(hits), tgt[rows_at(start, WINDOW), :]
                    )
                    weight = jnp.zeros((prows, LANES), f32)
                    for i, hit in enumerate(hits):
                        weight += jnp.where(hit, q_ref[pl.ds(first + i, 1), :], 0.0)
                    qring[lax.rem(t, sections)] = jnp.broadcast_to(
                        jnp.sum(weight, -1, keepdims=True), (prows, LANES)
                    )
                    packed_receive(prows, t)
                    saved = rows_at(lax.rem(t, ring) * ROWS, prows)
                    kept = rows_at(lax.rem(t, ring_packed) * prows, prows)
                    forward(rows, saved, near.at[kept])

                    @pl.when(section < last)
                    def _():
                        state_copy(xout, prows, t).start()

                k = t - lag

                @pl.when(k >= 0)
                def _():
                    @pl.when(k == 0)
                    def _():
                        finish_weights()

                    rows = rows_at(k * prows, prows)
                    saved = rows_at(lax.rem(k, ring) * ROWS, prows)
                    diff = xout[rows, :] - packed[rows, :]
                    spread[0:prows, :] = loss_part(prows, diff, qring[lax.rem(k, sections)])

                    @pl.when(section < last)
                    def _():
                        cot_copy(prows, k).wait_recv()
                        spread[0:prows, :] += cin[rows, :]

                    kept = rows_at(lax.rem(k, ring_packed) * prows, prows)
                    backward(prows, rows, saved, near.at[kept], spread[0:prows, :])
                    cot_do(prows, k, lambda copy: copy.start())

            @pl.loop(0, chunks)
            def _(i):
                cot_do(prows, i, lambda copy: copy.wait_send())

                @pl.when(section < last)
                def _():
                    state_copy(xout, prows, i).wait_send()

    depth = min(4, groups)
    width = groups // depth
    y, z = lax.rem(dp, width), dp // width
    ypart, zpart = PIECE // width, PIECE // groups
    halves = feats // PIECE
    pieces = range(4 * halves)
    matrix = [m for m in (3, 1, 2, 0) for _ in range(halves)]
    first = [PIECE * (p % halves) for p in pieces]
    ysum = near

    def y_copy(p, step):
        to = lax.rem(y + step, width)
        i = p * width + step
        return pltpu.make_async_remote_copy(
            src_ref=acc.at[matrix[p], rows_at(first[p] + to * ypart, ypart)],
            dst_ref=ybuf.at[p * (width - 1) + step - 1],
            send_sem=y_send.at[i],
            recv_sem=y_recv.at[i],
            device_id=(section, z * width + to),
            device_id_type=MESH,
        )

    def z_copy(p, step):
        to = lax.rem(z + step, depth)
        i = p * depth + step
        return pltpu.make_async_remote_copy(
            src_ref=ysum.at[rows_at(p * ypart + to * zpart, zpart)],
            dst_ref=zbuf.at[p * (depth - 1) + step - 1],
            send_sem=z_send.at[i],
            recv_sem=z_recv.at[i],
            device_id=(section, to * width + y),
            device_id_type=MESH,
        )

    def z_back(p, step):
        to = lax.rem(z + step, depth)
        i = p * depth + step
        rows = rows_at(first[p] + y * ypart + z * zpart, zpart)
        return pltpu.make_async_remote_copy(
            src_ref=final.at[matrix[p], rows],
            dst_ref=final.at[matrix[p], rows],
            send_sem=za_send.at[i],
            recv_sem=za_recv.at[i],
            device_id=(section, to * width + y),
            device_id_type=MESH,
        )

    def y_back(p, step):
        to = lax.rem(y + step, width)
        i = p * width + step
        rows = rows_at(first[p] + y * ypart, ypart)
        return pltpu.make_async_remote_copy(
            src_ref=final.at[matrix[p], rows],
            dst_ref=final.at[matrix[p], rows],
            send_sem=ya_send.at[i],
            recv_sem=ya_recv.at[i],
            device_id=(section, z * width + to),
            device_id_type=MESH,
        )

    def small_copy(step):
        return pltpu.make_async_remote_copy(
            src_ref=small.at[dp],
            dst_ref=small.at[dp],
            send_sem=small_send.at[step],
            recv_sem=small_recv.at[step],
            device_id=peer(step),
            device_id_type=MESH,
        )

    def tiny_copy(step):
        return pltpu.make_async_remote_copy(
            src_ref=tiny.at[section],
            dst_ref=tiny.at[section],
            send_sem=tiny_send.at[step],
            recv_sem=tiny_recv.at[step],
            device_id=(lax.rem(section + step, sections), dp),
            device_id_type=MESH,
        )

    def out_copy(p):
        rows = pl.ds(first[p], PIECE)
        return pltpu.make_async_copy(
            final.at[matrix[p], rows], grads_ref.at[matrix[p], rows], out_sem.at[p]
        )

    for p in pieces:
        for step in range(1, width):
            y_copy(p, step).start()
    for p in pieces:
        own = acc[matrix[p], rows_at(first[p] + y * ypart, ypart), :]
        for step in range(1, width):
            y_copy(p, step).wait_recv()
            own = own + ybuf[p * (width - 1) + step - 1]
        ysum[p * ypart : (p + 1) * ypart, :] = own
        for step in range(1, depth):
            z_copy(p, step).start()
    squares = jnp.zeros((1, 1), f32)
    for p in pieces:
        own = ysum[rows_at(p * ypart + z * zpart, zpart), :]
        for step in range(1, depth):
            z_copy(p, step).wait_recv()
            own = own + zbuf[p * (depth - 1) + step - 1]
        final[matrix[p], rows_at(first[p] + y * ypart + z * zpart, zpart), :] = own
        squares = squares + jnp.sum(own * own, axis=(0, 1), keepdims=True)
        for step in range(1, depth):
            z_back(p, step).start()
    loss = jnp.sum(loss_acc[...], axis=(0, 1), keepdims=True)
    wide_row = lax.broadcasted_iota(jnp.int32, (8, feats), 0)
    small[dp] = jnp.where(
        wide_row == 0,
        jnp.sum(gain_acc[0], 0, keepdims=True),
        jnp.where(
            wide_row == 1,
            jnp.sum(gain_acc[1], 0, keepdims=True),
            jnp.where(wide_row < 4, loss, squares),
        ),
    )
    for step in range(1, groups):
        small_copy(step).start()
    for p in pieces:
        for step in range(1, depth):
            z_back(p, step).wait_recv()
        for step in range(1, width):
            y_back(p, step).start()
    for step in range(1, groups):
        small_copy(step).wait_recv()
    total = small[0]
    for other in range(1, groups):
        total = total + small[other]
    gain_squares = jnp.sum(total[0:2] * total[0:2], axis=(0, 1), keepdims=True)
    tiny[section] = jnp.where(tile_row < 4, total[2:3, 0:1], total[4:5, 0:1] + gain_squares)
    for step in range(1, sections):
        tiny_copy(step).start()
    for p in pieces:
        for step in range(1, width):
            y_back(p, step).wait_recv()
        out_copy(p).start()
    for step in range(1, sections):
        tiny_copy(step).wait_recv()
    whole = tiny[0]
    for other in range(1, sections):
        whole = whole + tiny[other]
    norm = jnp.sqrt(whole[4:5, 0:1])
    clip = jnp.minimum(1.0, clip_limit / norm)
    stats = total
    for row, number in ((2, clip), (3, whole[0:1, 0:1]), (4, weight_ref[0:1, 0:1]), (5, norm)):
        stats = jnp.where(wide_row == row, number, stats)
    stat_ref[...] = stats

    for step in range(1, groups):
        weight_copy(step).wait_send()
        small_copy(step).wait_send()
    for step in range(1, sections):
        tiny_copy(step).wait_send()
    for p in pieces:
        out_copy(p).wait()
        for step in range(1, width):
            y_copy(p, step).wait_send()
            y_back(p, step).wait_send()
        for step in range(1, depth):
            z_copy(p, step).wait_send()
            z_back(p, step).wait_send()


def rollout(packing, sections, groups, inputs, target, lengths, lat_index, land, w_up, w_down, gains):
    columns, feats = inputs.shape
    chunks = columns // ROWS
    prows = ROWS * (sections - 2) // sections + 16
    grid_rows = columns // LANES
    packed_bytes = 4 * chunks * prows * feats
    ring = min((SAVE_BYTES - packed_bytes) // (8 * ROWS * feats), chunks)
    depth = min(4, groups)
    width = groups // depth
    pieces = 4 * feats // PIECE
    hbm = pl.BlockSpec(memory_space=pl.ANY)
    vmem = pl.BlockSpec(memory_space=pltpu.VMEM)
    dma = pltpu.SemaphoreType.DMA
    wide = pltpu.VMEM((columns, feats), f32)
    lows = pltpu.VMEM((2, feats, feats), bf16)
    grads = pltpu.VMEM((4, feats, feats), f32)
    square = pltpu.VMEM((2, feats, feats), f32)
    flat = lambda array: array.reshape(grid_rows, LANES)
    return pl.pallas_call(
        functools.partial(rollout_kernel, sections, groups, packing),
        out_shape=(
            jax.ShapeDtypeStruct((4, feats, feats), f32),
            jax.ShapeDtypeStruct((8, feats), f32),
            jax.ShapeDtypeStruct((1, 1), jnp.int32),
        ),
        in_specs=[hbm] * 8,
        out_specs=(hbm, vmem, vmem),
        scratch_shapes=[
            wide,
            wide,
            wide,
            wide,
            pltpu.VMEM((chunks * prows if packing else 8, feats), f32),
            pltpu.VMEM((NEAR * ROWS, feats), f32),
            pltpu.VMEM((2, ring * ROWS, feats), bf16),
            pltpu.VMEM((2, ring * ROWS, feats), bf16),
            pltpu.VMEM((sections, prows, LANES), f32),
            lows,
            lows,
            lows,
            lows,
            pltpu.VMEM((grid_rows, LANES), f32),
            pltpu.VMEM((grid_rows, LANES), f32),
            pltpu.VMEM((8, LANES), f32),
            pltpu.VMEM((8, LANES), f32),
            pltpu.VMEM((8, feats), f32),
            pltpu.VMEM((2, 8, feats), f32),
            pltpu.VMEM((groups, 8, LANES), f32),
            pltpu.VMEM((ROWS, feats), f32),
            pltpu.VMEM((grid_rows, LANES), jnp.int32),
            pltpu.VMEM((grid_rows, LANES), jnp.int32),
            pltpu.VMEM((grid_rows, LANES), jnp.int32),
            pltpu.VMEM((2, feats), f32),
            square,
            square,
            grads,
            grads,
            pltpu.VMEM((max(pieces * (width - 1), 1), PIECE // width, feats), f32),
            pltpu.VMEM((pieces * (depth - 1), PIECE // groups, feats), f32),
            pltpu.VMEM((groups, 8, feats), f32),
            pltpu.VMEM((sections, 8, LANES), f32),
            dma((chunks,)),
            dma((chunks,)),
            dma((chunks,)),
            dma((chunks,)),
            dma((chunks,)),
            dma((chunks,)),
            dma((groups,)),
            dma((groups,)),
            dma((pieces * width,)),
            dma((pieces * width,)),
            dma((pieces * depth,)),
            dma((pieces * depth,)),
            dma((pieces * depth,)),
            dma((pieces * depth,)),
            dma((pieces * width,)),
            dma((pieces * width,)),
            dma((groups,)),
            dma((groups,)),
            dma((sections,)),
            dma((sections,)),
            dma((pieces,)),
            dma((6,)),
        ],
        compiler_params=pltpu.CompilerParams(
            collective_id=0 if packing else 1,
            has_side_effects=True,
            vmem_limit_bytes=63 * 1024 * 1024,
        ),
        name="rollout_packed" if packing else "rollout_all",
    )(
        inputs,
        target,
        flat(lengths),
        flat(lat_index),
        flat(land),
        w_up,
        w_down,
        gains,
    )


def adam_step(weights_old, gradient, moment_one, moment_two, decay_rate):
    moment_one = beta_one * moment_one + (1.0 - beta_one) * gradient
    moment_two = beta_two * moment_two + (1.0 - beta_two) * gradient * gradient
    second_hat = moment_two * (1.0 / (1.0 - beta_two**STEP))
    root = second_hat * lax.rsqrt(second_hat)
    pace = moment_one * (learn_rate / (1.0 - beta_one**STEP))
    step = pace * pl.reciprocal(root + adam_eps)
    new_weights = weights_old * (1.0 - learn_rate * decay_rate) - step
    return (new_weights, moment_one, moment_two)


def update_kernel(
    grads_ref,
    stat_hbm,
    w_up,
    w_down,
    gains,
    m_up,
    m_down,
    m_gains,
    v_up,
    v_down,
    v_gains,
    loss_out,
    total_out,
    norm_out,
    new_up,
    new_down,
    new_gains,
    new_m_up,
    new_m_down,
    new_m_gains,
    new_v_up,
    new_v_down,
    new_v_gains,
    held,
    stat_ref,
    gain_ref,
    in_sem,
    out_sem,
    small_in,
    small_out,
):
    old = ((grads_ref, grads_ref), (w_up, w_down), (m_up, m_down), (v_up, v_down))
    new = ((new_up, new_down), (new_m_up, new_m_down), (new_v_up, new_v_down))

    def fetch(i, part):
        source = old[part][i // 2].at[i if part == 0 else i % 2]
        return pltpu.make_async_copy(source, held.at[part, i], in_sem.at[part, i])

    def store(i, part):
        return pltpu.make_async_copy(
            held.at[part + 1, i], new[part][i // 2].at[i % 2], out_sem.at[part, i]
        )

    small_fetch = [pltpu.make_async_copy(stat_hbm, stat_ref, small_in.at[3])]
    small_store = []
    for part, (source, out) in enumerate(
        ((gains, new_gains), (m_gains, new_m_gains), (v_gains, new_v_gains))
    ):
        small_fetch.append(pltpu.make_async_copy(source, gain_ref.at[part], small_in.at[part]))
        small_store.append(pltpu.make_async_copy(gain_ref.at[part], out, small_out.at[part]))
    for copy in small_fetch:
        copy.start()
    for i in range(4):
        for part in range(4):
            fetch(i, part).start()
    for copy in small_fetch:
        copy.wait()
    clip = stat_ref[2:3, 0:1]
    for row, out in ((3, loss_out), (4, total_out), (5, norm_out)):
        out[...] = stat_ref[row : row + 1, 0:1]
    fresh = adam_step(gain_ref[0], stat_ref[0:2] * clip, gain_ref[1], gain_ref[2], 0.0)
    for part in range(3):
        gain_ref[part] = fresh[part]
        small_store[part].start()
    for i in range(4):
        for part in range(4):
            fetch(i, part).wait()
        fresh = adam_step(held[1, i], held[0, i] * clip, held[2, i], held[3, i], weight_decay)
        for part in range(3):
            held[part + 1, i] = fresh[part]
            store(i, part).start()
    for i in range(4):
        for part in range(3):
            store(i, part).wait()
    for copy in small_store:
        copy.wait()


def update(grads, stats, *state):
    hbm = pl.BlockSpec(memory_space=pl.ANY)
    vmem = pl.BlockSpec(memory_space=pltpu.VMEM)
    return pl.pallas_call(
        update_kernel,
        in_specs=[hbm] * 11,
        out_specs=(vmem,) * 3 + (hbm,) * 9,
        out_shape=(jax.ShapeDtypeStruct((1, 1), f32),) * 3
        + tuple(jax.ShapeDtypeStruct(a.shape, f32) for a in state),
        scratch_shapes=[
            pltpu.VMEM((4,) + grads.shape, f32),
            pltpu.VMEM(stats.shape, f32),
            pltpu.VMEM((3,) + state[2].shape, f32),
            pltpu.SemaphoreType.DMA((4, 4)),
            pltpu.SemaphoreType.DMA((3, 4)),
            pltpu.SemaphoreType.DMA((4,)),
            pltpu.SemaphoreType.DMA((3,)),
        ],
        compiler_params=pltpu.CompilerParams(vmem_limit_bytes=63 * 1024 * 1024),
        name="update",
    )(grads, stats, *state)


def per_device(
    inputs,
    targets,
    lengths,
    lat_index,
    land,
    w_up,
    w_down,
    gains,
    m_up,
    m_down,
    m_gains,
    v_up,
    v_down,
    v_gains,
):
    sections, groups = lax.axis_size("section"), lax.axis_size("dp")
    state = tuple(
        a[0] for a in (w_up, w_down, gains, m_up, m_down, m_gains, v_up, v_down, v_gains)
    )
    operands = (inputs, targets[0], lengths, lat_index, land) + state[:3]
    packed = rollout(True, sections, groups, *operands)

    grads, stats, unused = lax.cond(
        packed[2].reshape(()) > 0,
        lambda: rollout(False, sections, groups, *operands),
        lambda: packed,
    )
    new = update(grads, stats, *state)
    return tuple(a.reshape(()) for a in new[:3]) + tuple(a[None] for a in new[3:])


def solution(mesh):
    return jax.shard_map(
        per_device,
        mesh=mesh,
        in_specs=(
            P("dp", None),
            P("section", "dp", None),
            P("dp"),
            P("dp"),
            P("dp"),
            P("section", None, None, None),
            P("section", None, None, None),
            P("section", None, None),
            P("section", None, None, None),
            P("section", None, None, None),
            P("section", None, None),
            P("section", None, None, None),
            P("section", None, None, None),
            P("section", None, None),
        ),
        out_specs=(
            P(),
            P(),
            P(),
            P("section", None, None, None),
            P("section", None, None, None),
            P("section", None, None),
            P("section", None, None, None),
            P("section", None, None, None),
            P("section", None, None),
            P("section", None, None, None),
            P("section", None, None, None),
            P("section", None, None),
        ),
        check_vma=False,
    )
```

```python
import functools
import math

import jax
import jax.numpy as jnp
from jax import lax
from jax.experimental import pallas as pl
from jax.experimental.pallas import tpu as pltpu
from jax.sharding import PartitionSpec as P

NLAT = 128
STEP = 10

norm_eps = 1e-06
clip_limit = 0.05
beta_one = 0.9
beta_two = 0.999
adam_eps = 1e-08
learn_rate = 0.1
weight_decay = 0.01

f32, bf16 = jnp.float32, jnp.bfloat16
MESH = pl.DeviceIdType.MESH
LANES = 128
PIECE = 128
ROWS = 512
SPARE = 80
WINDOW = 1536
SAVE_BYTES = 18 * 1024 * 1024
NEAR = 4


def dot(a, b):
    return jnp.dot(a, b, preferred_element_type=f32)


def dot_lhs_t(a, b):
    return lax.dot_general(a, b, (((0,), (0,)), ((), ())), preferred_element_type=f32)


def split_dot(product, onehot, values):
    high = values.astype(bf16)
    low = (values - high.astype(f32)).astype(bf16)
    return product(onehot, high) + product(onehot, low)


def rollout_kernel(
    sections,
    groups,
    packing,
    inputs_ref,
    target_ref,
    len_hbm,
    lat_hbm,
    land_hbm,
    up_hbm,
    down_hbm,
    gain_hbm,
    grads_ref,
    stat_ref,
    miss_ref,
    xin,
    xout,
    cin,
    tgt,
    packed,
    near,
    save_h,
    save_d,
    qring,
    up_lo,
    up_t,
    down_lo,
    down_t,
    rank_ref,
    q_ref,
    scale_ref,
    weight_ref,
    loss_acc,
    gain_acc,
    wbuf,
    spread,
    len_ref,
    lat_ref,
    land_ref,
    gain_ref,
    acc,
    gain_land,
    land,
    small,
    tiny,
    in_sem,
    tgt_sem,
    st_send,
    st_recv,
    ct_send,
    ct_recv,
    w_send,
    w_recv,
    rs_send,
    rs_recv,
    ag_send,
    ag_recv,
    small_send,
    small_recv,
    tiny_send,
    tiny_recv,
    out_sem,
    weight_sem,
    mate_send,
    mate_recv,
    pair_send,
    pair_recv,
):
    section = lax.axis_index("section")
    dp = lax.axis_index("dp")
    columns = xin.shape[0]
    feats = xin.shape[1]
    chunks = columns // ROWS
    live_rows = ROWS * (sections - 2) // sections
    prows = live_rows + 16
    total_packed = chunks * prows
    expand = live_rows + 512
    last = sections - 1
    core = lax.rem(section, 2)
    mate = section + 1 - 2 * core
    final = acc.at[pl.ds(4, 4)]
    up_ref, down_ref = acc.at[pl.ds(0, 2)], acc.at[pl.ds(2, 2)]
    ring = save_h.shape[1] // ROWS
    natural = section < (2 if packing else sections)
    plain_next = (section == 0) if packing else (section < last)
    packs = (section == 1) if packing else (section < 0)

    def peer(step):
        return (section, lax.rem(dp + step, groups))

    sources = (up_hbm, down_hbm, gain_hbm, len_hbm, lat_hbm, land_hbm)
    places = (up_ref, down_ref, gain_ref.at[0], len_ref, lat_ref, land_ref)
    fetches = [
        pltpu.make_async_copy(source, place, weight_sem.at[i])
        for i, (source, place) in enumerate(zip(sources, places))
    ]
    for fetch in fetches:
        fetch.start()

    barrier = pltpu.get_barrier_semaphore()
    for step in range(1, sections):
        other = lax.rem(section + step, sections)
        pl.semaphore_signal(barrier, inc=1, device_id=(other, dp), device_id_type=MESH)
    for step in range(1, groups):
        pl.semaphore_signal(barrier, inc=1, device_id=peer(step), device_id_type=MESH)

    def rows_at(index, size, align=16):
        return pl.ds(pl.multiple_of(index, align), size)

    def input_copy(i):
        rows = rows_at(i * ROWS, ROWS)
        return pltpu.make_async_copy(inputs_ref.at[rows], xin.at[rows], in_sem.at[i])

    def target_copy(i):
        rows = rows_at(i * ROWS, ROWS)
        return pltpu.make_async_copy(target_ref.at[rows], tgt.at[rows], tgt_sem.at[i])

    def near_copy(i):
        place = rows_at(lax.rem(i, NEAR) * ROWS, ROWS)
        return pltpu.make_async_copy(
            target_ref.at[rows_at(i * ROWS, ROWS)], near.at[place], tgt_sem.at[i]
        )

    @pl.when(section == 0)
    def _():
        @pl.loop(0, NEAR)
        def _(i):
            input_copy(i).start()

    @pl.when(natural)
    def _():
        @pl.loop(0, NEAR)
        def _(i):
            near_copy(i).start()

    @pl.when(jnp.logical_not(natural))
    def _():
        @pl.loop(0, chunks)
        def _(i):
            target_copy(i).start()

    def prepare_backward():
        for layer in range(2):
            up_t[layer] = up_ref[layer].T.astype(bf16)
            down_t[layer] = (0.5 * down_ref[layer]).T.astype(bf16)
        gain_acc[...] = jnp.zeros_like(gain_acc)
        loss_acc[...] = jnp.zeros_like(loss_acc)
        for i in range(4):
            acc[i] = jnp.zeros((feats, feats), f32)

    def mate_weight(i):
        source = gain_ref.at[0] if i == 4 else acc.at[i]
        place = gain_ref.at[1] if i == 4 else acc.at[4 + i]
        return pltpu.make_async_remote_copy(
            src_ref=source,
            dst_ref=place,
            send_sem=mate_send.at[i],
            recv_sem=mate_recv.at[i],
            device_id=(mate, dp),
            device_id_type=MESH,
        )

    def prepare_mate():
        for i in range(5):
            mate_weight(i).wait_recv()
        for layer in range(2):
            up = acc[4 + layer]
            down = acc[6 + layer]
            up_lo[2 + layer] = (0.5 * up).astype(bf16)
            down_lo[2 + layer] = down.astype(bf16)
            up_t[2 + layer] = up.T.astype(bf16)
            down_t[2 + layer] = (0.5 * down).T.astype(bf16)
        for i in range(4, 8):
            acc[i] = jnp.zeros((feats, feats), f32)

    def mate_gradient(i):
        if i < 4:
            source = acc.at[4 + i]
            place = xin.at[pl.ds(columns - (4 - i) * feats, feats)]
        else:
            source, place = gain_acc.at[pl.ds(2, 2)], gain_land
        return pltpu.make_async_remote_copy(
            src_ref=source,
            dst_ref=place,
            send_sem=mate_send.at[5 + i],
            recv_sem=mate_recv.at[5 + i],
            device_id=(mate, dp),
            device_id_type=MESH,
        )

    def pair_copy(j):
        return pltpu.make_async_remote_copy(
            src_ref=packed.at[rows_at(j * prows, prows)],
            dst_ref=cin.at[rows_at(swapped(j) * prows, prows)],
            send_sem=pair_send.at[j],
            recv_sem=pair_recv.at[j],
            device_id=(mate, dp),
            device_id_type=MESH,
        )

    def swapped(j):
        return j + 1 - 2 * lax.rem(j, 2)

    grid_rows = columns // LANES
    tile_row = lax.broadcasted_iota(jnp.int32, (8, LANES), 0)

    def window_start(j):
        shift = jnp.where(j < 7, 0, jnp.where(j < 11, 256, 384))
        return jnp.clip(ROWS * (j - 1) + shift, 0, columns - WINDOW)

    def expand_start(k):
        return jnp.clip(live_rows * k - 272, 0, total_packed - expand)

    def chunks_for(k):
        return (expand_start(k) + expand - 1) // prows

    def weight_copy(step):
        return pltpu.make_async_remote_copy(
            src_ref=wbuf.at[dp],
            dst_ref=wbuf.at[dp],
            send_sem=w_send.at[step],
            recv_sem=w_recv.at[step],
            device_id=peer(step),
            device_id_type=MESH,
        )

    def prepare_columns():
        length = len_ref[...]
        latitude = (lat_ref[...].astype(f32) + 0.5) * (math.pi / NLAT) - math.pi / 2
        area = jnp.cos(latitude) * (1.0 + land_ref[...].astype(f32))
        q_ref[0] = area * (section < length).astype(f32)
        q_ref[1] = area * (mate < length).astype(f32)
        local_weight = jnp.sum(
            area * jnp.minimum(length, sections).astype(f32), axis=(0, 1), keepdims=True
        )
        misses = jnp.zeros((1, 1), f32)
        if packing:
            beyond = length > 2
            flag = beyond.astype(bf16)
            lane_a = lax.broadcasted_iota(jnp.int32, (LANES, LANES), 0)
            lane_b = lax.broadcasted_iota(jnp.int32, (LANES, LANES), 1)
            within = dot(flag, (lane_a < lane_b).astype(bf16))
            row_total = jnp.sum(flag.astype(f32), axis=1, keepdims=True)
            row_a = lax.broadcasted_iota(jnp.int32, (grid_rows, grid_rows), 0)
            row_b = lax.broadcasted_iota(jnp.int32, (grid_rows, grid_rows), 1)
            before = dot(
                (row_b < row_a).astype(bf16),
                jnp.broadcast_to(row_total, (grid_rows, LANES)).astype(bf16),
            )
            rank = jnp.where(beyond, within + before, -1e6)
            rank_ref[...] = rank
            place = (
                lax.broadcasted_iota(jnp.int32, (grid_rows, LANES), 0) * LANES
                + lax.broadcasted_iota(jnp.int32, (grid_rows, LANES), 1)
            )
            rank_i = rank.astype(jnp.int32)
            missed = beyond & (rank_i >= total_packed - SPARE)
            for j in range(chunks):
                shift = 0 if j < 7 else 256 if j < 11 else 384
                start = min(max(ROWS * (j - 1) + shift, 0), columns - WINDOW)
                member = (rank_i >= j * prows) & (rank_i < (j + 1) * prows)
                ready = ROWS * (j + 2 if j < 7 else j + 3)
                missed |= member & ((place < start) | (place >= min(start + WINDOW, ready)))
            row_chunk = lax.broadcasted_iota(jnp.int32, (grid_rows, LANES), 0) // (ROWS // LANES)
            row_start = jnp.clip(live_rows * row_chunk - 272, 0, total_packed - expand)
            missed |= beyond & ((rank_i < row_start) | (rank_i >= row_start + expand))
            misses = jnp.sum(missed.astype(f32), axis=(0, 1), keepdims=True)
        wbuf[dp] = jnp.where(tile_row < 4, local_weight, misses)
        for step in range(1, groups):
            weight_copy(step).start()

    def finish_weights():
        for step in range(1, groups):
            weight_copy(step).wait_recv()
        total = wbuf[0]
        for other in range(1, groups):
            total = total + wbuf[other]
        weight_ref[...] = total
        miss_ref[...] = (total[4:5, 0:1] > 0.0).astype(jnp.int32)
        scale_ref[...] = 2.0 / jnp.broadcast_to(total[0:1], (8, LANES))

    for fetch in fetches:
        fetch.wait()
    for layer in range(2):
        up_lo[layer] = (0.5 * up_ref[layer]).astype(bf16)
        down_lo[layer] = down_ref[layer].astype(bf16)
    pl.semaphore_wait(barrier, sections - 1 + groups - 1)

    def pack_matrix(j):
        start = window_start(j)
        base = (j * prows).astype(f32)
        target_row = lax.broadcasted_iota(jnp.int32, (prows, LANES), 0).astype(f32)
        first = start // LANES
        hits = []
        for i in range(WINDOW // LANES):
            hits.append(target_row == rank_ref[pl.ds(first + i, 1), :] - base)
        return start, first, hits

    def as_onehot(hits):
        return jnp.concatenate([jnp.where(hit, 1.0, 0.0).astype(bf16) for hit in hits], axis=1)

    def unpack_rows(k):
        start = expand_start(k)
        base = start.astype(f32)
        source_row = lax.broadcasted_iota(jnp.int32, (expand, LANES), 0).astype(f32)
        hits = []
        for i in range(ROWS // LANES):
            hits.append(source_row == rank_ref[pl.ds(k * (ROWS // LANES) + i, 1), :] - base)
        return dot_lhs_t(as_onehot(hits), cin[rows_at(start, expand), :].astype(bf16))

    def forward(source, place, owner, saved, keep):
        x = source[...]
        for layer in range(2):
            if layer == 1:
                keep[...] = x
            r = lax.rsqrt(jnp.mean(x * x, -1, keepdims=True) + norm_eps)
            normed = (x * r * gain_ref[owner, layer : layer + 1]).astype(bf16)
            half = dot(normed, up_lo[2 * owner + layer])
            t = jnp.tanh(half)
            a = 1.0 + t
            h = half * a
            hidden = h.astype(bf16)
            save_h[layer, saved, :] = hidden
            save_d[layer, saved, :] = (a + h * (1.0 - t)).astype(bf16)
            x = x + dot(hidden, down_lo[2 * owner + layer])
        place[...] = x

    def loss_part(size, diff, weight):
        weighted = jnp.concatenate(
            [diff[:, :LANES] * weight, diff[:, LANES:] * weight], axis=1
        )
        loss_acc[...] += jnp.sum((weighted * diff).reshape(size // 8, 8, feats), 0)
        return weighted * scale_ref[0:1, 0:1]

    def backward(size, source, place, owner, saved, keep, g):
        for layer in (1, 0):
            low = g.astype(bf16)
            acc[4 * owner + 2 + layer] += dot_lhs_t(save_h[layer, saved, :], low)
            pull = dot(low, down_t[2 * owner + layer])
            g_pre = (pull * save_d[layer, saved, :].astype(f32)).astype(bf16)
            x = keep[...] if layer == 1 else source[...]
            r = lax.rsqrt(jnp.mean(x * x, -1, keepdims=True) + norm_eps)
            gain = gain_ref[owner, layer : layer + 1]
            xr = x * r
            normed = (xr * gain).astype(bf16)
            acc[4 * owner + layer] += dot_lhs_t(normed, g_pre)
            g_normed = dot(g_pre, up_t[2 * owner + layer])
            prod = g_normed * xr
            gain_acc[2 * owner + layer] += jnp.sum(prod.reshape(size // 8, 8, feats), 0)
            mean = jnp.mean(prod * gain, -1, keepdims=True)
            g = g + r * (gain * g_normed - xr * mean)
        place[...] = g

    def state_copy(source, size, i, to, count=None):
        rows = rows_at(i * size, size if count is None else count)
        return pltpu.make_async_remote_copy(
            src_ref=source.at[rows],
            dst_ref=xin.at[rows],
            send_sem=st_send.at[i],
            recv_sem=st_recv.at[i],
            device_id=(to, dp),
            device_id_type=MESH,
        )

    def cot_copy(size, i, to, count=None):
        rows = rows_at(i * size, size if count is None else count)
        return pltpu.make_async_remote_copy(
            src_ref=xin.at[rows],
            dst_ref=cin.at[rows],
            send_sem=ct_send.at[i],
            recv_sem=ct_recv.at[i],
            device_id=(to, dp),
            device_id_type=MESH,
        )

    up_one = lax.rem(section + 1, sections)
    down_one = lax.rem(section + sections - 1, sections)
    up_chip = lax.rem(section + 2, sections)
    down_chip = jnp.where(section < 4, 1, section - 2)

    def shorter(copy, size, i, action):
        @pl.when(i < chunks - 1)
        def _():
            action(copy(size, i, size))

        @pl.when(i == chunks - 1)
        def _():
            action(copy(size, i, size - SPARE))

    def packed_state(size, i, count):
        return state_copy(packed, size, i, 2 + lax.rem(i, 2), count)

    def packed_receive(size, i):
        @pl.when(section < 4)
        def _():
            shorter(packed_state, size, i, lambda copy: copy.wait_recv())

        @pl.when(section >= 4)
        def _():
            state_copy(xout, size, i, up_chip).wait_recv()

    def cot_part(size, i, count):
        return cot_copy(size, i, down_chip, count)

    def cot_wait(size, i):
        shorter(cot_part, size, i, lambda copy: copy.wait_recv())

    def cot_do(size, i, action):
        @pl.when(section < 4)
        def _():
            shorter(cot_part, size, i, action)

        @pl.when(section >= 4)
        def _():
            action(cot_copy(size, i, down_chip))

    @pl.when(natural)
    def _():
        if packing:
            most = chunks if ring == chunks else ring - 1
            lag = jnp.where(section == 0, most, most - 2)
        else:
            lag = jnp.minimum(ring - 1, 3 * (last - section))

        @pl.when(section > 0)
        def _():
            prepare_columns()
            if packing:
                xout[2 * ROWS : WINDOW, :] = jnp.zeros((WINDOW - 2 * ROWS, feats), f32)
                cin[total_packed - SPARE : total_packed, :] = jnp.zeros((SPARE, feats), f32)

        @pl.loop(0, chunks + lag)
        def _(t):
            @pl.when(t < chunks)
            def _():
                @pl.when(section == 0)
                def _():
                    input_copy(t).wait()

                    @pl.when(t + NEAR < chunks)
                    def _():
                        input_copy(t + NEAR).start()

                @pl.when(section > 0)
                def _():
                    state_copy(xout, ROWS, t, up_one).wait_recv()

                rows = rows_at(t * ROWS, ROWS)
                saved = rows_at(lax.rem(t, ring) * ROWS, ROWS)
                forward(xin.at[rows], xout.at[rows], 0, saved, tgt.at[saved])

                @pl.when(plain_next)
                def _():
                    state_copy(xout, ROWS, t, up_one).start()

            if packing:

                j = jnp.where(t < 8, t - 1, t - 2)

                @pl.when(packs & (t >= 1) & (t != 8) & (j < chunks))
                def _():
                    start, _, hits = pack_matrix(j)
                    packed[rows_at(j * prows, prows), :] = split_dot(
                        dot, as_onehot(hits), xout[rows_at(start, WINDOW), :]
                    )
                    shorter(packed_state, prows, j, lambda copy: copy.start())

            @pl.when((section == 0) & (t == 3))
            def _():
                prepare_columns()

            @pl.when(t == jnp.minimum(lag, 4))
            def _():
                prepare_backward()

            k = t - lag

            @pl.when((k >= 0) & (k < chunks))
            def _():
                @pl.when(k == 0)
                def _():
                    finish_weights()

                near_copy(k).wait()
                rows = rows_at(k * ROWS, ROWS)
                place = rows_at(lax.rem(k, NEAR) * ROWS, ROWS)
                saved = rows_at(lax.rem(k, ring) * ROWS, ROWS)

                weight = jnp.concatenate(
                    [
                        jnp.broadcast_to(
                            q_ref[0, pl.ds(k * (ROWS // LANES) + i, 1), :], (LANES, LANES)
                        ).T
                        for i in range(ROWS // LANES)
                    ],
                    axis=0,
                )
                diff = xout[rows, :] - near[place, :]
                spread[...] = loss_part(ROWS, diff, weight)

                @pl.when(k + NEAR < chunks)
                def _():
                    near_copy(k + NEAR).start()

                @pl.when(plain_next)
                def _():
                    cot_copy(ROWS, k, down_one).wait_recv()
                    spread[...] += cin[rows, :]

                if packing:

                    @pl.when(packs)
                    def _():
                        had = jnp.where(k == 0, -1, chunks_for(jnp.maximum(k - 1, 0)))
                        for i in range(3):

                            @pl.when(had + 1 + i <= chunks_for(k))
                            def _():
                                cot_wait(prows, had + 1 + i)

                        spread[...] += unpack_rows(k)

                backward(ROWS, xin.at[rows], xin.at[rows], 0, saved, tgt.at[saved], spread[...])

                @pl.when(section > 0)
                def _():
                    cot_copy(ROWS, k, down_one).start()

        @pl.loop(0, chunks)
        def _(i):
            @pl.when(plain_next)
            def _():
                state_copy(xout, ROWS, i, up_one).wait_send()

            if packing:

                @pl.when(packs)
                def _():
                    shorter(packed_state, prows, i, lambda copy: copy.wait_send())

            @pl.when(section > 0)
            def _():
                cot_copy(ROWS, i, down_one).wait_send()

    if packing:

        @pl.when(jnp.logical_not(natural))
        def _():
            turns = chunks // 2
            final_chip = section >= sections - 2
            lag = jnp.where(final_chip, 0, 1)
            for i in range(5):
                mate_weight(i).start()
            prepare_columns()
            for i in range(5):
                mate_weight(i).wait_send()
            prepare_backward()
            prepare_mate()

            @pl.when(section < 4)
            def _():
                xin[total_packed - SPARE : total_packed, :] = jnp.zeros((SPARE, feats), f32)

            def pack_target(j):
                start, first, hits = pack_matrix(j)
                packed[rows_at(j * prows, prows), :] = split_dot(
                    dot, as_onehot(hits), tgt[rows_at(start, WINDOW), :]
                )
                return first, hits

            def places(turn):
                j = 2 * turn + core
                slot = 2 * lax.rem(turn, 2)
                rows, other = rows_at(j * prows, prows), rows_at(swapped(j) * prows, prows)
                saved = [rows_at((slot + part) * ROWS, prows) for part in range(2)]
                keep = [near.at[rows_at((slot + part) * prows, prows)] for part in range(2)]
                return j, slot, rows, other, saved, keep

            @pl.loop(0, turns + lag)
            def _(turn):
                @pl.when(turn < turns)
                def _():
                    @pl.when(turn == 0)
                    def _():
                        target_copy(0).wait()
                        target_copy(1).wait()

                    for i in range(2, 4):

                        @pl.when(2 * turn + i < chunks)
                        def _():
                            target_copy(2 * turn + i).wait()

                    j, slot, rows, other, saved, keep = places(turn)
                    pack_target(swapped(j))
                    pair_copy(swapped(j)).start()
                    first, hits = pack_target(j)
                    for part in range(2):
                        owner = jnp.where(core == part, 0, 1)
                        weight = jnp.zeros((prows, LANES), f32)
                        for i, hit in enumerate(hits):
                            weight += jnp.where(hit, q_ref[owner, pl.ds(first + i, 1), :], 0.0)
                        qring[slot + part] = jnp.broadcast_to(
                            jnp.sum(weight, -1, keepdims=True), (prows, LANES)
                        )
                    packed_receive(prows, j)
                    forward(xin.at[rows], xout.at[other], core, saved[0], keep[0])
                    forward(xout.at[other], xout.at[rows], 1 - core, saved[1], keep[1])

                    @pl.when(jnp.logical_not(final_chip))
                    def _():
                        state_copy(xout, prows, j, up_chip).start()

                @pl.when(turn >= lag)
                def _():
                    @pl.when(turn == lag)
                    def _():
                        finish_weights()

                    j, slot, rows, other, saved, keep = places(turn - lag)
                    part_rows = pl.ds(0, prows)
                    pair_copy(j).wait_recv()

                    def error(part, out):
                        here = core == part
                        target = jnp.where(here, packed[rows, :], cin[other, :])
                        return loss_part(prows, out - target, qring[slot + part])

                    spread[part_rows, :] = error(1, xout[rows, :])

                    @pl.when(jnp.logical_not(final_chip))
                    def _():
                        cot_copy(prows, j, down_chip).wait_recv()
                        spread[part_rows, :] += cin[rows, :]

                    backward(
                        prows,
                        xout.at[other],
                        spread.at[part_rows],
                        1 - core,
                        saved[1],
                        keep[1],
                        spread[part_rows, :],
                    )
                    g = error(0, xout[other, :]) + spread[part_rows, :]
                    backward(prows, xin.at[rows], xin.at[rows], core, saved[0], keep[0], g)
                    cot_do(prows, j, lambda copy: copy.start())

            @pl.loop(0, turns)
            def _(turn):
                j = 2 * turn + core
                cot_do(prows, j, lambda copy: copy.wait_send())
                pair_copy(swapped(j)).wait_send()

                @pl.when(jnp.logical_not(final_chip))
                def _():
                    state_copy(xout, prows, j, up_chip).wait_send()

            for i in range(5):
                mate_gradient(i).start()
            for i in range(5):
                mate_gradient(i).wait_recv()
                if i < 4:
                    acc[i] += xin[columns - (4 - i) * feats : columns - (3 - i) * feats, :]
                else:
                    gain_acc[0:2] += gain_land[...]
            for i in range(5):
                mate_gradient(i).wait_send()

    bits = groups.bit_length() - 1
    halves = feats // PIECE
    pieces = range(4 * halves)
    matrix = [m for m in (3, 1, 2, 0) for _ in range(halves)]
    first = [PIECE * (p % halves) for p in pieces]

    def bit_order(p):
        order = list(range(bits))
        if bits > 1 and p % 4 == 3:
            order[0], order[1] = order[1], order[0]
        return order

    def bit_value(bit):
        return lax.rem(dp // 2**bit, 2)

    def kept_start(p, step):
        start = 0
        for i in range(step):
            start = start + bit_value(bit_order(p)[i]) * (PIECE >> (i + 1))
        return start

    def across(p, step):
        bit = bit_order(p)[step]
        return (section, dp + (1 - 2 * bit_value(bit)) * 2**bit)

    def reduce_copy(p, step):
        size = PIECE >> (step + 1)
        away = 1 - bit_value(bit_order(p)[step])
        start = kept_start(p, step) + away * size
        if step == 0:
            source = acc.at[matrix[p], rows_at(first[p] + start, size, 8)]
        else:
            source = near.at[rows_at(p * PIECE + start, size, 8)]
        return pltpu.make_async_remote_copy(
            src_ref=source,
            dst_ref=land.at[p, pl.ds(PIECE - (PIECE >> step), size)],
            send_sem=rs_send.at[p * bits + step],
            recv_sem=rs_recv.at[p * bits + step],
            device_id=across(p, step),
            device_id_type=MESH,
        )

    def reduce_add(p, step):
        size = PIECE >> (step + 1)
        start = kept_start(p, step + 1)
        if step == 0:
            own = acc[matrix[p], rows_at(first[p] + start, size, 8), :]
        else:
            own = near[rows_at(p * PIECE + start, size, 8), :]
        own = own + land[p, PIECE - (PIECE >> step) : PIECE - (PIECE >> (step + 1)), :]
        if step == bits - 1:
            final[matrix[p], rows_at(first[p] + start, size, 8), :] = own
        else:
            near[rows_at(p * PIECE + start, size, 8), :] = own
        return own

    def gather_copy(p, step):
        rows = rows_at(first[p] + kept_start(p, step + 1), PIECE >> (step + 1), 8)
        return pltpu.make_async_remote_copy(
            src_ref=final.at[matrix[p], rows],
            dst_ref=final.at[matrix[p], rows],
            send_sem=ag_send.at[p * bits + step],
            recv_sem=ag_recv.at[p * bits + step],
            device_id=across(p, step),
            device_id_type=MESH,
        )

    def small_copy(step):
        return pltpu.make_async_remote_copy(
            src_ref=small.at[dp],
            dst_ref=small.at[dp],
            send_sem=small_send.at[step],
            recv_sem=small_recv.at[step],
            device_id=peer(step),
            device_id_type=MESH,
        )

    def tiny_copy(step):
        return pltpu.make_async_remote_copy(
            src_ref=tiny.at[section],
            dst_ref=tiny.at[section],
            send_sem=tiny_send.at[step],
            recv_sem=tiny_recv.at[step],
            device_id=(lax.rem(section + step, sections), dp),
            device_id_type=MESH,
        )

    def out_copy(p):
        rows = pl.ds(first[p], PIECE)
        return pltpu.make_async_copy(
            final.at[matrix[p], rows], grads_ref.at[matrix[p], rows], out_sem.at[p]
        )

    for p in pieces:
        reduce_copy(p, 0).start()
    squares = jnp.zeros((1, 1), f32)
    for step in range(bits):
        for p in pieces:
            reduce_copy(p, step).wait_recv()
            own = reduce_add(p, step)
            if step < bits - 1:
                reduce_copy(p, step + 1).start()
            else:
                gather_copy(p, step).start()
                squares = squares + jnp.sum(own * own, axis=(0, 1), keepdims=True)
    loss = jnp.sum(loss_acc[...], axis=(0, 1), keepdims=True)
    wide_row = lax.broadcasted_iota(jnp.int32, (8, feats), 0)
    small[dp] = jnp.where(
        wide_row == 0,
        jnp.sum(gain_acc[0], 0, keepdims=True),
        jnp.where(
            wide_row == 1,
            jnp.sum(gain_acc[1], 0, keepdims=True),
            jnp.where(wide_row < 4, loss, squares),
        ),
    )
    for step in range(1, groups):
        small_copy(step).start()
    for step in range(bits - 1, 0, -1):
        for p in pieces:
            gather_copy(p, step).wait_recv()
            gather_copy(p, step - 1).start()
    for step in range(1, groups):
        small_copy(step).wait_recv()
    total = small[0]
    for other in range(1, groups):
        total = total + small[other]
    gain_squares = jnp.sum(total[0:2] * total[0:2], axis=(0, 1), keepdims=True)
    tiny[section] = jnp.where(tile_row < 4, total[2:3, 0:1], total[4:5, 0:1] + gain_squares)
    for step in range(1, sections):
        tiny_copy(step).start()
    for p in pieces:
        gather_copy(p, 0).wait_recv()
        out_copy(p).start()
    for step in range(1, sections):
        tiny_copy(step).wait_recv()
    whole = tiny[0]
    for other in range(1, sections):
        whole = whole + tiny[other]
    norm = jnp.sqrt(whole[4:5, 0:1])
    clip = jnp.minimum(1.0, clip_limit / norm)
    stats = total
    for row, number in ((2, clip), (3, whole[0:1, 0:1]), (4, weight_ref[0:1, 0:1]), (5, norm)):
        stats = jnp.where(wide_row == row, number, stats)
    stat_ref[...] = stats

    for step in range(1, groups):
        weight_copy(step).wait_send()
        small_copy(step).wait_send()
    for step in range(1, sections):
        tiny_copy(step).wait_send()
    for p in pieces:
        out_copy(p).wait()
        for step in range(bits):
            reduce_copy(p, step).wait_send()
            gather_copy(p, step).wait_send()


def rollout(packing, sections, groups, inputs, target, lengths, lat_index, land, w_up, w_down, gains):
    columns, feats = inputs.shape
    chunks = columns // ROWS
    prows = ROWS * (sections - 2) // sections + 16
    grid_rows = columns // LANES
    packed_bytes = 4 * chunks * prows * feats
    ring = min((SAVE_BYTES - packed_bytes) // (8 * ROWS * feats), chunks)
    bits = groups.bit_length() - 1
    pieces = 4 * feats // PIECE
    hbm = pl.BlockSpec(memory_space=pl.ANY)
    vmem = pl.BlockSpec(memory_space=pltpu.VMEM)
    dma = pltpu.SemaphoreType.DMA
    wide = pltpu.VMEM((columns, feats), f32)
    lows = pltpu.VMEM((4, feats, feats), bf16)
    flat = lambda array: array.reshape(grid_rows, LANES)
    return pl.pallas_call(
        functools.partial(rollout_kernel, sections, groups, packing),
        out_shape=(
            jax.ShapeDtypeStruct((4, feats, feats), f32),
            jax.ShapeDtypeStruct((8, feats), f32),
            jax.ShapeDtypeStruct((1, 1), jnp.int32),
        ),
        in_specs=[hbm] * 8,
        out_specs=(hbm, vmem, vmem),
        scratch_shapes=[
            wide,
            wide,
            wide,
            wide,
            pltpu.VMEM((chunks * prows if packing else 8, feats), f32),
            pltpu.VMEM((NEAR * ROWS, feats), f32),
            pltpu.VMEM((2, ring * ROWS, feats), bf16),
            pltpu.VMEM((2, ring * ROWS, feats), bf16),
            pltpu.VMEM((sections, prows, LANES), f32),
            lows,
            lows,
            lows,
            lows,
            pltpu.VMEM((grid_rows, LANES), f32),
            pltpu.VMEM((2, grid_rows, LANES), f32),
            pltpu.VMEM((8, LANES), f32),
            pltpu.VMEM((8, LANES), f32),
            pltpu.VMEM((8, feats), f32),
            pltpu.VMEM((4, 8, feats), f32),
            pltpu.VMEM((groups, 8, LANES), f32),
            pltpu.VMEM((ROWS, feats), f32),
            pltpu.VMEM((grid_rows, LANES), jnp.int32),
            pltpu.VMEM((grid_rows, LANES), jnp.int32),
            pltpu.VMEM((grid_rows, LANES), jnp.int32),
            pltpu.VMEM((2, 2, feats), f32),
            pltpu.VMEM((8, feats, feats), f32),
            pltpu.VMEM((2, 8, feats), f32),
            pltpu.VMEM((pieces, PIECE, feats), f32),
            pltpu.VMEM((groups, 8, feats), f32),
            pltpu.VMEM((sections, 8, LANES), f32),
            dma((chunks,)),
            dma((chunks,)),
            dma((chunks,)),
            dma((chunks,)),
            dma((chunks,)),
            dma((chunks,)),
            dma((groups,)),
            dma((groups,)),
            dma((pieces * bits,)),
            dma((pieces * bits,)),
            dma((pieces * bits,)),
            dma((pieces * bits,)),
            dma((groups,)),
            dma((groups,)),
            dma((sections,)),
            dma((sections,)),
            dma((pieces,)),
            dma((6,)),
            dma((10,)),
            dma((10,)),
            dma((chunks,)),
            dma((chunks,)),
        ],
        compiler_params=pltpu.CompilerParams(
            collective_id=0 if packing else 1,
            has_side_effects=True,
            vmem_limit_bytes=63 * 1024 * 1024,
        ),
        name="rollout_packed" if packing else "rollout_all",
    )(
        inputs,
        target,
        flat(lengths),
        flat(lat_index),
        flat(land),
        w_up,
        w_down,
        gains,
    )


def adam_step(weights_old, gradient, moment_one, moment_two, decay_rate):
    moment_one = beta_one * moment_one + (1.0 - beta_one) * gradient
    moment_two = beta_two * moment_two + (1.0 - beta_two) * gradient * gradient
    second_hat = moment_two * (1.0 / (1.0 - beta_two**STEP))
    root = second_hat * lax.rsqrt(second_hat)
    pace = moment_one * (learn_rate / (1.0 - beta_one**STEP))
    step = pace * pl.reciprocal(root + adam_eps)
    new_weights = weights_old * (1.0 - learn_rate * decay_rate) - step
    return (new_weights, moment_one, moment_two)


def update_kernel(
    grads_ref,
    stat_hbm,
    w_up,
    w_down,
    gains,
    m_up,
    m_down,
    m_gains,
    v_up,
    v_down,
    v_gains,
    loss_out,
    total_out,
    norm_out,
    new_up,
    new_down,
    new_gains,
    new_m_up,
    new_m_down,
    new_m_gains,
    new_v_up,
    new_v_down,
    new_v_gains,
    held,
    stat_ref,
    gain_ref,
    in_sem,
    out_sem,
    small_in,
    small_out,
):
    old = ((grads_ref, grads_ref), (w_up, w_down), (m_up, m_down), (v_up, v_down))
    new = ((new_up, new_down), (new_m_up, new_m_down), (new_v_up, new_v_down))

    def fetch(i, part):
        source = old[part][i // 2].at[i if part == 0 else i % 2]
        return pltpu.make_async_copy(source, held.at[part, i], in_sem.at[part, i])

    def store(i, part):
        return pltpu.make_async_copy(
            held.at[part + 1, i], new[part][i // 2].at[i % 2], out_sem.at[part, i]
        )

    small_fetch = [pltpu.make_async_copy(stat_hbm, stat_ref, small_in.at[3])]
    small_store = []
    for part, (source, out) in enumerate(
        ((gains, new_gains), (m_gains, new_m_gains), (v_gains, new_v_gains))
    ):
        small_fetch.append(pltpu.make_async_copy(source, gain_ref.at[part], small_in.at[part]))
        small_store.append(pltpu.make_async_copy(gain_ref.at[part], out, small_out.at[part]))
    for copy in small_fetch:
        copy.start()
    for i in range(4):
        for part in range(4):
            fetch(i, part).start()
    for copy in small_fetch:
        copy.wait()
    clip = stat_ref[2:3, 0:1]
    for row, out in ((3, loss_out), (4, total_out), (5, norm_out)):
        out[...] = stat_ref[row : row + 1, 0:1]
    fresh = adam_step(gain_ref[0], stat_ref[0:2] * clip, gain_ref[1], gain_ref[2], 0.0)
    for part in range(3):
        gain_ref[part] = fresh[part]
        small_store[part].start()
    for i in range(4):
        for part in range(4):
            fetch(i, part).wait()
        fresh = adam_step(held[1, i], held[0, i] * clip, held[2, i], held[3, i], weight_decay)
        for part in range(3):
            held[part + 1, i] = fresh[part]
            store(i, part).start()
    for i in range(4):
        for part in range(3):
            store(i, part).wait()
    for copy in small_store:
        copy.wait()


def update(grads, stats, *state):
    hbm = pl.BlockSpec(memory_space=pl.ANY)
    vmem = pl.BlockSpec(memory_space=pltpu.VMEM)
    return pl.pallas_call(
        update_kernel,
        in_specs=[hbm] * 11,
        out_specs=(vmem,) * 3 + (hbm,) * 9,
        out_shape=(jax.ShapeDtypeStruct((1, 1), f32),) * 3
        + tuple(jax.ShapeDtypeStruct(a.shape, f32) for a in state),
        scratch_shapes=[
            pltpu.VMEM((4,) + grads.shape, f32),
            pltpu.VMEM(stats.shape, f32),
            pltpu.VMEM((3,) + state[2].shape, f32),
            pltpu.SemaphoreType.DMA((4, 4)),
            pltpu.SemaphoreType.DMA((3, 4)),
            pltpu.SemaphoreType.DMA((4,)),
            pltpu.SemaphoreType.DMA((3,)),
        ],
        compiler_params=pltpu.CompilerParams(vmem_limit_bytes=63 * 1024 * 1024),
        name="update",
    )(grads, stats, *state)


def per_device(
    inputs,
    targets,
    lengths,
    lat_index,
    land,
    w_up,
    w_down,
    gains,
    m_up,
    m_down,
    m_gains,
    v_up,
    v_down,
    v_gains,
):
    sections, groups = lax.axis_size("section"), lax.axis_size("dp")
    state = tuple(
        a[0] for a in (w_up, w_down, gains, m_up, m_down, m_gains, v_up, v_down, v_gains)
    )
    operands = (inputs, targets[0], lengths, lat_index, land) + state[:3]
    packed = rollout(True, sections, groups, *operands)

    grads, stats, unused = lax.cond(
        packed[2].reshape(()) > 0,
        lambda: rollout(False, sections, groups, *operands),
        lambda: packed,
    )
    new = update(grads, stats, *state)
    return tuple(a.reshape(()) for a in new[:3]) + tuple(a[None] for a in new[3:])


def solution(mesh):
    return jax.shard_map(
        per_device,
        mesh=mesh,
        in_specs=(
            P("dp", None),
            P("section", "dp", None),
            P("dp"),
            P("dp"),
            P("dp"),
            P("section", None, None, None),
            P("section", None, None, None),
            P("section", None, None),
            P("section", None, None, None),
            P("section", None, None, None),
            P("section", None, None),
            P("section", None, None, None),
            P("section", None, None, None),
            P("section", None, None),
        ),
        out_specs=(
            P(),
            P(),
            P(),
            P("section", None, None, None),
            P("section", None, None, None),
            P("section", None, None),
            P("section", None, None, None),
            P("section", None, None, None),
            P("section", None, None),
            P("section", None, None, None),
            P("section", None, None, None),
            P("section", None, None),
        ),
        check_vma=False,
    )
```

```python
import functools
import math

import jax
import jax.numpy as jnp
from jax import lax
from jax.experimental import pallas as pl
from jax.experimental.pallas import tpu as pltpu
from jax.sharding import PartitionSpec as P

NLAT = 128
STEP = 10

norm_eps = 1e-06
clip_limit = 0.05
beta_one = 0.9
beta_two = 0.999
adam_eps = 1e-08
learn_rate = 0.1
weight_decay = 0.01

f32, bf16 = jnp.float32, jnp.bfloat16
MESH = pl.DeviceIdType.MESH
LANES = 128
PIECE = 128
ROWS = 512
SPARE = 80
WINDOW = 1536
SAVE_BYTES = 17 * 1024 * 1024
SLOTS = 10
NEAR = 3


def dot(a, b):
    return jnp.dot(a, b, preferred_element_type=f32)


def dot_lhs_t(a, b):
    return lax.dot_general(a, b, (((0,), (0,)), ((), ())), preferred_element_type=f32)


def split_dot(product, onehot, values):
    high = values.astype(bf16)
    low = (values - high.astype(f32)).astype(bf16)
    return product(onehot, high) + product(onehot, low)


def rollout_kernel(
    sections,
    groups,
    packing,
    inputs_ref,
    target_ref,
    len_hbm,
    lat_hbm,
    land_hbm,
    up_hbm,
    down_hbm,
    gain_hbm,
    grads_ref,
    stat_ref,
    miss_ref,
    xin,
    xout,
    cin,
    tgt,
    packed,
    near,
    save_h,
    save_d,
    qring,
    up_lo,
    up_t,
    down_lo,
    down_t,
    rank_ref,
    q_ref,
    scale_ref,
    weight_ref,
    loss_acc,
    gain_acc,
    wbuf,
    spread,
    len_ref,
    lat_ref,
    land_ref,
    gain_ref,
    acc,
    gain_land,
    land,
    small,
    tiny,
    in_sem,
    tgt_sem,
    st_send,
    st_recv,
    ct_send,
    ct_recv,
    w_send,
    w_recv,
    rs_send,
    rs_recv,
    ag_send,
    ag_recv,
    small_send,
    small_recv,
    tiny_send,
    tiny_recv,
    out_sem,
    weight_sem,
    mate_send,
    mate_recv,
    pair_send,
    pair_recv,
):
    section = lax.axis_index("section")
    dp = lax.axis_index("dp")
    columns = xin.shape[0]
    feats = xin.shape[1]
    chunks = columns // ROWS
    live_rows = ROWS * (sections - 2) // sections
    prows = live_rows + 16
    total_packed = chunks * prows
    expand = live_rows + 512
    last = sections - 1
    core = lax.rem(section, 2)
    mate = section + 1 - 2 * core
    final = acc.at[pl.ds(4, 4)]
    up_ref, down_ref = acc.at[pl.ds(0, 2)], acc.at[pl.ds(2, 2)]
    ring = save_h.shape[1] // ROWS
    natural = section < (2 if packing else sections)
    plain_next = (section == 0) if packing else (section < last)
    packs = (section == 1) if packing else (section < 0)

    def peer(step):
        return (section, lax.rem(dp + step, groups))

    sources = (up_hbm, down_hbm, gain_hbm, len_hbm, lat_hbm, land_hbm)
    places = (up_ref, down_ref, gain_ref.at[0], len_ref, lat_ref, land_ref)
    fetches = [
        pltpu.make_async_copy(source, place, weight_sem.at[i])
        for i, (source, place) in enumerate(zip(sources, places))
    ]
    for fetch in fetches:
        fetch.start()

    barrier = pltpu.get_barrier_semaphore()
    for step in range(1, sections):
        other = lax.rem(section + step, sections)
        pl.semaphore_signal(barrier, inc=1, device_id=(other, dp), device_id_type=MESH)
    for step in range(1, groups):
        pl.semaphore_signal(barrier, inc=1, device_id=peer(step), device_id_type=MESH)

    def rows_at(index, size, align=16):
        return pl.ds(pl.multiple_of(index, align), size)

    def input_copy(i):
        rows = rows_at(i * ROWS, ROWS)
        return pltpu.make_async_copy(inputs_ref.at[rows], xin.at[rows], in_sem.at[i])

    def target_copy(i):
        rows = rows_at(i * ROWS, ROWS)
        return pltpu.make_async_copy(target_ref.at[rows], tgt.at[rows], tgt_sem.at[i])

    def near_copy(i):
        place = rows_at(lax.rem(i, NEAR) * ROWS, ROWS)
        return pltpu.make_async_copy(
            target_ref.at[rows_at(i * ROWS, ROWS)], near.at[place], tgt_sem.at[i]
        )

    @pl.when(section == 0)
    def _():
        @pl.loop(0, NEAR)
        def _(i):
            input_copy(i).start()

    @pl.when(natural)
    def _():
        @pl.loop(0, NEAR)
        def _(i):
            near_copy(i).start()

    @pl.when(jnp.logical_not(natural))
    def _():
        @pl.loop(0, chunks)
        def _(i):
            target_copy(i).start()

    def prepare_backward():
        for layer in range(2):
            up_t[layer] = up_ref[layer].T.astype(bf16)
            down_t[layer] = (0.5 * down_ref[layer]).T.astype(bf16)
        gain_acc[...] = jnp.zeros_like(gain_acc)
        loss_acc[...] = jnp.zeros_like(loss_acc)
        for i in range(4):
            acc[i] = jnp.zeros((feats, feats), f32)

    def mate_weight(i):
        source = gain_ref.at[0] if i == 4 else acc.at[i]
        place = gain_ref.at[1] if i == 4 else acc.at[4 + i]
        return pltpu.make_async_remote_copy(
            src_ref=source,
            dst_ref=place,
            send_sem=mate_send.at[i],
            recv_sem=mate_recv.at[i],
            device_id=(mate, dp),
            device_id_type=MESH,
        )

    def prepare_mate():
        for i in range(5):
            mate_weight(i).wait_recv()
        for layer in range(2):
            up = acc[4 + layer]
            down = acc[6 + layer]
            up_lo[2 + layer] = (0.5 * up).astype(bf16)
            down_lo[2 + layer] = down.astype(bf16)
            up_t[2 + layer] = up.T.astype(bf16)
            down_t[2 + layer] = (0.5 * down).T.astype(bf16)
        for i in range(4, 8):
            acc[i] = jnp.zeros((feats, feats), f32)

    def mate_gradient(i):
        if i < 4:
            source = acc.at[4 + i]
            place = xin.at[pl.ds(columns - (4 - i) * feats, feats)]
        else:
            source, place = gain_acc.at[pl.ds(2, 2)], gain_land
        return pltpu.make_async_remote_copy(
            src_ref=source,
            dst_ref=place,
            send_sem=mate_send.at[5 + i],
            recv_sem=mate_recv.at[5 + i],
            device_id=(mate, dp),
            device_id_type=MESH,
        )

    def pair_copy(j):
        return pltpu.make_async_remote_copy(
            src_ref=packed.at[slot_rows(j, prows)],
            dst_ref=cin.at[rows_at(swapped(j) * prows, prows)],
            send_sem=pair_send.at[j],
            recv_sem=pair_recv.at[j],
            device_id=(mate, dp),
            device_id_type=MESH,
        )

    def slot_rows(j, count):
        return rows_at(lax.rem(j, SLOTS) * prows, count)

    def swapped(j):
        return j + 1 - 2 * lax.rem(j, 2)

    grid_rows = columns // LANES
    tile_row = lax.broadcasted_iota(jnp.int32, (8, LANES), 0)

    def window_start(j):
        shift = jnp.where(j < 7, 0, jnp.where(j < 11, 256, 384))
        return jnp.clip(ROWS * (j - 1) + shift, 0, columns - WINDOW)

    def expand_start(k):
        end = live_rows * k + expand - 288
        end = jnp.where(k >= 11, jnp.minimum(end, prows * (k + 1)), end)
        return jnp.clip(end - expand, 0, total_packed - expand)

    def chunks_for(k):
        return (expand_start(k) + expand - 1) // prows

    def weight_copy(step):
        return pltpu.make_async_remote_copy(
            src_ref=wbuf.at[dp],
            dst_ref=wbuf.at[dp],
            send_sem=w_send.at[step],
            recv_sem=w_recv.at[step],
            device_id=peer(step),
            device_id_type=MESH,
        )

    def prepare_columns():
        length = len_ref[...]
        latitude = (lat_ref[...].astype(f32) + 0.5) * (math.pi / NLAT) - math.pi / 2
        area = jnp.cos(latitude) * (1.0 + land_ref[...].astype(f32))
        q_ref[0] = area * (section < length).astype(f32)
        q_ref[1] = area * (mate < length).astype(f32)
        local_weight = jnp.sum(
            area * jnp.minimum(length, sections).astype(f32), axis=(0, 1), keepdims=True
        )
        misses = jnp.zeros((1, 1), f32)
        if packing:
            beyond = length > 2
            flag = beyond.astype(bf16)
            lane_a = lax.broadcasted_iota(jnp.int32, (LANES, LANES), 0)
            lane_b = lax.broadcasted_iota(jnp.int32, (LANES, LANES), 1)
            within = dot(flag, (lane_a < lane_b).astype(bf16))
            row_total = jnp.sum(flag.astype(f32), axis=1, keepdims=True)
            row_a = lax.broadcasted_iota(jnp.int32, (grid_rows, grid_rows), 0)
            row_b = lax.broadcasted_iota(jnp.int32, (grid_rows, grid_rows), 1)
            before = dot(
                (row_b < row_a).astype(bf16),
                jnp.broadcast_to(row_total, (grid_rows, LANES)).astype(bf16),
            )
            rank = jnp.where(beyond, within + before, -1e6)
            rank_ref[...] = rank
            place = (
                lax.broadcasted_iota(jnp.int32, (grid_rows, LANES), 0) * LANES
                + lax.broadcasted_iota(jnp.int32, (grid_rows, LANES), 1)
            )
            rank_i = rank.astype(jnp.int32)
            missed = beyond & (rank_i >= total_packed - SPARE)
            for j in range(chunks):
                shift = 0 if j < 7 else 256 if j < 11 else 384
                start = min(max(ROWS * (j - 1) + shift, 0), columns - WINDOW)
                member = (rank_i >= j * prows) & (rank_i < (j + 1) * prows)
                ready = ROWS * (j + 2 if j < 7 else j + 3)
                missed |= member & ((place < start) | (place >= min(start + WINDOW, ready)))
            row_chunk = lax.broadcasted_iota(jnp.int32, (grid_rows, LANES), 0) // (ROWS // LANES)
            row_start = expand_start(row_chunk)
            missed |= beyond & ((rank_i < row_start) | (rank_i >= row_start + expand))
            misses = jnp.sum(missed.astype(f32), axis=(0, 1), keepdims=True)
        wbuf[dp] = jnp.where(tile_row < 4, local_weight, misses)
        for step in range(1, groups):
            weight_copy(step).start()

    def finish_weights():
        for step in range(1, groups):
            weight_copy(step).wait_recv()
        total = wbuf[0]
        for other in range(1, groups):
            total = total + wbuf[other]
        weight_ref[...] = total
        miss_ref[...] = (total[4:5, 0:1] > 0.0).astype(jnp.int32)
        scale_ref[...] = 2.0 / jnp.broadcast_to(total[0:1], (8, LANES))

    for fetch in fetches:
        fetch.wait()
    for layer in range(2):
        up_lo[layer] = (0.5 * up_ref[layer]).astype(bf16)
        down_lo[layer] = down_ref[layer].astype(bf16)
    pl.semaphore_wait(barrier, sections - 1 + groups - 1)

    def pack_matrix(j):
        start = window_start(j)
        base = (j * prows).astype(f32)
        target_row = lax.broadcasted_iota(jnp.int32, (prows, LANES), 0).astype(f32)
        first = start // LANES
        hits = []
        for i in range(WINDOW // LANES):
            hits.append(target_row == rank_ref[pl.ds(first + i, 1), :] - base)
        return start, first, hits

    def as_onehot(hits):
        return jnp.concatenate([jnp.where(hit, 1.0, 0.0).astype(bf16) for hit in hits], axis=1)

    def unpack_rows(k):
        start = expand_start(k)
        base = start.astype(f32)
        source_row = lax.broadcasted_iota(jnp.int32, (expand, LANES), 0).astype(f32)
        hits = []
        for i in range(ROWS // LANES):
            hits.append(source_row == rank_ref[pl.ds(k * (ROWS // LANES) + i, 1), :] - base)
        return dot_lhs_t(as_onehot(hits), cin[rows_at(start, expand), :].astype(bf16))

    def forward(source, place, owner, saved, keep):
        x = source[...]
        for layer in range(2):
            if layer == 1:
                keep[...] = x
            r = lax.rsqrt(jnp.mean(x * x, -1, keepdims=True) + norm_eps)
            normed = (x * r * gain_ref[owner, layer : layer + 1]).astype(bf16)
            half = dot(normed, up_lo[2 * owner + layer])
            t = jnp.tanh(half)
            a = 1.0 + t
            h = half * a
            hidden = h.astype(bf16)
            save_h[layer, saved, :] = hidden
            save_d[layer, saved, :] = (a + h * (1.0 - t)).astype(bf16)
            x = x + dot(hidden, down_lo[2 * owner + layer])
        place[...] = x

    def loss_part(size, diff, weight):
        weighted = jnp.concatenate(
            [diff[:, :LANES] * weight, diff[:, LANES:] * weight], axis=1
        )
        loss_acc[...] += jnp.sum((weighted * diff).reshape(size // 8, 8, feats), 0)
        return weighted * scale_ref[0:1, 0:1]

    def backward(size, source, place, owner, saved, keep, g):
        for layer in (1, 0):
            low = g.astype(bf16)
            acc[4 * owner + 2 + layer] += dot_lhs_t(save_h[layer, saved, :], low)
            pull = dot(low, down_t[2 * owner + layer])
            g_pre = (pull * save_d[layer, saved, :].astype(f32)).astype(bf16)
            x = keep[...] if layer == 1 else source[...]
            r = lax.rsqrt(jnp.mean(x * x, -1, keepdims=True) + norm_eps)
            gain = gain_ref[owner, layer : layer + 1]
            xr = x * r
            normed = (xr * gain).astype(bf16)
            acc[4 * owner + layer] += dot_lhs_t(normed, g_pre)
            g_normed = dot(g_pre, up_t[2 * owner + layer])
            prod = g_normed * xr
            gain_acc[2 * owner + layer] += jnp.sum(prod.reshape(size // 8, 8, feats), 0)
            mean = jnp.mean(prod * gain, -1, keepdims=True)
            g = g + r * (gain * g_normed - xr * mean)
        place[...] = g

    def state_copy(source, size, i, to, count=None):
        rows = rows_at(i * size, size if count is None else count)
        return pltpu.make_async_remote_copy(
            src_ref=source.at[rows],
            dst_ref=xin.at[rows],
            send_sem=st_send.at[i],
            recv_sem=st_recv.at[i],
            device_id=(to, dp),
            device_id_type=MESH,
        )

    def cot_copy(size, i, to, count=None):
        rows = rows_at(i * size, size if count is None else count)
        return pltpu.make_async_remote_copy(
            src_ref=xin.at[rows],
            dst_ref=cin.at[rows],
            send_sem=ct_send.at[i],
            recv_sem=ct_recv.at[i],
            device_id=(to, dp),
            device_id_type=MESH,
        )

    up_one = lax.rem(section + 1, sections)
    down_one = lax.rem(section + sections - 1, sections)
    up_chip = lax.rem(section + 2, sections)
    down_chip = jnp.where(section < 4, 1, section - 2)

    def shorter(copy, size, i, action):
        @pl.when(i < chunks - 1)
        def _():
            action(copy(size, i, size))

        @pl.when(i == chunks - 1)
        def _():
            action(copy(size, i, size - SPARE))

    def packed_state(size, i, count):
        return pltpu.make_async_remote_copy(
            src_ref=packed.at[slot_rows(i, count)],
            dst_ref=xin.at[rows_at(i * size, count)],
            send_sem=st_send.at[i],
            recv_sem=st_recv.at[i],
            device_id=(2 + lax.rem(i, 2), dp),
            device_id_type=MESH,
        )

    def packed_receive(size, i):
        @pl.when(section < 4)
        def _():
            shorter(packed_state, size, i, lambda copy: copy.wait_recv())

        @pl.when(section >= 4)
        def _():
            state_copy(xout, size, i, up_chip).wait_recv()

    def cot_part(size, i, count):
        return cot_copy(size, i, down_chip, count)

    def cot_wait(size, i):
        shorter(cot_part, size, i, lambda copy: copy.wait_recv())

    def cot_do(size, i, action):
        @pl.when(section < 4)
        def _():
            shorter(cot_part, size, i, action)

        @pl.when(section >= 4)
        def _():
            action(cot_copy(size, i, down_chip))

    @pl.when(natural)
    def _():
        if packing:
            most = chunks if ring == chunks else ring - 1
            lag = jnp.where(section == 0, most, most - 2)
        else:
            lag = jnp.minimum(ring - 1, 3 * (last - section))

        @pl.when(section > 0)
        def _():
            prepare_columns()
            if packing:
                xout[2 * ROWS : WINDOW, :] = jnp.zeros((WINDOW - 2 * ROWS, feats), f32)
                cin[total_packed - SPARE : total_packed, :] = jnp.zeros((SPARE, feats), f32)

        @pl.loop(0, chunks + lag)
        def _(t):
            @pl.when(t < chunks)
            def _():
                @pl.when(section == 0)
                def _():
                    input_copy(t).wait()

                    @pl.when(t + NEAR < chunks)
                    def _():
                        input_copy(t + NEAR).start()

                @pl.when(section > 0)
                def _():
                    state_copy(xout, ROWS, t, up_one).wait_recv()

                rows = rows_at(t * ROWS, ROWS)
                saved = rows_at(lax.rem(t, ring) * ROWS, ROWS)
                forward(xin.at[rows], xout.at[rows], 0, saved, tgt.at[saved])

                @pl.when(plain_next)
                def _():
                    state_copy(xout, ROWS, t, up_one).start()

            if packing:

                j = jnp.where(t < 8, t - 1, t - 2)

                @pl.when(packs & (t >= 1) & (t != 8) & (j < chunks))
                def _():
                    start, _, hits = pack_matrix(j)

                    @pl.when(j >= SLOTS)
                    def _():
                        shorter(packed_state, prows, j - SLOTS, lambda copy: copy.wait_send())

                    packed[slot_rows(j, prows), :] = split_dot(
                        dot, as_onehot(hits), xout[rows_at(start, WINDOW), :]
                    )
                    shorter(packed_state, prows, j, lambda copy: copy.start())

            @pl.when((section == 0) & (t == 3))
            def _():
                prepare_columns()

            @pl.when(t == jnp.minimum(lag, 4))
            def _():
                prepare_backward()

            k = t - lag

            @pl.when((k >= 0) & (k < chunks))
            def _():
                @pl.when(k == 0)
                def _():
                    finish_weights()

                near_copy(k).wait()
                rows = rows_at(k * ROWS, ROWS)
                place = rows_at(lax.rem(k, NEAR) * ROWS, ROWS)
                saved = rows_at(lax.rem(k, ring) * ROWS, ROWS)

                weight = jnp.concatenate(
                    [
                        jnp.broadcast_to(
                            q_ref[0, pl.ds(k * (ROWS // LANES) + i, 1), :], (LANES, LANES)
                        ).T
                        for i in range(ROWS // LANES)
                    ],
                    axis=0,
                )
                diff = xout[rows, :] - near[place, :]
                spread[...] = loss_part(ROWS, diff, weight)

                @pl.when(k + NEAR < chunks)
                def _():
                    near_copy(k + NEAR).start()

                @pl.when(plain_next)
                def _():
                    cot_copy(ROWS, k, down_one).wait_recv()
                    spread[...] += cin[rows, :]

                if packing:

                    @pl.when(packs)
                    def _():
                        had = jnp.where(k == 0, -1, chunks_for(jnp.maximum(k - 1, 0)))
                        for i in range(3):

                            @pl.when(had + 1 + i <= chunks_for(k))
                            def _():
                                cot_wait(prows, had + 1 + i)

                        spread[...] += unpack_rows(k)

                backward(ROWS, xin.at[rows], xin.at[rows], 0, saved, tgt.at[saved], spread[...])

                @pl.when(section > 0)
                def _():
                    cot_copy(ROWS, k, down_one).start()

        @pl.loop(0, chunks)
        def _(i):
            @pl.when(plain_next)
            def _():
                state_copy(xout, ROWS, i, up_one).wait_send()

            if packing:

                @pl.when(packs & (i + SLOTS >= chunks))
                def _():
                    shorter(packed_state, prows, i, lambda copy: copy.wait_send())

            @pl.when(section > 0)
            def _():
                cot_copy(ROWS, i, down_one).wait_send()

    if packing:

        @pl.when(jnp.logical_not(natural))
        def _():
            turns = chunks // 2
            final_chip = section >= sections - 2
            lag = jnp.where(final_chip, 0, 1)
            for i in range(5):
                mate_weight(i).start()
            prepare_columns()
            for i in range(5):
                mate_weight(i).wait_send()
            prepare_backward()
            prepare_mate()

            @pl.when(section < 4)
            def _():
                xin[total_packed - SPARE : total_packed, :] = jnp.zeros((SPARE, feats), f32)

            def pack_target(j):
                start, first, hits = pack_matrix(j)
                packed[slot_rows(j, prows), :] = split_dot(
                    dot, as_onehot(hits), tgt[rows_at(start, WINDOW), :]
                )
                return first, hits

            def places(turn):
                j = 2 * turn + core
                slot = 2 * lax.rem(turn, 2)
                rows, other = rows_at(j * prows, prows), rows_at(swapped(j) * prows, prows)
                saved = [rows_at((slot + part) * ROWS, prows) for part in range(2)]
                keep = [near.at[rows_at((slot + part) * prows, prows)] for part in range(2)]
                return j, slot, rows, other, saved, keep

            @pl.loop(0, turns + lag)
            def _(turn):
                @pl.when(turn < turns)
                def _():
                    @pl.when(turn == 0)
                    def _():
                        target_copy(0).wait()
                        target_copy(1).wait()

                    for i in range(2, 4):

                        @pl.when(2 * turn + i < chunks)
                        def _():
                            target_copy(2 * turn + i).wait()

                    j, slot, rows, other, saved, keep = places(turn)

                    @pl.when(swapped(j) >= SLOTS)
                    def _():
                        pair_copy(swapped(j) - SLOTS).wait_send()

                    pack_target(swapped(j))
                    pair_copy(swapped(j)).start()
                    first, hits = pack_target(j)
                    for part in range(2):
                        owner = jnp.where(core == part, 0, 1)
                        weight = jnp.zeros((prows, LANES), f32)
                        for i, hit in enumerate(hits):
                            weight += jnp.where(hit, q_ref[owner, pl.ds(first + i, 1), :], 0.0)
                        qring[slot + part] = jnp.broadcast_to(
                            jnp.sum(weight, -1, keepdims=True), (prows, LANES)
                        )
                    packed_receive(prows, j)
                    forward(xin.at[rows], xout.at[other], core, saved[0], keep[0])
                    forward(xout.at[other], xout.at[rows], 1 - core, saved[1], keep[1])

                    @pl.when(jnp.logical_not(final_chip))
                    def _():
                        state_copy(xout, prows, j, up_chip).start()

                @pl.when(turn >= lag)
                def _():
                    @pl.when(turn == lag)
                    def _():
                        finish_weights()

                    j, slot, rows, other, saved, keep = places(turn - lag)
                    part_rows = pl.ds(0, prows)
                    pair_copy(j).wait_recv()

                    def error(part, out):
                        here = core == part
                        target = jnp.where(here, packed[slot_rows(j, prows), :], cin[other, :])
                        return loss_part(prows, out - target, qring[slot + part])

                    spread[part_rows, :] = error(1, xout[rows, :])

                    @pl.when(jnp.logical_not(final_chip))
                    def _():
                        cot_copy(prows, j, down_chip).wait_recv()
                        spread[part_rows, :] += cin[rows, :]

                    backward(
                        prows,
                        xout.at[other],
                        spread.at[part_rows],
                        1 - core,
                        saved[1],
                        keep[1],
                        spread[part_rows, :],
                    )
                    g = error(0, xout[other, :]) + spread[part_rows, :]
                    backward(prows, xin.at[rows], xin.at[rows], core, saved[0], keep[0], g)
                    cot_do(prows, j, lambda copy: copy.start())

            @pl.loop(0, turns)
            def _(turn):
                j = 2 * turn + core
                cot_do(prows, j, lambda copy: copy.wait_send())

                @pl.when(swapped(j) + SLOTS >= chunks)
                def _():
                    pair_copy(swapped(j)).wait_send()

                @pl.when(jnp.logical_not(final_chip))
                def _():
                    state_copy(xout, prows, j, up_chip).wait_send()

            for i in range(5):
                mate_gradient(i).start()
            for i in range(5):
                mate_gradient(i).wait_recv()
                if i < 4:
                    acc[i] += xin[columns - (4 - i) * feats : columns - (3 - i) * feats, :]
                else:
                    gain_acc[0:2] += gain_land[...]
            for i in range(5):
                mate_gradient(i).wait_send()

    bits = groups.bit_length() - 1
    halves = feats // PIECE
    pieces = range(4 * halves)
    matrix = [m for m in (3, 1, 2, 0) for _ in range(halves)]
    first = [PIECE * (p % halves) for p in pieces]

    def bit_order(p):
        order = list(range(bits))
        if bits > 1 and p % 2 == 0:
            order[0], order[1] = order[1], order[0]
        return order

    def bit_value(bit):
        return lax.rem(dp // 2**bit, 2)

    def kept_start(p, step):
        start = 0
        for i in range(step):
            start = start + bit_value(bit_order(p)[i]) * (PIECE >> (i + 1))
        return start

    def across(p, step):
        bit = bit_order(p)[step]
        return (section, dp + (1 - 2 * bit_value(bit)) * 2**bit)

    def reduce_copy(p, step):
        size = PIECE >> (step + 1)
        away = 1 - bit_value(bit_order(p)[step])
        start = kept_start(p, step) + away * size
        if step == 0:
            source = acc.at[matrix[p], rows_at(first[p] + start, size, 8)]
        else:
            source = near.at[rows_at(p * PIECE + start, size, 8)]
        return pltpu.make_async_remote_copy(
            src_ref=source,
            dst_ref=land.at[p, pl.ds(PIECE - (PIECE >> step), size)],
            send_sem=rs_send.at[p * bits + step],
            recv_sem=rs_recv.at[p * bits + step],
            device_id=across(p, step),
            device_id_type=MESH,
        )

    def reduce_add(p, step):
        size = PIECE >> (step + 1)
        start = kept_start(p, step + 1)
        if step == 0:
            own = acc[matrix[p], rows_at(first[p] + start, size, 8), :]
        else:
            own = near[rows_at(p * PIECE + start, size, 8), :]
        own = own + land[p, PIECE - (PIECE >> step) : PIECE - (PIECE >> (step + 1)), :]
        if step == bits - 1:
            final[matrix[p], rows_at(first[p] + start, size, 8), :] = own
        else:
            near[rows_at(p * PIECE + start, size, 8), :] = own
        return own

    def gather_copy(p, step):
        rows = rows_at(first[p] + kept_start(p, step + 1), PIECE >> (step + 1), 8)
        return pltpu.make_async_remote_copy(
            src_ref=final.at[matrix[p], rows],
            dst_ref=final.at[matrix[p], rows],
            send_sem=ag_send.at[p * bits + step],
            recv_sem=ag_recv.at[p * bits + step],
            device_id=across(p, step),
            device_id_type=MESH,
        )

    def small_copy(step):
        return pltpu.make_async_remote_copy(
            src_ref=small.at[dp],
            dst_ref=small.at[dp],
            send_sem=small_send.at[step],
            recv_sem=small_recv.at[step],
            device_id=peer(step),
            device_id_type=MESH,
        )

    def tiny_copy(step):
        return pltpu.make_async_remote_copy(
            src_ref=tiny.at[section],
            dst_ref=tiny.at[section],
            send_sem=tiny_send.at[step],
            recv_sem=tiny_recv.at[step],
            device_id=(lax.rem(section + step, sections), dp),
            device_id_type=MESH,
        )

    def out_copy(p):
        rows = pl.ds(first[p], PIECE)
        return pltpu.make_async_copy(
            final.at[matrix[p], rows], grads_ref.at[matrix[p], rows], out_sem.at[p]
        )

    for p in pieces:
        reduce_copy(p, 0).start()
    squares = jnp.zeros((1, 1), f32)
    for step in range(bits):
        for p in pieces:
            reduce_copy(p, step).wait_recv()
            own = reduce_add(p, step)
            if step < bits - 1:
                reduce_copy(p, step + 1).start()
            else:
                gather_copy(p, step).start()
                squares = squares + jnp.sum(own * own, axis=(0, 1), keepdims=True)
    loss = jnp.sum(loss_acc[...], axis=(0, 1), keepdims=True)
    wide_row = lax.broadcasted_iota(jnp.int32, (8, feats), 0)
    small[dp] = jnp.where(
        wide_row == 0,
        jnp.sum(gain_acc[0], 0, keepdims=True),
        jnp.where(
            wide_row == 1,
            jnp.sum(gain_acc[1], 0, keepdims=True),
            jnp.where(wide_row < 4, loss, squares),
        ),
    )
    for step in range(1, groups):
        small_copy(step).start()
    for step in range(bits - 1, 0, -1):
        for p in pieces:
            gather_copy(p, step).wait_recv()
            gather_copy(p, step - 1).start()
    for step in range(1, groups):
        small_copy(step).wait_recv()
    total = small[0]
    for other in range(1, groups):
        total = total + small[other]
    gain_squares = jnp.sum(total[0:2] * total[0:2], axis=(0, 1), keepdims=True)
    tiny[section] = jnp.where(tile_row < 4, total[2:3, 0:1], total[4:5, 0:1] + gain_squares)
    for step in range(1, sections):
        tiny_copy(step).start()
    for p in pieces:
        gather_copy(p, 0).wait_recv()
        out_copy(p).start()
    for step in range(1, sections):
        tiny_copy(step).wait_recv()
    whole = tiny[0]
    for other in range(1, sections):
        whole = whole + tiny[other]
    norm = jnp.sqrt(whole[4:5, 0:1])
    clip = jnp.minimum(1.0, clip_limit / norm)
    stats = total
    for row, number in ((2, clip), (3, whole[0:1, 0:1]), (4, weight_ref[0:1, 0:1]), (5, norm)):
        stats = jnp.where(wide_row == row, number, stats)
    stat_ref[...] = stats

    for step in range(1, groups):
        weight_copy(step).wait_send()
        small_copy(step).wait_send()
    for step in range(1, sections):
        tiny_copy(step).wait_send()
    for p in pieces:
        out_copy(p).wait()
        for step in range(bits):
            reduce_copy(p, step).wait_send()
            gather_copy(p, step).wait_send()


def rollout(packing, sections, groups, inputs, target, lengths, lat_index, land, w_up, w_down, gains):
    columns, feats = inputs.shape
    chunks = columns // ROWS
    prows = ROWS * (sections - 2) // sections + 16
    grid_rows = columns // LANES
    packed_bytes = 4 * SLOTS * prows * feats
    ring = min((SAVE_BYTES - packed_bytes) // (8 * ROWS * feats), chunks)
    bits = groups.bit_length() - 1
    pieces = 4 * feats // PIECE
    hbm = pl.BlockSpec(memory_space=pl.ANY)
    vmem = pl.BlockSpec(memory_space=pltpu.VMEM)
    dma = pltpu.SemaphoreType.DMA
    wide = pltpu.VMEM((columns, feats), f32)
    lows = pltpu.VMEM((4, feats, feats), bf16)
    flat = lambda array: array.reshape(grid_rows, LANES)
    return pl.pallas_call(
        functools.partial(rollout_kernel, sections, groups, packing),
        out_shape=(
            jax.ShapeDtypeStruct((4, feats, feats), f32),
            jax.ShapeDtypeStruct((8, feats), f32),
            jax.ShapeDtypeStruct((1, 1), jnp.int32),
        ),
        in_specs=[hbm] * 8,
        out_specs=(hbm, vmem, vmem),
        scratch_shapes=[
            wide,
            wide,
            wide,
            wide,
            pltpu.VMEM((SLOTS * prows if packing else 8, feats), f32),
            pltpu.VMEM((max(NEAR * ROWS, 4 * prows), feats), f32),
            pltpu.VMEM((2, ring * ROWS, feats), bf16),
            pltpu.VMEM((2, ring * ROWS, feats), bf16),
            pltpu.VMEM((sections, prows, LANES), f32),
            lows,
            lows,
            lows,
            lows,
            pltpu.VMEM((grid_rows, LANES), f32),
            pltpu.VMEM((2, grid_rows, LANES), f32),
            pltpu.VMEM((8, LANES), f32),
            pltpu.VMEM((8, LANES), f32),
            pltpu.VMEM((8, feats), f32),
            pltpu.VMEM((4, 8, feats), f32),
            pltpu.VMEM((groups, 8, LANES), f32),
            pltpu.VMEM((ROWS, feats), f32),
            pltpu.VMEM((grid_rows, LANES), jnp.int32),
            pltpu.VMEM((grid_rows, LANES), jnp.int32),
            pltpu.VMEM((grid_rows, LANES), jnp.int32),
            pltpu.VMEM((2, 2, feats), f32),
            pltpu.VMEM((8, feats, feats), f32),
            pltpu.VMEM((2, 8, feats), f32),
            pltpu.VMEM((pieces, PIECE, feats), f32),
            pltpu.VMEM((groups, 8, feats), f32),
            pltpu.VMEM((sections, 8, LANES), f32),
            dma((chunks,)),
            dma((chunks,)),
            dma((chunks,)),
            dma((chunks,)),
            dma((chunks,)),
            dma((chunks,)),
            dma((groups,)),
            dma((groups,)),
            dma((pieces * bits,)),
            dma((pieces * bits,)),
            dma((pieces * bits,)),
            dma((pieces * bits,)),
            dma((groups,)),
            dma((groups,)),
            dma((sections,)),
            dma((sections,)),
            dma((pieces,)),
            dma((6,)),
            dma((10,)),
            dma((10,)),
            dma((chunks,)),
            dma((chunks,)),
        ],
        compiler_params=pltpu.CompilerParams(
            collective_id=0 if packing else 1,
            has_side_effects=True,
            vmem_limit_bytes=63 * 1024 * 1024,
        ),
        name="rollout_packed" if packing else "rollout_all",
    )(
        inputs,
        target,
        flat(lengths),
        flat(lat_index),
        flat(land),
        w_up,
        w_down,
        gains,
    )


def adam_step(weights_old, gradient, moment_one, moment_two, decay_rate):
    moment_one = beta_one * moment_one + (1.0 - beta_one) * gradient
    moment_two = beta_two * moment_two + (1.0 - beta_two) * gradient * gradient
    second_hat = moment_two * (1.0 / (1.0 - beta_two**STEP))
    root = second_hat * lax.rsqrt(second_hat)
    pace = moment_one * (learn_rate / (1.0 - beta_one**STEP))
    step = pace * pl.reciprocal(root + adam_eps)
    new_weights = weights_old * (1.0 - learn_rate * decay_rate) - step
    return (new_weights, moment_one, moment_two)


def update_kernel(
    grads_ref,
    stat_hbm,
    w_up,
    w_down,
    gains,
    m_up,
    m_down,
    m_gains,
    v_up,
    v_down,
    v_gains,
    loss_out,
    total_out,
    norm_out,
    new_up,
    new_down,
    new_gains,
    new_m_up,
    new_m_down,
    new_m_gains,
    new_v_up,
    new_v_down,
    new_v_gains,
    held,
    stat_ref,
    gain_ref,
    in_sem,
    out_sem,
    small_in,
    small_out,
):
    old = ((grads_ref, grads_ref), (w_up, w_down), (m_up, m_down), (v_up, v_down))
    new = ((new_up, new_down), (new_m_up, new_m_down), (new_v_up, new_v_down))

    def fetch(i, part):
        source = old[part][i // 2].at[i if part == 0 else i % 2]
        return pltpu.make_async_copy(source, held.at[part, i], in_sem.at[part, i])

    def store(i, part):
        return pltpu.make_async_copy(
            held.at[part + 1, i], new[part][i // 2].at[i % 2], out_sem.at[part, i]
        )

    small_fetch = [pltpu.make_async_copy(stat_hbm, stat_ref, small_in.at[3])]
    small_store = []
    for part, (source, out) in enumerate(
        ((gains, new_gains), (m_gains, new_m_gains), (v_gains, new_v_gains))
    ):
        small_fetch.append(pltpu.make_async_copy(source, gain_ref.at[part], small_in.at[part]))
        small_store.append(pltpu.make_async_copy(gain_ref.at[part], out, small_out.at[part]))
    for copy in small_fetch:
        copy.start()
    for i in range(4):
        for part in range(4):
            fetch(i, part).start()
    for copy in small_fetch:
        copy.wait()
    clip = stat_ref[2:3, 0:1]
    for row, out in ((3, loss_out), (4, total_out), (5, norm_out)):
        out[...] = stat_ref[row : row + 1, 0:1]
    fresh = adam_step(gain_ref[0], stat_ref[0:2] * clip, gain_ref[1], gain_ref[2], 0.0)
    for part in range(3):
        gain_ref[part] = fresh[part]
        small_store[part].start()
    for i in range(4):
        for part in range(4):
            fetch(i, part).wait()
        fresh = adam_step(held[1, i], held[0, i] * clip, held[2, i], held[3, i], weight_decay)
        for part in range(3):
            held[part + 1, i] = fresh[part]
            store(i, part).start()
    for i in range(4):
        for part in range(3):
            store(i, part).wait()
    for copy in small_store:
        copy.wait()


def update(grads, stats, *state):
    hbm = pl.BlockSpec(memory_space=pl.ANY)
    vmem = pl.BlockSpec(memory_space=pltpu.VMEM)
    return pl.pallas_call(
        update_kernel,
        in_specs=[hbm] * 11,
        out_specs=(vmem,) * 3 + (hbm,) * 9,
        out_shape=(jax.ShapeDtypeStruct((1, 1), f32),) * 3
        + tuple(jax.ShapeDtypeStruct(a.shape, f32) for a in state),
        scratch_shapes=[
            pltpu.VMEM((4,) + grads.shape, f32),
            pltpu.VMEM(stats.shape, f32),
            pltpu.VMEM((3,) + state[2].shape, f32),
            pltpu.SemaphoreType.DMA((4, 4)),
            pltpu.SemaphoreType.DMA((3, 4)),
            pltpu.SemaphoreType.DMA((4,)),
            pltpu.SemaphoreType.DMA((3,)),
        ],
        compiler_params=pltpu.CompilerParams(vmem_limit_bytes=63 * 1024 * 1024),
        name="update",
    )(grads, stats, *state)


def per_device(
    inputs,
    targets,
    lengths,
    lat_index,
    land,
    w_up,
    w_down,
    gains,
    m_up,
    m_down,
    m_gains,
    v_up,
    v_down,
    v_gains,
):
    sections, groups = lax.axis_size("section"), lax.axis_size("dp")
    state = tuple(
        a[0] for a in (w_up, w_down, gains, m_up, m_down, m_gains, v_up, v_down, v_gains)
    )
    operands = (inputs, targets[0], lengths, lat_index, land) + state[:3]
    packed = rollout(True, sections, groups, *operands)

    grads, stats, unused = lax.cond(
        packed[2].reshape(()) > 0,
        lambda: rollout(False, sections, groups, *operands),
        lambda: packed,
    )
    new = update(grads, stats, *state)
    return tuple(a.reshape(()) for a in new[:3]) + tuple(a[None] for a in new[3:])


def solution(mesh):
    return jax.shard_map(
        per_device,
        mesh=mesh,
        in_specs=(
            P("dp", None),
            P("section", "dp", None),
            P("dp"),
            P("dp"),
            P("dp"),
            P("section", None, None, None),
            P("section", None, None, None),
            P("section", None, None),
            P("section", None, None, None),
            P("section", None, None, None),
            P("section", None, None),
            P("section", None, None, None),
            P("section", None, None, None),
            P("section", None, None),
        ),
        out_specs=(
            P(),
            P(),
            P(),
            P("section", None, None, None),
            P("section", None, None, None),
            P("section", None, None),
            P("section", None, None, None),
            P("section", None, None, None),
            P("section", None, None),
            P("section", None, None, None),
            P("section", None, None, None),
            P("section", None, None),
        ),
        check_vma=False,
    )
```

```python
import functools
import math

import jax
import jax.numpy as jnp
from jax import lax
from jax.experimental import pallas as pl
from jax.experimental.pallas import tpu as pltpu
from jax.sharding import PartitionSpec as P

NLAT = 128
STEP = 10

norm_eps = 1e-06
clip_limit = 0.05
beta_one = 0.9
beta_two = 0.999
adam_eps = 1e-08
learn_rate = 0.1
weight_decay = 0.01

f32, bf16 = jnp.float32, jnp.bfloat16
MESH = pl.DeviceIdType.MESH
LANES = 128
PIECE = 128
ROWS = 512
SPARE = 80
WINDOW = 1536
SAVE_BYTES = 17 * 1024 * 1024
SLOTS = 10
NEAR = 3


def dot(a, b):
    return jnp.dot(a, b, preferred_element_type=f32)


def dot_lhs_t(a, b):
    return lax.dot_general(a, b, (((0,), (0,)), ((), ())), preferred_element_type=f32)


def split_dot(product, onehot, values):
    high = values.astype(bf16)
    low = (values - high.astype(f32)).astype(bf16)
    return product(onehot, high) + product(onehot, low)


def rollout_kernel(
    sections,
    groups,
    packing,
    inputs_ref,
    target_ref,
    len_hbm,
    lat_hbm,
    land_hbm,
    up_hbm,
    down_hbm,
    gain_hbm,
    grads_ref,
    stat_ref,
    miss_ref,
    xin,
    xout,
    cin,
    tgt,
    packed,
    near,
    save_h,
    save_d,
    qring,
    up_lo,
    up_t,
    down_lo,
    down_t,
    rank_ref,
    q_ref,
    scale_ref,
    weight_ref,
    loss_acc,
    gain_acc,
    wbuf,
    spread,
    len_ref,
    lat_ref,
    land_ref,
    gain_ref,
    acc,
    gain_land,
    land,
    small,
    tiny,
    in_sem,
    tgt_sem,
    st_send,
    st_recv,
    ct_send,
    ct_recv,
    w_send,
    w_recv,
    rs_send,
    rs_recv,
    ag_send,
    ag_recv,
    small_send,
    small_recv,
    tiny_send,
    tiny_recv,
    out_sem,
    weight_sem,
    mate_send,
    mate_recv,
    pair_send,
    pair_recv,
):
    section = lax.axis_index("section")
    dp = lax.axis_index("dp")
    columns = xin.shape[0]
    feats = xin.shape[1]
    chunks = columns // ROWS
    live_rows = ROWS * (sections - 2) // sections
    prows = live_rows + 16
    total_packed = chunks * prows
    expand = live_rows + 512
    last = sections - 1
    core = lax.rem(section, 2)
    mate = section + 1 - 2 * core
    final = acc.at[pl.ds(4, 4)]
    up_ref, down_ref = acc.at[pl.ds(0, 2)], acc.at[pl.ds(2, 2)]
    ring = save_h.shape[1] // ROWS
    natural = section < (2 if packing else sections)
    plain_next = (section == 0) if packing else (section < last)
    packs = (section == 1) if packing else (section < 0)

    def peer(step):
        return (section, lax.rem(dp + step, groups))

    sources = (up_hbm, down_hbm, gain_hbm, len_hbm, lat_hbm, land_hbm)
    places = (up_ref, down_ref, gain_ref.at[0], len_ref, lat_ref, land_ref)
    fetches = [
        pltpu.make_async_copy(source, place, weight_sem.at[i])
        for i, (source, place) in enumerate(zip(sources, places))
    ]
    for fetch in fetches:
        fetch.start()

    barrier = pltpu.get_barrier_semaphore()
    for step in range(1, sections):
        other = lax.rem(section + step, sections)
        pl.semaphore_signal(barrier, inc=1, device_id=(other, dp), device_id_type=MESH)
    for step in range(1, groups):
        pl.semaphore_signal(barrier, inc=1, device_id=peer(step), device_id_type=MESH)

    def rows_at(index, size, align=16):
        return pl.ds(pl.multiple_of(index, align), size)

    def input_copy(i):
        rows = rows_at(i * ROWS, ROWS)
        return pltpu.make_async_copy(inputs_ref.at[rows], xin.at[rows], in_sem.at[i])

    def target_copy(i):
        rows = rows_at(i * ROWS, ROWS)
        return pltpu.make_async_copy(target_ref.at[rows], tgt.at[rows], tgt_sem.at[i])

    def near_copy(i):
        place = rows_at(lax.rem(i, NEAR) * ROWS, ROWS)
        return pltpu.make_async_copy(
            target_ref.at[rows_at(i * ROWS, ROWS)], near.at[place], tgt_sem.at[i]
        )

    @pl.when(section == 0)
    def _():
        @pl.loop(0, NEAR)
        def _(i):
            input_copy(i).start()

    @pl.when(natural)
    def _():
        @pl.loop(0, NEAR)
        def _(i):
            near_copy(i).start()

    @pl.when(jnp.logical_not(natural))
    def _():
        @pl.loop(0, chunks)
        def _(i):
            target_copy(i).start()

    def prepare_backward():
        for layer in range(2):
            up_t[layer] = up_ref[layer].T.astype(bf16)
            down_t[layer] = (0.5 * down_ref[layer]).T.astype(bf16)
        gain_acc[...] = jnp.zeros_like(gain_acc)
        loss_acc[...] = jnp.zeros_like(loss_acc)
        for i in range(4):
            acc[i] = jnp.zeros((feats, feats), f32)

    def mate_weight(i):
        source = gain_ref.at[0] if i == 4 else acc.at[i]
        place = gain_ref.at[1] if i == 4 else acc.at[4 + i]
        return pltpu.make_async_remote_copy(
            src_ref=source,
            dst_ref=place,
            send_sem=mate_send.at[i],
            recv_sem=mate_recv.at[i],
            device_id=(mate, dp),
            device_id_type=MESH,
        )

    def prepare_mate():
        for i in range(5):
            mate_weight(i).wait_recv()
        for layer in range(2):
            up = acc[4 + layer]
            down = acc[6 + layer]
            up_lo[2 + layer] = (0.5 * up).astype(bf16)
            down_lo[2 + layer] = down.astype(bf16)
            up_t[2 + layer] = up.T.astype(bf16)
            down_t[2 + layer] = (0.5 * down).T.astype(bf16)
        for i in range(4, 8):
            acc[i] = jnp.zeros((feats, feats), f32)

    def mate_gradient(i):
        if i < 4:
            source = acc.at[4 + i]
            place = xin.at[pl.ds(columns - (4 - i) * feats, feats)]
        else:
            source, place = gain_acc.at[pl.ds(2, 2)], gain_land
        return pltpu.make_async_remote_copy(
            src_ref=source,
            dst_ref=place,
            send_sem=mate_send.at[5 + i],
            recv_sem=mate_recv.at[5 + i],
            device_id=(mate, dp),
            device_id_type=MESH,
        )

    def pair_copy(j):
        return pltpu.make_async_remote_copy(
            src_ref=packed.at[slot_rows(j, prows)],
            dst_ref=cin.at[rows_at(swapped(j) * prows, prows)],
            send_sem=pair_send.at[j],
            recv_sem=pair_recv.at[j],
            device_id=(mate, dp),
            device_id_type=MESH,
        )

    def slot_rows(j, count):
        return rows_at(lax.rem(j, SLOTS) * prows, count)

    def swapped(j):
        return j + 1 - 2 * lax.rem(j, 2)

    grid_rows = columns // LANES
    tile_row = lax.broadcasted_iota(jnp.int32, (8, LANES), 0)

    def window_start(j):
        shift = jnp.where(j < 7, 0, jnp.where(j < 11, 256, 384))
        return jnp.clip(ROWS * (j - 1) + shift, 0, columns - WINDOW)

    def expand_start(k):
        end = live_rows * k + expand - 288
        end = jnp.where(k >= 11, jnp.minimum(end, prows * (k + 1)), end)
        return jnp.clip(end - expand, 0, total_packed - expand)

    def chunks_for(k):
        return (expand_start(k) + expand - 1) // prows

    def weight_copy(step):
        return pltpu.make_async_remote_copy(
            src_ref=wbuf.at[dp],
            dst_ref=wbuf.at[dp],
            send_sem=w_send.at[step],
            recv_sem=w_recv.at[step],
            device_id=peer(step),
            device_id_type=MESH,
        )

    def prepare_columns():
        length = len_ref[...]
        latitude = (lat_ref[...].astype(f32) + 0.5) * (math.pi / NLAT) - math.pi / 2
        area = jnp.cos(latitude) * (1.0 + land_ref[...].astype(f32))
        q_ref[0] = area * (section < length).astype(f32)
        q_ref[1] = area * (mate < length).astype(f32)
        local_weight = jnp.sum(
            area * jnp.minimum(length, sections).astype(f32), axis=(0, 1), keepdims=True
        )
        misses = jnp.zeros((1, 1), f32)
        if packing:
            beyond = length > 2
            flag = beyond.astype(bf16)
            lane_a = lax.broadcasted_iota(jnp.int32, (LANES, LANES), 0)
            lane_b = lax.broadcasted_iota(jnp.int32, (LANES, LANES), 1)
            within = dot(flag, (lane_a < lane_b).astype(bf16))
            row_total = jnp.sum(flag.astype(f32), axis=1, keepdims=True)
            row_a = lax.broadcasted_iota(jnp.int32, (grid_rows, grid_rows), 0)
            row_b = lax.broadcasted_iota(jnp.int32, (grid_rows, grid_rows), 1)
            before = dot(
                (row_b < row_a).astype(bf16),
                jnp.broadcast_to(row_total, (grid_rows, LANES)).astype(bf16),
            )
            rank = jnp.where(beyond, within + before, -1e6)
            rank_ref[...] = rank
            place = (
                lax.broadcasted_iota(jnp.int32, (grid_rows, LANES), 0) * LANES
                + lax.broadcasted_iota(jnp.int32, (grid_rows, LANES), 1)
            )
            rank_i = rank.astype(jnp.int32)
            missed = beyond & (rank_i >= total_packed - SPARE)
            for j in range(chunks):
                shift = 0 if j < 7 else 256 if j < 11 else 384
                start = min(max(ROWS * (j - 1) + shift, 0), columns - WINDOW)
                member = (rank_i >= j * prows) & (rank_i < (j + 1) * prows)
                ready = ROWS * (j + 2 if j < 7 else j + 3)
                missed |= member & ((place < start) | (place >= min(start + WINDOW, ready)))
            row_chunk = lax.broadcasted_iota(jnp.int32, (grid_rows, LANES), 0) // (ROWS // LANES)
            row_start = expand_start(row_chunk)
            missed |= beyond & ((rank_i < row_start) | (rank_i >= row_start + expand))
            misses = jnp.sum(missed.astype(f32), axis=(0, 1), keepdims=True)
        wbuf[dp] = jnp.where(tile_row < 4, local_weight, misses)
        for step in range(1, groups):
            weight_copy(step).start()

    def finish_weights():
        for step in range(1, groups):
            weight_copy(step).wait_recv()
        total = wbuf[0]
        for other in range(1, groups):
            total = total + wbuf[other]
        weight_ref[...] = total
        miss_ref[...] = (total[4:5, 0:1] > 0.0).astype(jnp.int32)
        scale_ref[...] = 2.0 / jnp.broadcast_to(total[0:1], (8, LANES))

    for fetch in fetches:
        fetch.wait()
    for layer in range(2):
        up_lo[layer] = (0.5 * up_ref[layer]).astype(bf16)
        down_lo[layer] = down_ref[layer].astype(bf16)
    pl.semaphore_wait(barrier, sections - 1 + groups - 1)

    def pack_matrix(j):
        start = window_start(j)
        base = (j * prows).astype(f32)
        target_row = lax.broadcasted_iota(jnp.int32, (prows, LANES), 0).astype(f32)
        first = start // LANES
        hits = []
        for i in range(WINDOW // LANES):
            hits.append(target_row == rank_ref[pl.ds(first + i, 1), :] - base)
        return start, first, hits

    def as_onehot(hits):
        return jnp.concatenate([jnp.where(hit, 1.0, 0.0).astype(bf16) for hit in hits], axis=1)

    def unpack_rows(k):
        start = expand_start(k)
        base = start.astype(f32)
        source_row = lax.broadcasted_iota(jnp.int32, (expand, LANES), 0).astype(f32)
        hits = []
        for i in range(ROWS // LANES):
            hits.append(source_row == rank_ref[pl.ds(k * (ROWS // LANES) + i, 1), :] - base)
        return dot_lhs_t(as_onehot(hits), cin[rows_at(start, expand), :].astype(bf16))

    def forward(source, place, owner, saved, keep):
        x = source[...]
        for layer in range(2):
            if layer == 1:
                keep[...] = x
            r = lax.rsqrt(jnp.mean(x * x, -1, keepdims=True) + norm_eps)
            normed = (x * r * gain_ref[owner, layer : layer + 1]).astype(bf16)
            half = dot(normed, up_lo[2 * owner + layer])
            t = jnp.tanh(half)
            a = 1.0 + t
            h = half * a
            hidden = h.astype(bf16)
            save_h[layer, saved, :] = hidden
            save_d[layer, saved, :] = (a + h * (1.0 - t)).astype(bf16)
            x = x + dot(hidden, down_lo[2 * owner + layer])
        place[...] = x

    def loss_part(size, diff, weight):
        weighted = jnp.concatenate(
            [diff[:, :LANES] * weight, diff[:, LANES:] * weight], axis=1
        )
        loss_acc[...] += jnp.sum((weighted * diff).reshape(size // 8, 8, feats), 0)
        return weighted * scale_ref[0:1, 0:1]

    def backward(size, source, place, owner, saved, keep, g):
        for layer in (1, 0):
            low = g.astype(bf16)
            acc[4 * owner + 2 + layer] += dot_lhs_t(save_h[layer, saved, :], low)
            pull = dot(low, down_t[2 * owner + layer])
            g_pre = (pull * save_d[layer, saved, :].astype(f32)).astype(bf16)
            x = keep[...] if layer == 1 else source[...]
            r = lax.rsqrt(jnp.mean(x * x, -1, keepdims=True) + norm_eps)
            gain = gain_ref[owner, layer : layer + 1]
            xr = x * r
            normed = (xr * gain).astype(bf16)
            acc[4 * owner + layer] += dot_lhs_t(normed, g_pre)
            g_normed = dot(g_pre, up_t[2 * owner + layer])
            prod = g_normed * xr
            gain_acc[2 * owner + layer] += jnp.sum(prod.reshape(size // 8, 8, feats), 0)
            mean = jnp.mean(prod * gain, -1, keepdims=True)
            g = g + r * (gain * g_normed - xr * mean)
        place[...] = g

    def state_copy(source, size, i, to, count=None):
        rows = rows_at(i * size, size if count is None else count)
        return pltpu.make_async_remote_copy(
            src_ref=source.at[rows],
            dst_ref=xin.at[rows],
            send_sem=st_send.at[i],
            recv_sem=st_recv.at[i],
            device_id=(to, dp),
            device_id_type=MESH,
        )

    def cot_copy(size, i, to, count=None):
        rows = rows_at(i * size, size if count is None else count)
        return pltpu.make_async_remote_copy(
            src_ref=xin.at[rows],
            dst_ref=cin.at[rows],
            send_sem=ct_send.at[i],
            recv_sem=ct_recv.at[i],
            device_id=(to, dp),
            device_id_type=MESH,
        )

    up_one = lax.rem(section + 1, sections)
    down_one = lax.rem(section + sections - 1, sections)
    up_chip = lax.rem(section + 2, sections)
    down_chip = jnp.where(section < 4, 1, section - 2)

    def shorter(copy, size, i, action):
        @pl.when(i < chunks - 1)
        def _():
            action(copy(size, i, size))

        @pl.when(i == chunks - 1)
        def _():
            action(copy(size, i, size - SPARE))

    def packed_state(size, i, count):
        return pltpu.make_async_remote_copy(
            src_ref=packed.at[slot_rows(i, count)],
            dst_ref=xin.at[rows_at(i * size, count)],
            send_sem=st_send.at[i],
            recv_sem=st_recv.at[i],
            device_id=(2 + lax.rem(i, 2), dp),
            device_id_type=MESH,
        )

    def packed_receive(size, i):
        @pl.when(section < 4)
        def _():
            shorter(packed_state, size, i, lambda copy: copy.wait_recv())

        @pl.when(section >= 4)
        def _():
            state_copy(xout, size, i, up_chip).wait_recv()

    def cot_part(size, i, count):
        return cot_copy(size, i, down_chip, count)

    def cot_wait(size, i):
        shorter(cot_part, size, i, lambda copy: copy.wait_recv())

    def cot_do(size, i, action):
        @pl.when(section < 4)
        def _():
            shorter(cot_part, size, i, action)

        @pl.when(section >= 4)
        def _():
            action(cot_copy(size, i, down_chip))

    @pl.when(natural)
    def _():
        if packing:
            most = chunks if ring == chunks else ring - 1
            lag = jnp.where(section == 0, most, most - 2)
        else:
            lag = jnp.minimum(ring - 1, 3 * (last - section))

        @pl.when(section > 0)
        def _():
            prepare_columns()
            if packing:
                xout[2 * ROWS : WINDOW, :] = jnp.zeros((WINDOW - 2 * ROWS, feats), f32)
                cin[total_packed - SPARE : total_packed, :] = jnp.zeros((SPARE, feats), f32)

        @pl.loop(0, chunks + lag)
        def _(t):
            @pl.when(t < chunks)
            def _():
                @pl.when(section == 0)
                def _():
                    input_copy(t).wait()

                    @pl.when(t + NEAR < chunks)
                    def _():
                        input_copy(t + NEAR).start()

                @pl.when(section > 0)
                def _():
                    state_copy(xout, ROWS, t, up_one).wait_recv()

                rows = rows_at(t * ROWS, ROWS)
                saved = rows_at(lax.rem(t, ring) * ROWS, ROWS)
                forward(xin.at[rows], xout.at[rows], 0, saved, tgt.at[saved])

                @pl.when(plain_next)
                def _():
                    state_copy(xout, ROWS, t, up_one).start()

            if packing:

                j = jnp.where(t < 8, t - 1, t - 2)

                @pl.when(packs & (t >= 1) & (t != 8) & (j < chunks))
                def _():
                    start, _, hits = pack_matrix(j)

                    @pl.when(j >= SLOTS)
                    def _():
                        shorter(packed_state, prows, j - SLOTS, lambda copy: copy.wait_send())

                    packed[slot_rows(j, prows), :] = split_dot(
                        dot, as_onehot(hits), xout[rows_at(start, WINDOW), :]
                    )
                    shorter(packed_state, prows, j, lambda copy: copy.start())

            @pl.when((section == 0) & (t == 3))
            def _():
                prepare_columns()

            @pl.when(t == jnp.minimum(lag, 4))
            def _():
                prepare_backward()

            k = t - lag

            @pl.when((k >= 0) & (k < chunks))
            def _():
                @pl.when(k == 0)
                def _():
                    finish_weights()

                near_copy(k).wait()
                rows = rows_at(k * ROWS, ROWS)
                place = rows_at(lax.rem(k, NEAR) * ROWS, ROWS)
                saved = rows_at(lax.rem(k, ring) * ROWS, ROWS)

                weight = jnp.concatenate(
                    [
                        jnp.broadcast_to(
                            q_ref[0, pl.ds(k * (ROWS // LANES) + i, 1), :], (LANES, LANES)
                        ).T
                        for i in range(ROWS // LANES)
                    ],
                    axis=0,
                )
                diff = xout[rows, :] - near[place, :]
                spread[...] = loss_part(ROWS, diff, weight)

                @pl.when(k + NEAR < chunks)
                def _():
                    near_copy(k + NEAR).start()

                @pl.when(plain_next)
                def _():
                    cot_copy(ROWS, k, down_one).wait_recv()
                    spread[...] += cin[rows, :]

                if packing:

                    @pl.when(packs)
                    def _():
                        had = jnp.where(k == 0, -1, chunks_for(jnp.maximum(k - 1, 0)))
                        for i in range(3):

                            @pl.when(had + 1 + i <= chunks_for(k))
                            def _():
                                cot_wait(prows, had + 1 + i)

                        spread[...] += unpack_rows(k)

                backward(ROWS, xin.at[rows], xin.at[rows], 0, saved, tgt.at[saved], spread[...])

                @pl.when(section > 0)
                def _():
                    cot_copy(ROWS, k, down_one).start()

        @pl.loop(0, chunks)
        def _(i):
            @pl.when(plain_next)
            def _():
                state_copy(xout, ROWS, i, up_one).wait_send()

            if packing:

                @pl.when(packs & (i + SLOTS >= chunks))
                def _():
                    shorter(packed_state, prows, i, lambda copy: copy.wait_send())

            @pl.when(section > 0)
            def _():
                cot_copy(ROWS, i, down_one).wait_send()

    if packing:

        @pl.when(jnp.logical_not(natural))
        def _():
            turns = chunks // 2
            final_chip = section >= sections - 2
            lag = jnp.where(final_chip, 0, 1)
            for i in range(5):
                mate_weight(i).start()
            prepare_columns()
            for i in range(5):
                mate_weight(i).wait_send()
            prepare_backward()
            prepare_mate()

            @pl.when(section < 4)
            def _():
                xin[total_packed - SPARE : total_packed, :] = jnp.zeros((SPARE, feats), f32)

            def pack_target(j):
                start, first, hits = pack_matrix(j)
                packed[slot_rows(j, prows), :] = split_dot(
                    dot, as_onehot(hits), tgt[rows_at(start, WINDOW), :]
                )
                return first, hits

            def places(turn):
                j = 2 * turn + core
                slot = 2 * lax.rem(turn, 2)
                rows, other = rows_at(j * prows, prows), rows_at(swapped(j) * prows, prows)
                saved = [rows_at((slot + part) * ROWS, prows) for part in range(2)]
                keep = [near.at[rows_at((slot + part) * prows, prows)] for part in range(2)]
                return j, slot, rows, other, saved, keep

            @pl.loop(0, turns + lag)
            def _(turn):
                @pl.when(turn < turns)
                def _():
                    @pl.when(turn == 0)
                    def _():
                        target_copy(0).wait()
                        target_copy(1).wait()

                    for i in range(2, 4):

                        @pl.when(2 * turn + i < chunks)
                        def _():
                            target_copy(2 * turn + i).wait()

                    j, slot, rows, other, saved, keep = places(turn)

                    @pl.when(swapped(j) >= SLOTS)
                    def _():
                        pair_copy(swapped(j) - SLOTS).wait_send()

                    pack_target(swapped(j))
                    pair_copy(swapped(j)).start()
                    first, hits = pack_target(j)
                    for part in range(2):
                        owner = jnp.where(core == part, 0, 1)
                        weight = jnp.zeros((prows, LANES), f32)
                        for i, hit in enumerate(hits):
                            weight += jnp.where(hit, q_ref[owner, pl.ds(first + i, 1), :], 0.0)
                        qring[slot + part] = jnp.broadcast_to(
                            jnp.sum(weight, -1, keepdims=True), (prows, LANES)
                        )
                    packed_receive(prows, j)
                    forward(xin.at[rows], xout.at[other], core, saved[0], keep[0])
                    forward(xout.at[other], xout.at[rows], 1 - core, saved[1], keep[1])

                    @pl.when(jnp.logical_not(final_chip))
                    def _():
                        state_copy(xout, prows, j, up_chip).start()

                @pl.when(turn >= lag)
                def _():
                    @pl.when(turn == lag)
                    def _():
                        finish_weights()

                    j, slot, rows, other, saved, keep = places(turn - lag)
                    part_rows = pl.ds(0, prows)
                    pair_copy(j).wait_recv()

                    def error(part, out):
                        here = core == part
                        target = jnp.where(here, packed[slot_rows(j, prows), :], cin[other, :])
                        return loss_part(prows, out - target, qring[slot + part])

                    spread[part_rows, :] = error(1, xout[rows, :])

                    @pl.when(jnp.logical_not(final_chip))
                    def _():
                        cot_copy(prows, j, down_chip).wait_recv()
                        spread[part_rows, :] += cin[rows, :]

                    backward(
                        prows,
                        xout.at[other],
                        spread.at[part_rows],
                        1 - core,
                        saved[1],
                        keep[1],
                        spread[part_rows, :],
                    )
                    g = error(0, xout[other, :]) + spread[part_rows, :]
                    backward(prows, xin.at[rows], xin.at[rows], core, saved[0], keep[0], g)
                    cot_do(prows, j, lambda copy: copy.start())

            @pl.loop(0, turns)
            def _(turn):
                j = 2 * turn + core
                cot_do(prows, j, lambda copy: copy.wait_send())

                @pl.when(swapped(j) + SLOTS >= chunks)
                def _():
                    pair_copy(swapped(j)).wait_send()

                @pl.when(jnp.logical_not(final_chip))
                def _():
                    state_copy(xout, prows, j, up_chip).wait_send()

            for i in range(5):
                mate_gradient(i).start()
            for i in range(5):
                mate_gradient(i).wait_recv()
                if i < 4:
                    acc[i] += xin[columns - (4 - i) * feats : columns - (3 - i) * feats, :]
                else:
                    gain_acc[0:2] += gain_land[...]
            for i in range(5):
                mate_gradient(i).wait_send()

    bits = groups.bit_length() - 1
    halves = feats // PIECE
    pieces = range(4 * halves)
    matrix = [m for m in (3, 1, 2, 0) for _ in range(halves)]
    first = [PIECE * (p % halves) for p in pieces]

    def bit_order(p):
        order = list(range(bits))
        if p % 2 == 0:
            order.insert(0, order.pop(min(2 - p % 4 // 2, bits - 1)))
        return order

    def bit_value(bit):
        return lax.rem(dp // 2**bit, 2)

    def kept_start(p, step):
        start = 0
        for i in range(step):
            start = start + bit_value(bit_order(p)[i]) * (PIECE >> (i + 1))
        return start

    def across(p, step):
        bit = bit_order(p)[step]
        return (section, dp + (1 - 2 * bit_value(bit)) * 2**bit)

    def reduce_copy(p, step):
        size = PIECE >> (step + 1)
        away = 1 - bit_value(bit_order(p)[step])
        start = kept_start(p, step) + away * size
        if step == 0:
            source = acc.at[matrix[p], rows_at(first[p] + start, size, 8)]
        else:
            source = near.at[rows_at(p * PIECE + start, size, 8)]
        return pltpu.make_async_remote_copy(
            src_ref=source,
            dst_ref=land.at[p, pl.ds(PIECE - (PIECE >> step), size)],
            send_sem=rs_send.at[p * bits + step],
            recv_sem=rs_recv.at[p * bits + step],
            device_id=across(p, step),
            device_id_type=MESH,
        )

    def reduce_add(p, step):
        size = PIECE >> (step + 1)
        start = kept_start(p, step + 1)
        if step == 0:
            own = acc[matrix[p], rows_at(first[p] + start, size, 8), :]
        else:
            own = near[rows_at(p * PIECE + start, size, 8), :]
        own = own + land[p, PIECE - (PIECE >> step) : PIECE - (PIECE >> (step + 1)), :]
        if step == bits - 1:
            final[matrix[p], rows_at(first[p] + start, size, 8), :] = own
        else:
            near[rows_at(p * PIECE + start, size, 8), :] = own
        return own

    def gather_copy(p, step):
        rows = rows_at(first[p] + kept_start(p, step + 1), PIECE >> (step + 1), 8)
        return pltpu.make_async_remote_copy(
            src_ref=final.at[matrix[p], rows],
            dst_ref=final.at[matrix[p], rows],
            send_sem=ag_send.at[p * bits + step],
            recv_sem=ag_recv.at[p * bits + step],
            device_id=across(p, step),
            device_id_type=MESH,
        )

    def small_copy(step):
        return pltpu.make_async_remote_copy(
            src_ref=small.at[dp],
            dst_ref=small.at[dp],
            send_sem=small_send.at[step],
            recv_sem=small_recv.at[step],
            device_id=peer(step),
            device_id_type=MESH,
        )

    def tiny_copy(step):
        return pltpu.make_async_remote_copy(
            src_ref=tiny.at[section],
            dst_ref=tiny.at[section],
            send_sem=tiny_send.at[step],
            recv_sem=tiny_recv.at[step],
            device_id=(lax.rem(section + step, sections), dp),
            device_id_type=MESH,
        )

    def out_copy(p):
        rows = pl.ds(first[p], PIECE)
        return pltpu.make_async_copy(
            final.at[matrix[p], rows], grads_ref.at[matrix[p], rows], out_sem.at[p]
        )

    for p in pieces:
        reduce_copy(p, 0).start()
    squares = jnp.zeros((1, 1), f32)
    for step in range(bits):
        for p in pieces:
            reduce_copy(p, step).wait_recv()
            own = reduce_add(p, step)
            if step < bits - 1:
                reduce_copy(p, step + 1).start()
            else:
                gather_copy(p, step).start()
                squares = squares + jnp.sum(own * own, axis=(0, 1), keepdims=True)
    loss = jnp.sum(loss_acc[...], axis=(0, 1), keepdims=True)
    wide_row = lax.broadcasted_iota(jnp.int32, (8, feats), 0)
    small[dp] = jnp.where(
        wide_row == 0,
        jnp.sum(gain_acc[0], 0, keepdims=True),
        jnp.where(
            wide_row == 1,
            jnp.sum(gain_acc[1], 0, keepdims=True),
            jnp.where(wide_row < 4, loss, squares),
        ),
    )
    for step in range(1, groups):
        small_copy(step).start()
    for step in range(bits - 1, 0, -1):
        for p in pieces:
            gather_copy(p, step).wait_recv()
            gather_copy(p, step - 1).start()
    for step in range(1, groups):
        small_copy(step).wait_recv()
    total = small[0]
    for other in range(1, groups):
        total = total + small[other]
    gain_squares = jnp.sum(total[0:2] * total[0:2], axis=(0, 1), keepdims=True)
    tiny[section] = jnp.where(tile_row < 4, total[2:3, 0:1], total[4:5, 0:1] + gain_squares)
    for step in range(1, sections):
        tiny_copy(step).start()
    for p in pieces:
        gather_copy(p, 0).wait_recv()
        out_copy(p).start()
    for step in range(1, sections):
        tiny_copy(step).wait_recv()
    whole = tiny[0]
    for other in range(1, sections):
        whole = whole + tiny[other]
    norm = jnp.sqrt(whole[4:5, 0:1])
    clip = jnp.minimum(1.0, clip_limit / norm)
    stats = total
    for row, number in ((2, clip), (3, whole[0:1, 0:1]), (4, weight_ref[0:1, 0:1]), (5, norm)):
        stats = jnp.where(wide_row == row, number, stats)
    stat_ref[...] = stats

    for step in range(1, groups):
        weight_copy(step).wait_send()
        small_copy(step).wait_send()
    for step in range(1, sections):
        tiny_copy(step).wait_send()
    for p in pieces:
        out_copy(p).wait()
        for step in range(bits):
            reduce_copy(p, step).wait_send()
            gather_copy(p, step).wait_send()


def rollout(packing, sections, groups, inputs, target, lengths, lat_index, land, w_up, w_down, gains):
    columns, feats = inputs.shape
    chunks = columns // ROWS
    prows = ROWS * (sections - 2) // sections + 16
    grid_rows = columns // LANES
    packed_bytes = 4 * SLOTS * prows * feats
    ring = min((SAVE_BYTES - packed_bytes) // (8 * ROWS * feats), chunks)
    bits = groups.bit_length() - 1
    pieces = 4 * feats // PIECE
    hbm = pl.BlockSpec(memory_space=pl.ANY)
    vmem = pl.BlockSpec(memory_space=pltpu.VMEM)
    dma = pltpu.SemaphoreType.DMA
    wide = pltpu.VMEM((columns, feats), f32)
    lows = pltpu.VMEM((4, feats, feats), bf16)
    flat = lambda array: array.reshape(grid_rows, LANES)
    return pl.pallas_call(
        functools.partial(rollout_kernel, sections, groups, packing),
        out_shape=(
            jax.ShapeDtypeStruct((4, feats, feats), f32),
            jax.ShapeDtypeStruct((8, feats), f32),
            jax.ShapeDtypeStruct((1, 1), jnp.int32),
        ),
        in_specs=[hbm] * 8,
        out_specs=(hbm, vmem, vmem),
        scratch_shapes=[
            wide,
            wide,
            wide,
            wide,
            pltpu.VMEM((SLOTS * prows if packing else 8, feats), f32),
            pltpu.VMEM((max(NEAR * ROWS, 4 * prows), feats), f32),
            pltpu.VMEM((2, ring * ROWS, feats), bf16),
            pltpu.VMEM((2, ring * ROWS, feats), bf16),
            pltpu.VMEM((sections, prows, LANES), f32),
            lows,
            lows,
            lows,
            lows,
            pltpu.VMEM((grid_rows, LANES), f32),
            pltpu.VMEM((2, grid_rows, LANES), f32),
            pltpu.VMEM((8, LANES), f32),
            pltpu.VMEM((8, LANES), f32),
            pltpu.VMEM((8, feats), f32),
            pltpu.VMEM((4, 8, feats), f32),
            pltpu.VMEM((groups, 8, LANES), f32),
            pltpu.VMEM((ROWS, feats), f32),
            pltpu.VMEM((grid_rows, LANES), jnp.int32),
            pltpu.VMEM((grid_rows, LANES), jnp.int32),
            pltpu.VMEM((grid_rows, LANES), jnp.int32),
            pltpu.VMEM((2, 2, feats), f32),
            pltpu.VMEM((8, feats, feats), f32),
            pltpu.VMEM((2, 8, feats), f32),
            pltpu.VMEM((pieces, PIECE, feats), f32),
            pltpu.VMEM((groups, 8, feats), f32),
            pltpu.VMEM((sections, 8, LANES), f32),
            dma((chunks,)),
            dma((chunks,)),
            dma((chunks,)),
            dma((chunks,)),
            dma((chunks,)),
            dma((chunks,)),
            dma((groups,)),
            dma((groups,)),
            dma((pieces * bits,)),
            dma((pieces * bits,)),
            dma((pieces * bits,)),
            dma((pieces * bits,)),
            dma((groups,)),
            dma((groups,)),
            dma((sections,)),
            dma((sections,)),
            dma((pieces,)),
            dma((6,)),
            dma((10,)),
            dma((10,)),
            dma((chunks,)),
            dma((chunks,)),
        ],
        compiler_params=pltpu.CompilerParams(
            collective_id=0 if packing else 1,
            has_side_effects=True,
            vmem_limit_bytes=63 * 1024 * 1024,
        ),
        name="rollout_packed" if packing else "rollout_all",
    )(
        inputs,
        target,
        flat(lengths),
        flat(lat_index),
        flat(land),
        w_up,
        w_down,
        gains,
    )


def adam_step(weights_old, gradient, moment_one, moment_two, decay_rate):
    moment_one = beta_one * moment_one + (1.0 - beta_one) * gradient
    moment_two = beta_two * moment_two + (1.0 - beta_two) * gradient * gradient
    second_hat = moment_two * (1.0 / (1.0 - beta_two**STEP))
    root = second_hat * lax.rsqrt(second_hat)
    pace = moment_one * (learn_rate / (1.0 - beta_one**STEP))
    step = pace * pl.reciprocal(root + adam_eps)
    new_weights = weights_old * (1.0 - learn_rate * decay_rate) - step
    return (new_weights, moment_one, moment_two)


def update_kernel(
    grads_ref,
    stat_hbm,
    w_up,
    w_down,
    gains,
    m_up,
    m_down,
    m_gains,
    v_up,
    v_down,
    v_gains,
    loss_out,
    total_out,
    norm_out,
    new_up,
    new_down,
    new_gains,
    new_m_up,
    new_m_down,
    new_m_gains,
    new_v_up,
    new_v_down,
    new_v_gains,
    held,
    stat_ref,
    gain_ref,
    in_sem,
    out_sem,
    small_in,
    small_out,
):
    old = ((grads_ref, grads_ref), (w_up, w_down), (m_up, m_down), (v_up, v_down))
    new = ((new_up, new_down), (new_m_up, new_m_down), (new_v_up, new_v_down))

    def fetch(i, part):
        source = old[part][i // 2].at[i if part == 0 else i % 2]
        return pltpu.make_async_copy(source, held.at[part, i], in_sem.at[part, i])

    def store(i, part):
        return pltpu.make_async_copy(
            held.at[part + 1, i], new[part][i // 2].at[i % 2], out_sem.at[part, i]
        )

    small_fetch = [pltpu.make_async_copy(stat_hbm, stat_ref, small_in.at[3])]
    small_store = []
    for part, (source, out) in enumerate(
        ((gains, new_gains), (m_gains, new_m_gains), (v_gains, new_v_gains))
    ):
        small_fetch.append(pltpu.make_async_copy(source, gain_ref.at[part], small_in.at[part]))
        small_store.append(pltpu.make_async_copy(gain_ref.at[part], out, small_out.at[part]))
    for copy in small_fetch:
        copy.start()
    for i in range(4):
        for part in range(4):
            fetch(i, part).start()
    for copy in small_fetch:
        copy.wait()
    clip = stat_ref[2:3, 0:1]
    for row, out in ((3, loss_out), (4, total_out), (5, norm_out)):
        out[...] = stat_ref[row : row + 1, 0:1]
    fresh = adam_step(gain_ref[0], stat_ref[0:2] * clip, gain_ref[1], gain_ref[2], 0.0)
    for part in range(3):
        gain_ref[part] = fresh[part]
        small_store[part].start()
    for i in range(4):
        for part in range(4):
            fetch(i, part).wait()
        fresh = adam_step(held[1, i], held[0, i] * clip, held[2, i], held[3, i], weight_decay)
        for part in range(3):
            held[part + 1, i] = fresh[part]
            store(i, part).start()
    for i in range(4):
        for part in range(3):
            store(i, part).wait()
    for copy in small_store:
        copy.wait()


def update(grads, stats, *state):
    hbm = pl.BlockSpec(memory_space=pl.ANY)
    vmem = pl.BlockSpec(memory_space=pltpu.VMEM)
    return pl.pallas_call(
        update_kernel,
        in_specs=[hbm] * 11,
        out_specs=(vmem,) * 3 + (hbm,) * 9,
        out_shape=(jax.ShapeDtypeStruct((1, 1), f32),) * 3
        + tuple(jax.ShapeDtypeStruct(a.shape, f32) for a in state),
        scratch_shapes=[
            pltpu.VMEM((4,) + grads.shape, f32),
            pltpu.VMEM(stats.shape, f32),
            pltpu.VMEM((3,) + state[2].shape, f32),
            pltpu.SemaphoreType.DMA((4, 4)),
            pltpu.SemaphoreType.DMA((3, 4)),
            pltpu.SemaphoreType.DMA((4,)),
            pltpu.SemaphoreType.DMA((3,)),
        ],
        compiler_params=pltpu.CompilerParams(vmem_limit_bytes=63 * 1024 * 1024),
        name="update",
    )(grads, stats, *state)


def per_device(
    inputs,
    targets,
    lengths,
    lat_index,
    land,
    w_up,
    w_down,
    gains,
    m_up,
    m_down,
    m_gains,
    v_up,
    v_down,
    v_gains,
):
    sections, groups = lax.axis_size("section"), lax.axis_size("dp")
    state = tuple(
        a[0] for a in (w_up, w_down, gains, m_up, m_down, m_gains, v_up, v_down, v_gains)
    )
    operands = (inputs, targets[0], lengths, lat_index, land) + state[:3]
    packed = rollout(True, sections, groups, *operands)

    grads, stats, unused = lax.cond(
        packed[2].reshape(()) > 0,
        lambda: rollout(False, sections, groups, *operands),
        lambda: packed,
    )
    new = update(grads, stats, *state)
    return tuple(a.reshape(()) for a in new[:3]) + tuple(a[None] for a in new[3:])


def solution(mesh):
    return jax.shard_map(
        per_device,
        mesh=mesh,
        in_specs=(
            P("dp", None),
            P("section", "dp", None),
            P("dp"),
            P("dp"),
            P("dp"),
            P("section", None, None, None),
            P("section", None, None, None),
            P("section", None, None),
            P("section", None, None, None),
            P("section", None, None, None),
            P("section", None, None),
            P("section", None, None, None),
            P("section", None, None, None),
            P("section", None, None),
        ),
        out_specs=(
            P(),
            P(),
            P(),
            P("section", None, None, None),
            P("section", None, None, None),
            P("section", None, None),
            P("section", None, None, None),
            P("section", None, None, None),
            P("section", None, None),
            P("section", None, None, None),
            P("section", None, None, None),
            P("section", None, None),
        ),
        check_vma=False,
    )
```

```python
import functools
import math

import jax
import jax.numpy as jnp
from jax import lax
from jax.experimental import pallas as pl
from jax.experimental.pallas import tpu as pltpu
from jax.sharding import PartitionSpec as P

NLAT = 128
STEP = 10

norm_eps = 1e-06
clip_limit = 0.05
beta_one = 0.9
beta_two = 0.999
adam_eps = 1e-08
learn_rate = 0.1
weight_decay = 0.01

f32, bf16 = jnp.float32, jnp.bfloat16
MESH = pl.DeviceIdType.MESH
LANES = 128
PIECE = 128
ROWS = 512
SPARE = 80
WINDOW = 1536
SAVE_BYTES = 17 * 1024 * 1024
SLOTS = 10
NEAR = 3


def dot(a, b):
    return jnp.dot(a, b, preferred_element_type=f32)


def dot_lhs_t(a, b):
    return lax.dot_general(a, b, (((0,), (0,)), ((), ())), preferred_element_type=f32)


def split_dot(product, onehot, values):
    high = values.astype(bf16)
    low = (values - high.astype(f32)).astype(bf16)
    return product(onehot, high) + product(onehot, low)


def rollout_kernel(
    sections,
    groups,
    packing,
    inputs_ref,
    target_ref,
    len_hbm,
    lat_hbm,
    land_hbm,
    up_hbm,
    down_hbm,
    gain_hbm,
    grads_ref,
    stat_ref,
    miss_ref,
    xin,
    xout,
    cin,
    tgt,
    packed,
    near,
    save_h,
    save_d,
    qring,
    up_lo,
    up_t,
    down_lo,
    down_t,
    rank_ref,
    q_ref,
    scale_ref,
    weight_ref,
    loss_acc,
    gain_acc,
    wbuf,
    spread,
    len_ref,
    lat_ref,
    land_ref,
    gain_ref,
    acc,
    gain_land,
    land,
    small,
    tiny,
    in_sem,
    tgt_sem,
    st_send,
    st_recv,
    ct_send,
    ct_recv,
    w_send,
    w_recv,
    rs_send,
    rs_recv,
    ag_send,
    ag_recv,
    small_send,
    small_recv,
    tiny_send,
    tiny_recv,
    out_sem,
    weight_sem,
    mate_send,
    mate_recv,
    pair_send,
    pair_recv,
):
    section = lax.axis_index("section")
    dp = lax.axis_index("dp")
    columns = xin.shape[0]
    feats = xin.shape[1]
    chunks = columns // ROWS
    live_rows = ROWS * (sections - 2) // sections
    prows = live_rows + 16
    total_packed = chunks * prows
    expand = live_rows + 512
    last = sections - 1
    core = lax.rem(section, 2)
    mate = section + 1 - 2 * core
    final = acc.at[pl.ds(4, 4)]
    up_ref, down_ref = acc.at[pl.ds(0, 2)], acc.at[pl.ds(2, 2)]
    ring = save_h.shape[1] // ROWS
    natural = section < (2 if packing else sections)
    plain_next = (section == 0) if packing else (section < last)
    packs = (section == 1) if packing else (section < 0)

    def peer(step):
        return (section, lax.rem(dp + step, groups))

    sources = (up_hbm, down_hbm, gain_hbm, len_hbm, lat_hbm, land_hbm)
    places = (up_ref, down_ref, gain_ref.at[0], len_ref, lat_ref, land_ref)
    fetches = [
        pltpu.make_async_copy(source, place, weight_sem.at[i])
        for i, (source, place) in enumerate(zip(sources, places))
    ]
    for fetch in fetches:
        fetch.start()

    barrier = pltpu.get_barrier_semaphore()
    for step in range(1, sections):
        other = lax.rem(section + step, sections)
        pl.semaphore_signal(barrier, inc=1, device_id=(other, dp), device_id_type=MESH)
    for step in range(1, groups):
        pl.semaphore_signal(barrier, inc=1, device_id=peer(step), device_id_type=MESH)

    def rows_at(index, size, align=16):
        return pl.ds(pl.multiple_of(index, align), size)

    def input_copy(i):
        rows = rows_at(i * ROWS, ROWS)
        return pltpu.make_async_copy(inputs_ref.at[rows], xin.at[rows], in_sem.at[i])

    def target_copy(i):
        rows = rows_at(i * ROWS, ROWS)
        return pltpu.make_async_copy(target_ref.at[rows], tgt.at[rows], tgt_sem.at[i])

    def near_copy(i):
        place = rows_at(lax.rem(i, NEAR) * ROWS, ROWS)
        return pltpu.make_async_copy(
            target_ref.at[rows_at(i * ROWS, ROWS)], near.at[place], tgt_sem.at[i]
        )

    @pl.when(section == 0)
    def _():
        @pl.loop(0, NEAR)
        def _(i):
            input_copy(i).start()

    @pl.when(natural)
    def _():
        @pl.loop(0, NEAR)
        def _(i):
            near_copy(i).start()

    @pl.when(jnp.logical_not(natural))
    def _():
        @pl.loop(0, chunks)
        def _(i):
            target_copy(i).start()

    def prepare_backward():
        for layer in range(2):
            up_t[layer] = up_ref[layer].T.astype(bf16)
            down_t[layer] = (0.5 * down_ref[layer]).T.astype(bf16)
        gain_acc[...] = jnp.zeros_like(gain_acc)
        loss_acc[...] = jnp.zeros_like(loss_acc)
        for i in range(4):
            acc[i] = jnp.zeros((feats, feats), f32)

    def mate_weight(i):
        source = gain_ref.at[0] if i == 4 else acc.at[i]
        place = gain_ref.at[1] if i == 4 else acc.at[4 + i]
        return pltpu.make_async_remote_copy(
            src_ref=source,
            dst_ref=place,
            send_sem=mate_send.at[i],
            recv_sem=mate_recv.at[i],
            device_id=(mate, dp),
            device_id_type=MESH,
        )

    def prepare_mate():
        for i in range(5):
            mate_weight(i).wait_recv()
        for layer in range(2):
            up = acc[4 + layer]
            down = acc[6 + layer]
            up_lo[2 + layer] = (0.5 * up).astype(bf16)
            down_lo[2 + layer] = down.astype(bf16)
            up_t[2 + layer] = up.T.astype(bf16)
            down_t[2 + layer] = (0.5 * down).T.astype(bf16)
        for i in range(4, 8):
            acc[i] = jnp.zeros((feats, feats), f32)

    def mate_gradient(i):
        if i < 4:
            source = acc.at[4 + i]
            place = xin.at[pl.ds(columns - (4 - i) * feats, feats)]
        else:
            source, place = gain_acc.at[pl.ds(2, 2)], gain_land
        return pltpu.make_async_remote_copy(
            src_ref=source,
            dst_ref=place,
            send_sem=mate_send.at[5 + i],
            recv_sem=mate_recv.at[5 + i],
            device_id=(mate, dp),
            device_id_type=MESH,
        )

    def pair_copy(j):
        return pltpu.make_async_remote_copy(
            src_ref=packed.at[slot_rows(j, prows)],
            dst_ref=cin.at[rows_at(swapped(j) * prows, prows)],
            send_sem=pair_send.at[j],
            recv_sem=pair_recv.at[j],
            device_id=(mate, dp),
            device_id_type=MESH,
        )

    def slot_rows(j, count):
        return rows_at(lax.rem(j, SLOTS) * prows, count)

    def swapped(j):
        return j + 1 - 2 * lax.rem(j, 2)

    grid_rows = columns // LANES
    tile_row = lax.broadcasted_iota(jnp.int32, (8, LANES), 0)

    def window_start(j):
        shift = jnp.where(j < 7, 0, jnp.where(j < 11, 256, 384))
        return jnp.clip(ROWS * (j - 1) + shift, 0, columns - WINDOW)

    def expand_start(k):
        end = live_rows * k + expand - 288
        end = jnp.where(k >= 11, jnp.minimum(end, prows * (k + 1)), end)
        return jnp.clip(end - expand, 0, total_packed - expand)

    def chunks_for(k):
        return (expand_start(k) + expand - 1) // prows

    def weight_copy(step):
        return pltpu.make_async_remote_copy(
            src_ref=wbuf.at[dp],
            dst_ref=wbuf.at[dp],
            send_sem=w_send.at[step],
            recv_sem=w_recv.at[step],
            device_id=peer(step),
            device_id_type=MESH,
        )

    def prepare_columns():
        length = len_ref[...]
        latitude = (lat_ref[...].astype(f32) + 0.5) * (math.pi / NLAT) - math.pi / 2
        area = jnp.cos(latitude) * (1.0 + land_ref[...].astype(f32))
        q_ref[0] = area * (section < length).astype(f32)
        q_ref[1] = area * (mate < length).astype(f32)
        local_weight = jnp.sum(
            area * jnp.minimum(length, sections).astype(f32), axis=(0, 1), keepdims=True
        )
        misses = jnp.zeros((1, 1), f32)
        if packing:
            beyond = length > 2
            flag = beyond.astype(bf16)
            lane_a = lax.broadcasted_iota(jnp.int32, (LANES, LANES), 0)
            lane_b = lax.broadcasted_iota(jnp.int32, (LANES, LANES), 1)
            within = dot(flag, (lane_a < lane_b).astype(bf16))
            row_total = jnp.sum(flag.astype(f32), axis=1, keepdims=True)
            row_a = lax.broadcasted_iota(jnp.int32, (grid_rows, grid_rows), 0)
            row_b = lax.broadcasted_iota(jnp.int32, (grid_rows, grid_rows), 1)
            before = dot(
                (row_b < row_a).astype(bf16),
                jnp.broadcast_to(row_total, (grid_rows, LANES)).astype(bf16),
            )
            rank = jnp.where(beyond, within + before, -1e6)
            rank_ref[...] = rank
            place = (
                lax.broadcasted_iota(jnp.int32, (grid_rows, LANES), 0) * LANES
                + lax.broadcasted_iota(jnp.int32, (grid_rows, LANES), 1)
            )
            rank_i = rank.astype(jnp.int32)
            missed = beyond & (rank_i >= total_packed - SPARE)
            for j in range(chunks):
                shift = 0 if j < 7 else 256 if j < 11 else 384
                start = min(max(ROWS * (j - 1) + shift, 0), columns - WINDOW)
                member = (rank_i >= j * prows) & (rank_i < (j + 1) * prows)
                ready = ROWS * (j + 2 if j < 7 else j + 3)
                missed |= member & ((place < start) | (place >= min(start + WINDOW, ready)))
            row_chunk = lax.broadcasted_iota(jnp.int32, (grid_rows, LANES), 0) // (ROWS // LANES)
            row_start = expand_start(row_chunk)
            missed |= beyond & ((rank_i < row_start) | (rank_i >= row_start + expand))
            misses = jnp.sum(missed.astype(f32), axis=(0, 1), keepdims=True)
        wbuf[dp] = jnp.where(tile_row < 4, local_weight, misses)
        for step in range(1, groups):
            weight_copy(step).start()

    def finish_weights():
        for step in range(1, groups):
            weight_copy(step).wait_recv()
        total = wbuf[0]
        for other in range(1, groups):
            total = total + wbuf[other]
        weight_ref[...] = total
        miss_ref[...] = (total[4:5, 0:1] > 0.0).astype(jnp.int32)
        scale_ref[...] = 2.0 / jnp.broadcast_to(total[0:1], (8, LANES))

    for fetch in fetches:
        fetch.wait()
    for layer in range(2):
        up_lo[layer] = (0.5 * up_ref[layer]).astype(bf16)
        down_lo[layer] = down_ref[layer].astype(bf16)
    pl.semaphore_wait(barrier, sections - 1 + groups - 1)

    def pack_matrix(j):
        start = window_start(j)
        base = (j * prows).astype(f32)
        target_row = lax.broadcasted_iota(jnp.int32, (prows, LANES), 0).astype(f32)
        first = start // LANES
        hits = []
        for i in range(WINDOW // LANES):
            hits.append(target_row == rank_ref[pl.ds(first + i, 1), :] - base)
        return start, first, hits

    def as_onehot(hits):
        return jnp.concatenate([jnp.where(hit, 1.0, 0.0).astype(bf16) for hit in hits], axis=1)

    def unpack_rows(k):
        start = expand_start(k)
        base = start.astype(f32)
        source_row = lax.broadcasted_iota(jnp.int32, (expand, LANES), 0).astype(f32)
        hits = []
        for i in range(ROWS // LANES):
            hits.append(source_row == rank_ref[pl.ds(k * (ROWS // LANES) + i, 1), :] - base)
        return dot_lhs_t(as_onehot(hits), cin[rows_at(start, expand), :].astype(bf16))

    def forward(source, place, owner, saved, keep):
        x = source[...]
        for layer in range(2):
            if layer == 1:
                keep[...] = x
            r = lax.rsqrt(jnp.mean(x * x, -1, keepdims=True) + norm_eps)
            normed = (x * r * gain_ref[owner, layer : layer + 1]).astype(bf16)
            half = dot(normed, up_lo[2 * owner + layer])
            t = jnp.tanh(half)
            a = 1.0 + t
            h = half * a
            hidden = h.astype(bf16)
            save_h[layer, saved, :] = hidden
            save_d[layer, saved, :] = (a + h * (1.0 - t)).astype(bf16)
            x = x + dot(hidden, down_lo[2 * owner + layer])
        place[...] = x

    def loss_part(size, diff, weight):
        weighted = jnp.concatenate(
            [diff[:, :LANES] * weight, diff[:, LANES:] * weight], axis=1
        )
        loss_acc[...] += jnp.sum((weighted * diff).reshape(size // 8, 8, feats), 0)
        return weighted * scale_ref[0:1, 0:1]

    def backward(size, source, place, owner, saved, keep, g):
        for layer in (1, 0):
            low = g.astype(bf16)
            acc[4 * owner + 2 + layer] += dot_lhs_t(save_h[layer, saved, :], low)
            pull = dot(low, down_t[2 * owner + layer])
            g_pre = (pull * save_d[layer, saved, :].astype(f32)).astype(bf16)
            x = keep[...] if layer == 1 else source[...]
            r = lax.rsqrt(jnp.mean(x * x, -1, keepdims=True) + norm_eps)
            gain = gain_ref[owner, layer : layer + 1]
            xr = x * r
            normed = (xr * gain).astype(bf16)
            acc[4 * owner + layer] += dot_lhs_t(normed, g_pre)
            g_normed = dot(g_pre, up_t[2 * owner + layer])
            prod = g_normed * xr
            gain_acc[2 * owner + layer] += jnp.sum(prod.reshape(size // 8, 8, feats), 0)
            mean = jnp.mean(prod * gain, -1, keepdims=True)
            g = g + r * (gain * g_normed - xr * mean)
        place[...] = g

    def state_copy(source, size, i, to, count=None):
        rows = rows_at(i * size, size if count is None else count)
        return pltpu.make_async_remote_copy(
            src_ref=source.at[rows],
            dst_ref=xin.at[rows],
            send_sem=st_send.at[i],
            recv_sem=st_recv.at[i],
            device_id=(to, dp),
            device_id_type=MESH,
        )

    def cot_copy(size, i, to, count=None):
        rows = rows_at(i * size, size if count is None else count)
        return pltpu.make_async_remote_copy(
            src_ref=xin.at[rows],
            dst_ref=cin.at[rows],
            send_sem=ct_send.at[i],
            recv_sem=ct_recv.at[i],
            device_id=(to, dp),
            device_id_type=MESH,
        )

    up_one = lax.rem(section + 1, sections)
    down_one = lax.rem(section + sections - 1, sections)
    up_chip = lax.rem(section + 2, sections)
    down_chip = jnp.where(section < 4, 1, section - 2)

    def shorter(copy, size, i, action):
        @pl.when(i < chunks - 1)
        def _():
            action(copy(size, i, size))

        @pl.when(i == chunks - 1)
        def _():
            action(copy(size, i, size - SPARE))

    def packed_state(size, i, count):
        return pltpu.make_async_remote_copy(
            src_ref=packed.at[slot_rows(i, count)],
            dst_ref=xin.at[rows_at(i * size, count)],
            send_sem=st_send.at[i],
            recv_sem=st_recv.at[i],
            device_id=(2 + lax.rem(i, 2), dp),
            device_id_type=MESH,
        )

    def packed_receive(size, i):
        @pl.when(section < 4)
        def _():
            shorter(packed_state, size, i, lambda copy: copy.wait_recv())

        @pl.when(section >= 4)
        def _():
            state_copy(xout, size, i, up_chip).wait_recv()

    def cot_part(size, i, count):
        return cot_copy(size, i, down_chip, count)

    def cot_wait(size, i):
        shorter(cot_part, size, i, lambda copy: copy.wait_recv())

    def cot_do(size, i, action):
        @pl.when(section < 4)
        def _():
            shorter(cot_part, size, i, action)

        @pl.when(section >= 4)
        def _():
            action(cot_copy(size, i, down_chip))

    @pl.when(natural)
    def _():
        if packing:
            most = chunks if ring == chunks else ring - 1
            lag = jnp.where(section == 0, most, most - 2)
        else:
            lag = jnp.minimum(ring - 1, 3 * (last - section))

        @pl.when(section > 0)
        def _():
            prepare_columns()
            if packing:
                xout[2 * ROWS : WINDOW, :] = jnp.zeros((WINDOW - 2 * ROWS, feats), f32)
                cin[total_packed - SPARE : total_packed, :] = jnp.zeros((SPARE, feats), f32)

        @pl.loop(0, chunks + lag)
        def _(t):
            @pl.when(t < chunks)
            def _():
                @pl.when(section == 0)
                def _():
                    input_copy(t).wait()

                    @pl.when(t + NEAR < chunks)
                    def _():
                        input_copy(t + NEAR).start()

                @pl.when(section > 0)
                def _():
                    state_copy(xout, ROWS, t, up_one).wait_recv()

                rows = rows_at(t * ROWS, ROWS)
                saved = rows_at(lax.rem(t, ring) * ROWS, ROWS)
                forward(xin.at[rows], xout.at[rows], 0, saved, tgt.at[saved])

                @pl.when(plain_next)
                def _():
                    state_copy(xout, ROWS, t, up_one).start()

            if packing:

                j = jnp.where(t < 8, t - 1, t - 2)

                @pl.when(packs & (t >= 1) & (t != 8) & (j < chunks))
                def _():
                    start, _, hits = pack_matrix(j)

                    @pl.when(j >= SLOTS)
                    def _():
                        shorter(packed_state, prows, j - SLOTS, lambda copy: copy.wait_send())

                    packed[slot_rows(j, prows), :] = split_dot(
                        dot, as_onehot(hits), xout[rows_at(start, WINDOW), :]
                    )
                    shorter(packed_state, prows, j, lambda copy: copy.start())

            @pl.when((section == 0) & (t == 3))
            def _():
                prepare_columns()

            @pl.when(t == jnp.minimum(lag, 4))
            def _():
                prepare_backward()

            k = t - lag

            @pl.when((k >= 0) & (k < chunks))
            def _():
                @pl.when(k == 0)
                def _():
                    finish_weights()

                near_copy(k).wait()
                rows = rows_at(k * ROWS, ROWS)
                place = rows_at(lax.rem(k, NEAR) * ROWS, ROWS)
                saved = rows_at(lax.rem(k, ring) * ROWS, ROWS)

                weight = jnp.concatenate(
                    [
                        jnp.broadcast_to(
                            q_ref[0, pl.ds(k * (ROWS // LANES) + i, 1), :], (LANES, LANES)
                        ).T
                        for i in range(ROWS // LANES)
                    ],
                    axis=0,
                )
                diff = xout[rows, :] - near[place, :]
                spread[...] = loss_part(ROWS, diff, weight)

                @pl.when(k + NEAR < chunks)
                def _():
                    near_copy(k + NEAR).start()

                @pl.when(plain_next)
                def _():
                    cot_copy(ROWS, k, down_one).wait_recv()
                    spread[...] += cin[rows, :]

                if packing:

                    @pl.when(packs)
                    def _():
                        had = jnp.where(k == 0, -1, chunks_for(jnp.maximum(k - 1, 0)))
                        for i in range(3):

                            @pl.when(had + 1 + i <= chunks_for(k))
                            def _():
                                cot_wait(prows, had + 1 + i)

                        spread[...] += unpack_rows(k)

                backward(ROWS, xin.at[rows], xin.at[rows], 0, saved, tgt.at[saved], spread[...])

                @pl.when(section > 0)
                def _():
                    cot_copy(ROWS, k, down_one).start()

    if packing:

        @pl.when(jnp.logical_not(natural))
        def _():
            turns = chunks // 2
            final_chip = section >= sections - 2
            lag = jnp.where(final_chip, 0, 1)
            for i in range(5):
                mate_weight(i).start()
            prepare_columns()
            for i in range(5):
                mate_weight(i).wait_send()
            prepare_backward()
            prepare_mate()

            @pl.when(section < 4)
            def _():
                xin[total_packed - SPARE : total_packed, :] = jnp.zeros((SPARE, feats), f32)

            def pack_target(j):
                start, first, hits = pack_matrix(j)
                packed[slot_rows(j, prows), :] = split_dot(
                    dot, as_onehot(hits), tgt[rows_at(start, WINDOW), :]
                )
                return first, hits

            def places(turn):
                j = 2 * turn + core
                slot = 2 * lax.rem(turn, 2)
                rows, other = rows_at(j * prows, prows), rows_at(swapped(j) * prows, prows)
                saved = [rows_at((slot + part) * ROWS, prows) for part in range(2)]
                keep = [near.at[rows_at((slot + part) * prows, prows)] for part in range(2)]
                return j, slot, rows, other, saved, keep

            @pl.loop(0, turns + lag)
            def _(turn):
                @pl.when(turn < turns)
                def _():
                    @pl.when(turn == 0)
                    def _():
                        target_copy(0).wait()
                        target_copy(1).wait()

                    for i in range(2, 4):

                        @pl.when(2 * turn + i < chunks)
                        def _():
                            target_copy(2 * turn + i).wait()

                    j, slot, rows, other, saved, keep = places(turn)

                    @pl.when(swapped(j) >= SLOTS)
                    def _():
                        pair_copy(swapped(j) - SLOTS).wait_send()

                    pack_target(swapped(j))
                    pair_copy(swapped(j)).start()
                    first, hits = pack_target(j)
                    for part in range(2):
                        owner = jnp.where(core == part, 0, 1)
                        weight = jnp.zeros((prows, LANES), f32)
                        for i, hit in enumerate(hits):
                            weight += jnp.where(hit, q_ref[owner, pl.ds(first + i, 1), :], 0.0)
                        qring[slot + part] = jnp.broadcast_to(
                            jnp.sum(weight, -1, keepdims=True), (prows, LANES)
                        )
                    packed_receive(prows, j)
                    forward(xin.at[rows], xout.at[other], core, saved[0], keep[0])
                    forward(xout.at[other], xout.at[rows], 1 - core, saved[1], keep[1])

                    @pl.when(jnp.logical_not(final_chip))
                    def _():
                        state_copy(xout, prows, j, up_chip).start()

                @pl.when(turn >= lag)
                def _():
                    @pl.when(turn == lag)
                    def _():
                        finish_weights()

                    j, slot, rows, other, saved, keep = places(turn - lag)
                    part_rows = pl.ds(0, prows)
                    pair_copy(j).wait_recv()

                    def error(part, out):
                        here = core == part
                        target = jnp.where(here, packed[slot_rows(j, prows), :], cin[other, :])
                        return loss_part(prows, out - target, qring[slot + part])

                    spread[part_rows, :] = error(1, xout[rows, :])

                    @pl.when(jnp.logical_not(final_chip))
                    def _():
                        cot_copy(prows, j, down_chip).wait_recv()
                        spread[part_rows, :] += cin[rows, :]

                    backward(
                        prows,
                        xout.at[other],
                        spread.at[part_rows],
                        1 - core,
                        saved[1],
                        keep[1],
                        spread[part_rows, :],
                    )
                    g = error(0, xout[other, :]) + spread[part_rows, :]
                    backward(prows, xin.at[rows], xin.at[rows], core, saved[0], keep[0], g)
                    cot_do(prows, j, lambda copy: copy.start())

            for i in range(5):
                mate_gradient(i).start()
            for i in range(5):
                mate_gradient(i).wait_recv()
                if i < 4:
                    acc[i] += xin[columns - (4 - i) * feats : columns - (3 - i) * feats, :]
                else:
                    gain_acc[0:2] += gain_land[...]
            for i in range(5):
                mate_gradient(i).wait_send()

    bits = groups.bit_length() - 1
    halves = feats // PIECE
    pieces = range(4 * halves)
    matrix = [m for m in (3, 1, 2, 0) for _ in range(halves)]
    first = [PIECE * (p % halves) for p in pieces]

    def bit_order(p):
        order = list(range(bits))
        if p % 2 == 0:
            order.insert(0, order.pop(min(2 - p % 4 // 2, bits - 1)))
        return order

    def bit_value(bit):
        return lax.rem(dp // 2**bit, 2)

    def kept_start(p, step):
        start = 0
        for i in range(step):
            start = start + bit_value(bit_order(p)[i]) * (PIECE >> (i + 1))
        return start

    def across(p, step):
        bit = bit_order(p)[step]
        return (section, dp + (1 - 2 * bit_value(bit)) * 2**bit)

    def reduce_copy(p, step):
        size = PIECE >> (step + 1)
        away = 1 - bit_value(bit_order(p)[step])
        start = kept_start(p, step) + away * size
        if step == 0:
            source = acc.at[matrix[p], rows_at(first[p] + start, size, 8)]
        else:
            source = near.at[rows_at(p * PIECE + start, size, 8)]
        return pltpu.make_async_remote_copy(
            src_ref=source,
            dst_ref=land.at[p, pl.ds(PIECE - (PIECE >> step), size)],
            send_sem=rs_send.at[p * bits + step],
            recv_sem=rs_recv.at[p * bits + step],
            device_id=across(p, step),
            device_id_type=MESH,
        )

    def reduce_add(p, step):
        size = PIECE >> (step + 1)
        start = kept_start(p, step + 1)
        if step == 0:
            own = acc[matrix[p], rows_at(first[p] + start, size, 8), :]
        else:
            own = near[rows_at(p * PIECE + start, size, 8), :]
        own = own + land[p, PIECE - (PIECE >> step) : PIECE - (PIECE >> (step + 1)), :]
        if step == bits - 1:
            final[matrix[p], rows_at(first[p] + start, size, 8), :] = own
        else:
            near[rows_at(p * PIECE + start, size, 8), :] = own
        return own

    def gather_copy(p, step):
        rows = rows_at(first[p] + kept_start(p, step + 1), PIECE >> (step + 1), 8)
        return pltpu.make_async_remote_copy(
            src_ref=final.at[matrix[p], rows],
            dst_ref=final.at[matrix[p], rows],
            send_sem=ag_send.at[p * bits + step],
            recv_sem=ag_recv.at[p * bits + step],
            device_id=across(p, step),
            device_id_type=MESH,
        )

    def small_copy(step):
        return pltpu.make_async_remote_copy(
            src_ref=small.at[dp],
            dst_ref=small.at[dp],
            send_sem=small_send.at[step],
            recv_sem=small_recv.at[step],
            device_id=peer(step),
            device_id_type=MESH,
        )

    def tiny_copy(step):
        return pltpu.make_async_remote_copy(
            src_ref=tiny.at[section],
            dst_ref=tiny.at[section],
            send_sem=tiny_send.at[step],
            recv_sem=tiny_recv.at[step],
            device_id=(lax.rem(section + step, sections), dp),
            device_id_type=MESH,
        )

    def out_copy(p):
        rows = pl.ds(first[p], PIECE)
        return pltpu.make_async_copy(
            final.at[matrix[p], rows], grads_ref.at[matrix[p], rows], out_sem.at[p]
        )

    for p in pieces:
        reduce_copy(p, 0).start()
    squares = jnp.zeros((1, 1), f32)
    for step in range(bits):
        for p in pieces:
            reduce_copy(p, step).wait_recv()
            own = reduce_add(p, step)
            if step < bits - 1:
                reduce_copy(p, step + 1).start()
            else:
                gather_copy(p, step).start()
                squares = squares + jnp.sum(own * own, axis=(0, 1), keepdims=True)
    loss = jnp.sum(loss_acc[...], axis=(0, 1), keepdims=True)
    wide_row = lax.broadcasted_iota(jnp.int32, (8, feats), 0)
    small[dp] = jnp.where(
        wide_row == 0,
        jnp.sum(gain_acc[0], 0, keepdims=True),
        jnp.where(
            wide_row == 1,
            jnp.sum(gain_acc[1], 0, keepdims=True),
            jnp.where(wide_row < 4, loss, squares),
        ),
    )
    for step in range(1, groups):
        small_copy(step).start()
    for step in range(bits - 1, 0, -1):
        for p in pieces:
            gather_copy(p, step).wait_recv()
            gather_copy(p, step - 1).start()
    for step in range(1, groups):
        small_copy(step).wait_recv()
    total = small[0]
    for other in range(1, groups):
        total = total + small[other]
    gain_squares = jnp.sum(total[0:2] * total[0:2], axis=(0, 1), keepdims=True)
    tiny[section] = jnp.where(tile_row < 4, total[2:3, 0:1], total[4:5, 0:1] + gain_squares)
    for step in range(1, sections):
        tiny_copy(step).start()
    for p in pieces:
        gather_copy(p, 0).wait_recv()
        out_copy(p).start()
    for step in range(1, sections):
        tiny_copy(step).wait_recv()
    whole = tiny[0]
    for other in range(1, sections):
        whole = whole + tiny[other]
    norm = jnp.sqrt(whole[4:5, 0:1])
    clip = jnp.minimum(1.0, clip_limit / norm)
    stats = total
    for row, number in ((2, clip), (3, whole[0:1, 0:1]), (4, weight_ref[0:1, 0:1]), (5, norm)):
        stats = jnp.where(wide_row == row, number, stats)
    stat_ref[...] = stats

    @pl.when(natural)
    def _():
        @pl.loop(0, chunks)
        def _(i):
            @pl.when(plain_next)
            def _():
                state_copy(xout, ROWS, i, up_one).wait_send()

            if packing:

                @pl.when(packs & (i + SLOTS >= chunks))
                def _():
                    shorter(packed_state, prows, i, lambda copy: copy.wait_send())

            @pl.when(section > 0)
            def _():
                cot_copy(ROWS, i, down_one).wait_send()

    if packing:

        @pl.when(jnp.logical_not(natural))
        def _():
            @pl.loop(0, chunks // 2)
            def _(turn):
                j = 2 * turn + core
                cot_do(prows, j, lambda copy: copy.wait_send())

                @pl.when(swapped(j) + SLOTS >= chunks)
                def _():
                    pair_copy(swapped(j)).wait_send()

                @pl.when(section < sections - 2)
                def _():
                    state_copy(xout, prows, j, up_chip).wait_send()

    for step in range(1, groups):
        weight_copy(step).wait_send()
        small_copy(step).wait_send()
    for step in range(1, sections):
        tiny_copy(step).wait_send()
    for p in pieces:
        out_copy(p).wait()
        for step in range(bits):
            reduce_copy(p, step).wait_send()
            gather_copy(p, step).wait_send()


def rollout(packing, sections, groups, inputs, target, lengths, lat_index, land, w_up, w_down, gains):
    columns, feats = inputs.shape
    chunks = columns // ROWS
    prows = ROWS * (sections - 2) // sections + 16
    grid_rows = columns // LANES
    packed_bytes = 4 * SLOTS * prows * feats
    ring = min((SAVE_BYTES - packed_bytes) // (8 * ROWS * feats), chunks)
    bits = groups.bit_length() - 1
    pieces = 4 * feats // PIECE
    hbm = pl.BlockSpec(memory_space=pl.ANY)
    vmem = pl.BlockSpec(memory_space=pltpu.VMEM)
    dma = pltpu.SemaphoreType.DMA
    wide = pltpu.VMEM((columns, feats), f32)
    lows = pltpu.VMEM((4, feats, feats), bf16)
    flat = lambda array: array.reshape(grid_rows, LANES)
    return pl.pallas_call(
        functools.partial(rollout_kernel, sections, groups, packing),
        out_shape=(
            jax.ShapeDtypeStruct((4, feats, feats), f32),
            jax.ShapeDtypeStruct((8, feats), f32),
            jax.ShapeDtypeStruct((1, 1), jnp.int32),
        ),
        in_specs=[hbm] * 8,
        out_specs=(hbm, vmem, vmem),
        scratch_shapes=[
            wide,
            wide,
            wide,
            wide,
            pltpu.VMEM((SLOTS * prows if packing else 8, feats), f32),
            pltpu.VMEM((max(NEAR * ROWS, 4 * prows), feats), f32),
            pltpu.VMEM((2, ring * ROWS, feats), bf16),
            pltpu.VMEM((2, ring * ROWS, feats), bf16),
            pltpu.VMEM((sections, prows, LANES), f32),
            lows,
            lows,
            lows,
            lows,
            pltpu.VMEM((grid_rows, LANES), f32),
            pltpu.VMEM((2, grid_rows, LANES), f32),
            pltpu.VMEM((8, LANES), f32),
            pltpu.VMEM((8, LANES), f32),
            pltpu.VMEM((8, feats), f32),
            pltpu.VMEM((4, 8, feats), f32),
            pltpu.VMEM((groups, 8, LANES), f32),
            pltpu.VMEM((ROWS, feats), f32),
            pltpu.VMEM((grid_rows, LANES), jnp.int32),
            pltpu.VMEM((grid_rows, LANES), jnp.int32),
            pltpu.VMEM((grid_rows, LANES), jnp.int32),
            pltpu.VMEM((2, 2, feats), f32),
            pltpu.VMEM((8, feats, feats), f32),
            pltpu.VMEM((2, 8, feats), f32),
            pltpu.VMEM((pieces, PIECE, feats), f32),
            pltpu.VMEM((groups, 8, feats), f32),
            pltpu.VMEM((sections, 8, LANES), f32),
            dma((chunks,)),
            dma((chunks,)),
            dma((chunks,)),
            dma((chunks,)),
            dma((chunks,)),
            dma((chunks,)),
            dma((groups,)),
            dma((groups,)),
            dma((pieces * bits,)),
            dma((pieces * bits,)),
            dma((pieces * bits,)),
            dma((pieces * bits,)),
            dma((groups,)),
            dma((groups,)),
            dma((sections,)),
            dma((sections,)),
            dma((pieces,)),
            dma((6,)),
            dma((10,)),
            dma((10,)),
            dma((chunks,)),
            dma((chunks,)),
        ],
        compiler_params=pltpu.CompilerParams(
            collective_id=0 if packing else 1,
            has_side_effects=True,
            vmem_limit_bytes=63 * 1024 * 1024,
        ),
        name="rollout_packed" if packing else "rollout_all",
    )(
        inputs,
        target,
        flat(lengths),
        flat(lat_index),
        flat(land),
        w_up,
        w_down,
        gains,
    )


def adam_step(weights_old, gradient, moment_one, moment_two, decay_rate):
    moment_one = beta_one * moment_one + (1.0 - beta_one) * gradient
    moment_two = beta_two * moment_two + (1.0 - beta_two) * gradient * gradient
    second_hat = moment_two * (1.0 / (1.0 - beta_two**STEP))
    root = second_hat * lax.rsqrt(second_hat)
    pace = moment_one * (learn_rate / (1.0 - beta_one**STEP))
    step = pace * pl.reciprocal(root + adam_eps)
    new_weights = weights_old * (1.0 - learn_rate * decay_rate) - step
    return (new_weights, moment_one, moment_two)


def update_kernel(
    grads_ref,
    stat_hbm,
    w_up,
    w_down,
    gains,
    m_up,
    m_down,
    m_gains,
    v_up,
    v_down,
    v_gains,
    loss_out,
    total_out,
    norm_out,
    new_up,
    new_down,
    new_gains,
    new_m_up,
    new_m_down,
    new_m_gains,
    new_v_up,
    new_v_down,
    new_v_gains,
    held,
    stat_ref,
    gain_ref,
    in_sem,
    out_sem,
    small_in,
    small_out,
):
    old = ((grads_ref, grads_ref), (w_up, w_down), (m_up, m_down), (v_up, v_down))
    new = ((new_up, new_down), (new_m_up, new_m_down), (new_v_up, new_v_down))

    def fetch(i, part):
        source = old[part][i // 2].at[i if part == 0 else i % 2]
        return pltpu.make_async_copy(source, held.at[part, i], in_sem.at[part, i])

    def store(i, part):
        return pltpu.make_async_copy(
            held.at[part + 1, i], new[part][i // 2].at[i % 2], out_sem.at[part, i]
        )

    small_fetch = [pltpu.make_async_copy(stat_hbm, stat_ref, small_in.at[3])]
    small_store = []
    for part, (source, out) in enumerate(
        ((gains, new_gains), (m_gains, new_m_gains), (v_gains, new_v_gains))
    ):
        small_fetch.append(pltpu.make_async_copy(source, gain_ref.at[part], small_in.at[part]))
        small_store.append(pltpu.make_async_copy(gain_ref.at[part], out, small_out.at[part]))
    for copy in small_fetch:
        copy.start()
    for i in range(4):
        for part in range(4):
            fetch(i, part).start()
    for copy in small_fetch:
        copy.wait()
    clip = stat_ref[2:3, 0:1]
    for row, out in ((3, loss_out), (4, total_out), (5, norm_out)):
        out[...] = stat_ref[row : row + 1, 0:1]
    fresh = adam_step(gain_ref[0], stat_ref[0:2] * clip, gain_ref[1], gain_ref[2], 0.0)
    for part in range(3):
        gain_ref[part] = fresh[part]
        small_store[part].start()
    for i in range(4):
        for part in range(4):
            fetch(i, part).wait()
        fresh = adam_step(held[1, i], held[0, i] * clip, held[2, i], held[3, i], weight_decay)
        for part in range(3):
            held[part + 1, i] = fresh[part]
            store(i, part).start()
    for i in range(4):
        for part in range(3):
            store(i, part).wait()
    for copy in small_store:
        copy.wait()


def update(grads, stats, *state):
    hbm = pl.BlockSpec(memory_space=pl.ANY)
    vmem = pl.BlockSpec(memory_space=pltpu.VMEM)
    return pl.pallas_call(
        update_kernel,
        in_specs=[hbm] * 11,
        out_specs=(vmem,) * 3 + (hbm,) * 9,
        out_shape=(jax.ShapeDtypeStruct((1, 1), f32),) * 3
        + tuple(jax.ShapeDtypeStruct(a.shape, f32) for a in state),
        scratch_shapes=[
            pltpu.VMEM((4,) + grads.shape, f32),
            pltpu.VMEM(stats.shape, f32),
            pltpu.VMEM((3,) + state[2].shape, f32),
            pltpu.SemaphoreType.DMA((4, 4)),
            pltpu.SemaphoreType.DMA((3, 4)),
            pltpu.SemaphoreType.DMA((4,)),
            pltpu.SemaphoreType.DMA((3,)),
        ],
        compiler_params=pltpu.CompilerParams(vmem_limit_bytes=63 * 1024 * 1024),
        name="update",
    )(grads, stats, *state)


def per_device(
    inputs,
    targets,
    lengths,
    lat_index,
    land,
    w_up,
    w_down,
    gains,
    m_up,
    m_down,
    m_gains,
    v_up,
    v_down,
    v_gains,
):
    sections, groups = lax.axis_size("section"), lax.axis_size("dp")
    state = tuple(
        a[0] for a in (w_up, w_down, gains, m_up, m_down, m_gains, v_up, v_down, v_gains)
    )
    operands = (inputs, targets[0], lengths, lat_index, land) + state[:3]
    packed = rollout(True, sections, groups, *operands)

    grads, stats, unused = lax.cond(
        packed[2].reshape(()) > 0,
        lambda: rollout(False, sections, groups, *operands),
        lambda: packed,
    )
    new = update(grads, stats, *state)
    return tuple(a.reshape(()) for a in new[:3]) + tuple(a[None] for a in new[3:])


def solution(mesh):
    return jax.shard_map(
        per_device,
        mesh=mesh,
        in_specs=(
            P("dp", None),
            P("section", "dp", None),
            P("dp"),
            P("dp"),
            P("dp"),
            P("section", None, None, None),
            P("section", None, None, None),
            P("section", None, None),
            P("section", None, None, None),
            P("section", None, None, None),
            P("section", None, None),
            P("section", None, None, None),
            P("section", None, None, None),
            P("section", None, None),
        ),
        out_specs=(
            P(),
            P(),
            P(),
            P("section", None, None, None),
            P("section", None, None, None),
            P("section", None, None),
            P("section", None, None, None),
            P("section", None, None, None),
            P("section", None, None),
            P("section", None, None, None),
            P("section", None, None, None),
            P("section", None, None),
        ),
        check_vma=False,
    )
```

```python
import functools
import math

import jax
import jax.numpy as jnp
from jax import lax
from jax.experimental import pallas as pl
from jax.experimental.pallas import tpu as pltpu
from jax.sharding import PartitionSpec as P

NLAT = 128
STEP = 10

norm_eps = 1e-06
clip_limit = 0.05
beta_one = 0.9
beta_two = 0.999
adam_eps = 1e-08
learn_rate = 0.1
weight_decay = 0.01

f32, bf16 = jnp.float32, jnp.bfloat16
MESH = pl.DeviceIdType.MESH
LANES = 128
PIECE = 128
ROWS = 512
SPARE = 80
WINDOW = 1536
SAVE_BYTES = 17 * 1024 * 1024
SLOTS = 10
NEAR = 3


def dot(a, b):
    return jnp.dot(a, b, preferred_element_type=f32)


def dot_lhs_t(a, b):
    return lax.dot_general(a, b, (((0,), (0,)), ((), ())), preferred_element_type=f32)


def split_dot(product, onehot, values):
    high = values.astype(bf16)
    low = (values - high.astype(f32)).astype(bf16)
    return product(onehot, high) + product(onehot, low)


def rollout_kernel(
    sections,
    groups,
    packing,
    inputs_ref,
    target_ref,
    len_hbm,
    lat_hbm,
    land_hbm,
    up_hbm,
    down_hbm,
    gain_hbm,
    grads_ref,
    stat_ref,
    miss_ref,
    xin,
    xout,
    cin,
    tgt,
    packed,
    near,
    save_h,
    save_d,
    qring,
    up_lo,
    up_t,
    down_lo,
    down_t,
    rank_ref,
    area_ref,
    q_ref,
    scale_ref,
    weight_ref,
    loss_acc,
    gain_acc,
    wbuf,
    spread,
    len_ref,
    lat_ref,
    land_ref,
    gain_ref,
    acc,
    gain_land,
    land,
    small,
    tiny,
    in_sem,
    tgt_sem,
    st_send,
    st_recv,
    ct_send,
    ct_recv,
    w_send,
    w_recv,
    rs_send,
    rs_recv,
    ag_send,
    ag_recv,
    small_send,
    small_recv,
    tiny_send,
    tiny_recv,
    out_sem,
    weight_sem,
    mate_send,
    mate_recv,
    pair_send,
    pair_recv,
):
    section = lax.axis_index("section")
    dp = lax.axis_index("dp")
    columns = xin.shape[0]
    feats = xin.shape[1]
    chunks = columns // ROWS
    live_rows = ROWS * (sections - 2) // sections
    prows = live_rows + 16
    total_packed = chunks * prows
    expand = live_rows + 512
    last = sections - 1
    core = lax.rem(section, 2)
    mate = section + 1 - 2 * core
    final = acc.at[pl.ds(4, 4)]
    up_ref, down_ref = acc.at[pl.ds(0, 2)], acc.at[pl.ds(2, 2)]
    ring = save_h.shape[1] // ROWS
    natural = section < (2 if packing else sections)
    plain_next = (section == 0) if packing else (section < last)
    packs = (section == 1) if packing else (section < 0)

    def peer(step):
        return (section, lax.rem(dp + step, groups))

    sources = (up_hbm, down_hbm, gain_hbm, len_hbm, lat_hbm, land_hbm)
    places = (up_ref, down_ref, gain_ref.at[0], len_ref, lat_ref, land_ref)
    fetches = [
        pltpu.make_async_copy(source, place, weight_sem.at[i])
        for i, (source, place) in enumerate(zip(sources, places))
    ]
    for fetch in fetches:
        fetch.start()

    barrier = pltpu.get_barrier_semaphore()
    for step in range(1, sections):
        other = lax.rem(section + step, sections)
        pl.semaphore_signal(barrier, inc=1, device_id=(other, dp), device_id_type=MESH)
    for step in range(1, groups):
        pl.semaphore_signal(barrier, inc=1, device_id=peer(step), device_id_type=MESH)

    def rows_at(index, size, align=16):
        return pl.ds(pl.multiple_of(index, align), size)

    def input_copy(i):
        rows = rows_at(i * ROWS, ROWS)
        return pltpu.make_async_copy(inputs_ref.at[rows], xin.at[rows], in_sem.at[i])

    def target_copy(i):
        rows = rows_at(i * ROWS, ROWS)
        return pltpu.make_async_copy(target_ref.at[rows], tgt.at[rows], tgt_sem.at[i])

    def near_copy(i):
        place = rows_at(lax.rem(i, NEAR) * ROWS, ROWS)
        return pltpu.make_async_copy(
            target_ref.at[rows_at(i * ROWS, ROWS)], near.at[place], tgt_sem.at[i]
        )

    @pl.when(section == 0)
    def _():
        @pl.loop(0, NEAR)
        def _(i):
            input_copy(i).start()

    @pl.when(natural)
    def _():
        @pl.loop(0, NEAR)
        def _(i):
            near_copy(i).start()

    @pl.when(jnp.logical_not(natural))
    def _():
        @pl.loop(0, chunks)
        def _(i):
            target_copy(i).start()

    def prepare_backward():
        for layer in range(2):
            up_t[layer] = up_ref[layer].T.astype(bf16)
            down_t[layer] = (0.5 * down_ref[layer]).T.astype(bf16)
        gain_acc[...] = jnp.zeros_like(gain_acc)
        loss_acc[...] = jnp.zeros_like(loss_acc)
        for i in range(4):
            acc[i] = jnp.zeros((feats, feats), f32)

    def mate_weight(i):
        source = gain_ref.at[0] if i == 4 else acc.at[i]
        place = gain_ref.at[1] if i == 4 else acc.at[4 + i]
        return pltpu.make_async_remote_copy(
            src_ref=source,
            dst_ref=place,
            send_sem=mate_send.at[i],
            recv_sem=mate_recv.at[i],
            device_id=(mate, dp),
            device_id_type=MESH,
        )

    def prepare_mate():
        for i in range(5):
            mate_weight(i).wait_recv()
        for layer in range(2):
            up = acc[4 + layer]
            down = acc[6 + layer]
            up_lo[2 + layer] = (0.5 * up).astype(bf16)
            down_lo[2 + layer] = down.astype(bf16)
            up_t[2 + layer] = up.T.astype(bf16)
            down_t[2 + layer] = (0.5 * down).T.astype(bf16)
        for i in range(4, 8):
            acc[i] = jnp.zeros((feats, feats), f32)

    def mate_gradient(i):
        if i < 4:
            source = acc.at[4 + i]
            place = xin.at[pl.ds(columns - (4 - i) * feats, feats)]
        else:
            source, place = gain_acc.at[pl.ds(2, 2)], gain_land
        return pltpu.make_async_remote_copy(
            src_ref=source,
            dst_ref=place,
            send_sem=mate_send.at[5 + i],
            recv_sem=mate_recv.at[5 + i],
            device_id=(mate, dp),
            device_id_type=MESH,
        )

    def pair_copy(j):
        return pltpu.make_async_remote_copy(
            src_ref=packed.at[slot_rows(j, prows)],
            dst_ref=cin.at[rows_at(swapped(j) * prows, prows)],
            send_sem=pair_send.at[j],
            recv_sem=pair_recv.at[j],
            device_id=(mate, dp),
            device_id_type=MESH,
        )

    def slot_rows(j, count):
        return rows_at(lax.rem(j, SLOTS) * prows, count)

    def swapped(j):
        return j + 1 - 2 * lax.rem(j, 2)

    grid_rows = columns // LANES
    tile_row = lax.broadcasted_iota(jnp.int32, (8, LANES), 0)

    def window_start(j):
        shift = jnp.where(j < 7, 0, jnp.where(j < 11, 256, 384))
        return jnp.clip(ROWS * (j - 1) + shift, 0, columns - WINDOW)

    def expand_start(k):
        end = live_rows * k + expand - 288
        end = jnp.where(k >= 11, jnp.minimum(end, prows * (k + 1)), end)
        return jnp.clip(end - expand, 0, total_packed - expand)

    def chunks_for(k):
        return (expand_start(k) + expand - 1) // prows

    def weight_copy(step):
        return pltpu.make_async_remote_copy(
            src_ref=wbuf.at[dp],
            dst_ref=wbuf.at[dp],
            send_sem=w_send.at[step],
            recv_sem=w_recv.at[step],
            device_id=peer(step),
            device_id_type=MESH,
        )

    def prepare_columns():
        length = len_ref[...]
        latitude = (lat_ref[...].astype(f32) + 0.5) * (math.pi / NLAT) - math.pi / 2
        area = jnp.cos(latitude) * (1.0 + land_ref[...].astype(f32))
        q_ref[0] = area * (section < length).astype(f32)
        q_ref[1] = area * (mate < length).astype(f32)
        area_ref[...] = area
        if packing:
            beyond = length > 2
            flag = beyond.astype(bf16)
            lane_a = lax.broadcasted_iota(jnp.int32, (LANES, LANES), 0)
            lane_b = lax.broadcasted_iota(jnp.int32, (LANES, LANES), 1)
            within = dot(flag, (lane_a < lane_b).astype(bf16))
            row_total = jnp.sum(flag.astype(f32), axis=1, keepdims=True)
            row_a = lax.broadcasted_iota(jnp.int32, (grid_rows, grid_rows), 0)
            row_b = lax.broadcasted_iota(jnp.int32, (grid_rows, grid_rows), 1)
            before = dot(
                (row_b < row_a).astype(bf16),
                jnp.broadcast_to(row_total, (grid_rows, LANES)).astype(bf16),
            )
            rank = jnp.where(beyond, within + before, -1e6)
            rank_ref[...] = rank

    def prepare_totals():
        length = len_ref[...]
        local_weight = jnp.sum(
            area_ref[...] * jnp.minimum(length, sections).astype(f32), axis=(0, 1), keepdims=True
        )
        misses = jnp.zeros((1, 1), f32)
        if packing:
            beyond = length > 2
            rank = rank_ref[...]
            place = (
                lax.broadcasted_iota(jnp.int32, (grid_rows, LANES), 0) * LANES
                + lax.broadcasted_iota(jnp.int32, (grid_rows, LANES), 1)
            )
            rank_i = rank.astype(jnp.int32)
            missed = beyond & (rank_i >= total_packed - SPARE)
            for j in range(chunks):
                shift = 0 if j < 7 else 256 if j < 11 else 384
                start = min(max(ROWS * (j - 1) + shift, 0), columns - WINDOW)
                member = (rank_i >= j * prows) & (rank_i < (j + 1) * prows)
                ready = ROWS * (j + 2 if j < 7 else j + 3)
                missed |= member & ((place < start) | (place >= min(start + WINDOW, ready)))
            row_chunk = lax.broadcasted_iota(jnp.int32, (grid_rows, LANES), 0) // (ROWS // LANES)
            row_start = expand_start(row_chunk)
            missed |= beyond & ((rank_i < row_start) | (rank_i >= row_start + expand))
            misses = jnp.sum(missed.astype(f32), axis=(0, 1), keepdims=True)
        wbuf[dp] = jnp.where(tile_row < 4, local_weight, misses)
        for step in range(1, groups):
            weight_copy(step).start()

    def finish_weights():
        for step in range(1, groups):
            weight_copy(step).wait_recv()
        total = wbuf[0]
        for other in range(1, groups):
            total = total + wbuf[other]
        weight_ref[...] = total
        miss_ref[...] = (total[4:5, 0:1] > 0.0).astype(jnp.int32)
        scale_ref[...] = 2.0 / jnp.broadcast_to(total[0:1], (8, LANES))

    for fetch in fetches:
        fetch.wait()
    for layer in range(2):
        up_lo[layer] = (0.5 * up_ref[layer]).astype(bf16)
        down_lo[layer] = down_ref[layer].astype(bf16)
    pl.semaphore_wait(barrier, sections - 1 + groups - 1)

    def pack_matrix(j):
        start = window_start(j)
        base = (j * prows).astype(f32)
        target_row = lax.broadcasted_iota(jnp.int32, (prows, LANES), 0).astype(f32)
        first = start // LANES
        hits = []
        for i in range(WINDOW // LANES):
            hits.append(target_row == rank_ref[pl.ds(first + i, 1), :] - base)
        return start, first, hits

    def as_onehot(hits):
        return jnp.concatenate([jnp.where(hit, 1.0, 0.0).astype(bf16) for hit in hits], axis=1)

    def unpack_rows(k):
        start = expand_start(k)
        base = start.astype(f32)
        source_row = lax.broadcasted_iota(jnp.int32, (expand, LANES), 0).astype(f32)
        hits = []
        for i in range(ROWS // LANES):
            hits.append(source_row == rank_ref[pl.ds(k * (ROWS // LANES) + i, 1), :] - base)
        return dot_lhs_t(as_onehot(hits), cin[rows_at(start, expand), :].astype(bf16))

    def forward(source, place, owner, saved, keep):
        x = source[...]
        for layer in range(2):
            if layer == 1:
                keep[...] = x
            r = lax.rsqrt(jnp.mean(x * x, -1, keepdims=True) + norm_eps)
            normed = (x * r * gain_ref[owner, layer : layer + 1]).astype(bf16)
            half = dot(normed, up_lo[2 * owner + layer])
            t = jnp.tanh(half)
            a = 1.0 + t
            h = half * a
            hidden = h.astype(bf16)
            save_h[layer, saved, :] = hidden
            save_d[layer, saved, :] = (a + h * (1.0 - t)).astype(bf16)
            x = x + dot(hidden, down_lo[2 * owner + layer])
        place[...] = x

    def loss_part(size, diff, weight):
        weighted = jnp.concatenate(
            [diff[:, :LANES] * weight, diff[:, LANES:] * weight], axis=1
        )
        loss_acc[...] += jnp.sum((weighted * diff).reshape(size // 8, 8, feats), 0)
        return weighted * scale_ref[0:1, 0:1]

    def backward(size, source, place, owner, saved, keep, g):
        for layer in (1, 0):
            low = g.astype(bf16)
            acc[4 * owner + 2 + layer] += dot_lhs_t(save_h[layer, saved, :], low)
            pull = dot(low, down_t[2 * owner + layer])
            g_pre = (pull * save_d[layer, saved, :].astype(f32)).astype(bf16)
            x = keep[...] if layer == 1 else source[...]
            r = lax.rsqrt(jnp.mean(x * x, -1, keepdims=True) + norm_eps)
            gain = gain_ref[owner, layer : layer + 1]
            xr = x * r
            normed = (xr * gain).astype(bf16)
            acc[4 * owner + layer] += dot_lhs_t(normed, g_pre)
            g_normed = dot(g_pre, up_t[2 * owner + layer])
            prod = g_normed * xr
            gain_acc[2 * owner + layer] += jnp.sum(prod.reshape(size // 8, 8, feats), 0)
            mean = jnp.mean(prod * gain, -1, keepdims=True)
            g = g + r * (gain * g_normed - xr * mean)
        place[...] = g

    def state_copy(source, size, i, to, count=None):
        rows = rows_at(i * size, size if count is None else count)
        return pltpu.make_async_remote_copy(
            src_ref=source.at[rows],
            dst_ref=xin.at[rows],
            send_sem=st_send.at[i],
            recv_sem=st_recv.at[i],
            device_id=(to, dp),
            device_id_type=MESH,
        )

    def cot_copy(size, i, to, count=None):
        rows = rows_at(i * size, size if count is None else count)
        return pltpu.make_async_remote_copy(
            src_ref=xin.at[rows],
            dst_ref=cin.at[rows],
            send_sem=ct_send.at[i],
            recv_sem=ct_recv.at[i],
            device_id=(to, dp),
            device_id_type=MESH,
        )

    up_one = lax.rem(section + 1, sections)
    down_one = lax.rem(section + sections - 1, sections)
    up_chip = lax.rem(section + 2, sections)
    down_chip = jnp.where(section < 4, 1, section - 2)

    def shorter(copy, size, i, action):
        @pl.when(i < chunks - 1)
        def _():
            action(copy(size, i, size))

        @pl.when(i == chunks - 1)
        def _():
            action(copy(size, i, size - SPARE))

    def packed_state(size, i, count):
        return pltpu.make_async_remote_copy(
            src_ref=packed.at[slot_rows(i, count)],
            dst_ref=xin.at[rows_at(i * size, count)],
            send_sem=st_send.at[i],
            recv_sem=st_recv.at[i],
            device_id=(2 + lax.rem(i, 2), dp),
            device_id_type=MESH,
        )

    def packed_receive(size, i):
        @pl.when(section < 4)
        def _():
            shorter(packed_state, size, i, lambda copy: copy.wait_recv())

        @pl.when(section >= 4)
        def _():
            state_copy(xout, size, i, up_chip).wait_recv()

    def cot_part(size, i, count):
        return cot_copy(size, i, down_chip, count)

    def cot_wait(size, i):
        shorter(cot_part, size, i, lambda copy: copy.wait_recv())

    def cot_do(size, i, action):
        @pl.when(section < 4)
        def _():
            shorter(cot_part, size, i, action)

        @pl.when(section >= 4)
        def _():
            action(cot_copy(size, i, down_chip))

    @pl.when(natural)
    def _():
        if packing:
            most = chunks if ring == chunks else ring - 1
            lag = jnp.where(section == 0, most, most - 2)
        else:
            lag = jnp.minimum(ring - 1, 3 * (last - section))

        @pl.when(section > 0)
        def _():
            prepare_columns()
            if not packing:
                prepare_totals()
            if packing:
                xout[2 * ROWS : WINDOW, :] = jnp.zeros((WINDOW - 2 * ROWS, feats), f32)
                cin[total_packed - SPARE : total_packed, :] = jnp.zeros((SPARE, feats), f32)

        @pl.loop(0, chunks + lag)
        def _(t):
            @pl.when(t < chunks)
            def _():
                @pl.when(section == 0)
                def _():
                    input_copy(t).wait()

                    @pl.when(t + NEAR < chunks)
                    def _():
                        input_copy(t + NEAR).start()

                @pl.when(section > 0)
                def _():
                    state_copy(xout, ROWS, t, up_one).wait_recv()

                rows = rows_at(t * ROWS, ROWS)
                saved = rows_at(lax.rem(t, ring) * ROWS, ROWS)
                forward(xin.at[rows], xout.at[rows], 0, saved, tgt.at[saved])

                @pl.when(plain_next)
                def _():
                    state_copy(xout, ROWS, t, up_one).start()

            if packing:

                j = jnp.where(t < 8, t - 1, t - 2)

                @pl.when(packs & (t >= 1) & (t != 8) & (j < chunks))
                def _():
                    start, _, hits = pack_matrix(j)

                    @pl.when(j >= SLOTS)
                    def _():
                        shorter(packed_state, prows, j - SLOTS, lambda copy: copy.wait_send())

                    packed[slot_rows(j, prows), :] = split_dot(
                        dot, as_onehot(hits), xout[rows_at(start, WINDOW), :]
                    )
                    shorter(packed_state, prows, j, lambda copy: copy.start())

            @pl.when((section == 0) & (t == 3))
            def _():
                prepare_columns()
                if not packing:
                    prepare_totals()

            if packing:

                @pl.when(t == 3)
                def _():
                    prepare_totals()

            @pl.when(t == jnp.minimum(lag, 4))
            def _():
                prepare_backward()

            k = t - lag

            @pl.when((k >= 0) & (k < chunks))
            def _():
                @pl.when(k == 0)
                def _():
                    finish_weights()

                near_copy(k).wait()
                rows = rows_at(k * ROWS, ROWS)
                place = rows_at(lax.rem(k, NEAR) * ROWS, ROWS)
                saved = rows_at(lax.rem(k, ring) * ROWS, ROWS)

                weight = jnp.concatenate(
                    [
                        jnp.broadcast_to(
                            q_ref[0, pl.ds(k * (ROWS // LANES) + i, 1), :], (LANES, LANES)
                        ).T
                        for i in range(ROWS // LANES)
                    ],
                    axis=0,
                )
                diff = xout[rows, :] - near[place, :]
                spread[...] = loss_part(ROWS, diff, weight)

                @pl.when(k + NEAR < chunks)
                def _():
                    near_copy(k + NEAR).start()

                @pl.when(plain_next)
                def _():
                    cot_copy(ROWS, k, down_one).wait_recv()
                    spread[...] += cin[rows, :]

                if packing:

                    @pl.when(packs)
                    def _():
                        had = jnp.where(k == 0, -1, chunks_for(jnp.maximum(k - 1, 0)))
                        for i in range(3):

                            @pl.when(had + 1 + i <= chunks_for(k))
                            def _():
                                cot_wait(prows, had + 1 + i)

                        spread[...] += unpack_rows(k)

                backward(ROWS, xin.at[rows], xin.at[rows], 0, saved, tgt.at[saved], spread[...])

                @pl.when(section > 0)
                def _():
                    cot_copy(ROWS, k, down_one).start()

    if packing:

        @pl.when(jnp.logical_not(natural))
        def _():
            turns = chunks // 2
            final_chip = section >= sections - 2
            lag = jnp.where(final_chip, 0, 1)
            for i in range(5):
                mate_weight(i).start()
            prepare_columns()
            prepare_totals()
            for i in range(5):
                mate_weight(i).wait_send()
            prepare_backward()
            prepare_mate()

            @pl.when(section < 4)
            def _():
                xin[total_packed - SPARE : total_packed, :] = jnp.zeros((SPARE, feats), f32)

            def pack_target(j):
                start, first, hits = pack_matrix(j)
                packed[slot_rows(j, prows), :] = split_dot(
                    dot, as_onehot(hits), tgt[rows_at(start, WINDOW), :]
                )
                return first, hits

            def places(turn):
                j = 2 * turn + core
                slot = 2 * lax.rem(turn, 2)
                rows, other = rows_at(j * prows, prows), rows_at(swapped(j) * prows, prows)
                saved = [rows_at((slot + part) * ROWS, prows) for part in range(2)]
                keep = [near.at[rows_at((slot + part) * prows, prows)] for part in range(2)]
                return j, slot, rows, other, saved, keep

            @pl.loop(0, turns + lag)
            def _(turn):
                @pl.when(turn < turns)
                def _():
                    @pl.when(turn == 0)
                    def _():
                        target_copy(0).wait()
                        target_copy(1).wait()

                    for i in range(2, 4):

                        @pl.when(2 * turn + i < chunks)
                        def _():
                            target_copy(2 * turn + i).wait()

                    j, slot, rows, other, saved, keep = places(turn)

                    @pl.when(swapped(j) >= SLOTS)
                    def _():
                        pair_copy(swapped(j) - SLOTS).wait_send()

                    pack_target(swapped(j))
                    pair_copy(swapped(j)).start()
                    first, hits = pack_target(j)
                    for part in range(2):
                        owner = jnp.where(core == part, 0, 1)
                        weight = jnp.zeros((prows, LANES), f32)
                        for i, hit in enumerate(hits):
                            weight += jnp.where(hit, q_ref[owner, pl.ds(first + i, 1), :], 0.0)
                        qring[slot + part] = jnp.broadcast_to(
                            jnp.sum(weight, -1, keepdims=True), (prows, LANES)
                        )
                    packed_receive(prows, j)
                    forward(xin.at[rows], xout.at[other], core, saved[0], keep[0])
                    forward(xout.at[other], xout.at[rows], 1 - core, saved[1], keep[1])

                    @pl.when(jnp.logical_not(final_chip))
                    def _():
                        state_copy(xout, prows, j, up_chip).start()

                @pl.when(turn >= lag)
                def _():
                    @pl.when(turn == lag)
                    def _():
                        finish_weights()

                    j, slot, rows, other, saved, keep = places(turn - lag)
                    part_rows = pl.ds(0, prows)
                    pair_copy(j).wait_recv()

                    def error(part, out):
                        here = core == part
                        target = jnp.where(here, packed[slot_rows(j, prows), :], cin[other, :])
                        return loss_part(prows, out - target, qring[slot + part])

                    spread[part_rows, :] = error(1, xout[rows, :])

                    @pl.when(jnp.logical_not(final_chip))
                    def _():
                        cot_copy(prows, j, down_chip).wait_recv()
                        spread[part_rows, :] += cin[rows, :]

                    backward(
                        prows,
                        xout.at[other],
                        spread.at[part_rows],
                        1 - core,
                        saved[1],
                        keep[1],
                        spread[part_rows, :],
                    )
                    g = error(0, xout[other, :]) + spread[part_rows, :]
                    backward(prows, xin.at[rows], xin.at[rows], core, saved[0], keep[0], g)
                    cot_do(prows, j, lambda copy: copy.start())

            for i in range(5):
                mate_gradient(i).start()
            for i in range(5):
                mate_gradient(i).wait_recv()
                if i < 4:
                    acc[i] += xin[columns - (4 - i) * feats : columns - (3 - i) * feats, :]
                else:
                    gain_acc[0:2] += gain_land[...]
            for i in range(5):
                mate_gradient(i).wait_send()

    bits = groups.bit_length() - 1
    halves = feats // PIECE
    pieces = range(4 * halves)
    matrix = [m for m in (3, 1, 2, 0) for _ in range(halves)]
    first = [PIECE * (p % halves) for p in pieces]

    def bit_order(p):
        order = list(range(bits))
        if p % 2 == 0:
            order.insert(0, order.pop(min(2 - p % 4 // 2, bits - 1)))
        return order

    def bit_value(bit):
        return lax.rem(dp // 2**bit, 2)

    def kept_start(p, step):
        start = 0
        for i in range(step):
            start = start + bit_value(bit_order(p)[i]) * (PIECE >> (i + 1))
        return start

    def across(p, step):
        bit = bit_order(p)[step]
        return (section, dp + (1 - 2 * bit_value(bit)) * 2**bit)

    def reduce_copy(p, step):
        size = PIECE >> (step + 1)
        away = 1 - bit_value(bit_order(p)[step])
        start = kept_start(p, step) + away * size
        if step == 0:
            source = acc.at[matrix[p], rows_at(first[p] + start, size, 8)]
        else:
            source = near.at[rows_at(p * PIECE + start, size, 8)]
        return pltpu.make_async_remote_copy(
            src_ref=source,
            dst_ref=land.at[p, pl.ds(PIECE - (PIECE >> step), size)],
            send_sem=rs_send.at[p * bits + step],
            recv_sem=rs_recv.at[p * bits + step],
            device_id=across(p, step),
            device_id_type=MESH,
        )

    def reduce_add(p, step):
        size = PIECE >> (step + 1)
        start = kept_start(p, step + 1)
        if step == 0:
            own = acc[matrix[p], rows_at(first[p] + start, size, 8), :]
        else:
            own = near[rows_at(p * PIECE + start, size, 8), :]
        own = own + land[p, PIECE - (PIECE >> step) : PIECE - (PIECE >> (step + 1)), :]
        if step == bits - 1:
            final[matrix[p], rows_at(first[p] + start, size, 8), :] = own
        else:
            near[rows_at(p * PIECE + start, size, 8), :] = own
        return own

    def gather_copy(p, step):
        rows = rows_at(first[p] + kept_start(p, step + 1), PIECE >> (step + 1), 8)
        return pltpu.make_async_remote_copy(
            src_ref=final.at[matrix[p], rows],
            dst_ref=final.at[matrix[p], rows],
            send_sem=ag_send.at[p * bits + step],
            recv_sem=ag_recv.at[p * bits + step],
            device_id=across(p, step),
            device_id_type=MESH,
        )

    def small_copy(step):
        return pltpu.make_async_remote_copy(
            src_ref=small.at[dp],
            dst_ref=small.at[dp],
            send_sem=small_send.at[step],
            recv_sem=small_recv.at[step],
            device_id=peer(step),
            device_id_type=MESH,
        )

    def tiny_copy(step):
        return pltpu.make_async_remote_copy(
            src_ref=tiny.at[section],
            dst_ref=tiny.at[section],
            send_sem=tiny_send.at[step],
            recv_sem=tiny_recv.at[step],
            device_id=(lax.rem(section + step, sections), dp),
            device_id_type=MESH,
        )

    def out_copy(p):
        rows = pl.ds(first[p], PIECE)
        return pltpu.make_async_copy(
            final.at[matrix[p], rows], grads_ref.at[matrix[p], rows], out_sem.at[p]
        )

    for p in pieces:
        reduce_copy(p, 0).start()
    squares = jnp.zeros((1, 1), f32)
    for step in range(bits):
        for p in pieces:
            reduce_copy(p, step).wait_recv()
            own = reduce_add(p, step)
            if step < bits - 1:
                reduce_copy(p, step + 1).start()
            else:
                gather_copy(p, step).start()
                squares = squares + jnp.sum(own * own, axis=(0, 1), keepdims=True)
    loss = jnp.sum(loss_acc[...], axis=(0, 1), keepdims=True)
    wide_row = lax.broadcasted_iota(jnp.int32, (8, feats), 0)
    small[dp] = jnp.where(
        wide_row == 0,
        jnp.sum(gain_acc[0], 0, keepdims=True),
        jnp.where(
            wide_row == 1,
            jnp.sum(gain_acc[1], 0, keepdims=True),
            jnp.where(wide_row < 4, loss, squares),
        ),
    )
    for step in range(1, groups):
        small_copy(step).start()
    for step in range(bits - 1, 0, -1):
        for p in pieces:
            gather_copy(p, step).wait_recv()
            gather_copy(p, step - 1).start()
    for step in range(1, groups):
        small_copy(step).wait_recv()
    total = small[0]
    for other in range(1, groups):
        total = total + small[other]
    gain_squares = jnp.sum(total[0:2] * total[0:2], axis=(0, 1), keepdims=True)
    tiny[section] = jnp.where(tile_row < 4, total[2:3, 0:1], total[4:5, 0:1] + gain_squares)
    for step in range(1, sections):
        tiny_copy(step).start()
    for p in pieces:
        gather_copy(p, 0).wait_recv()
        out_copy(p).start()
    for step in range(1, sections):
        tiny_copy(step).wait_recv()
    whole = tiny[0]
    for other in range(1, sections):
        whole = whole + tiny[other]
    norm = jnp.sqrt(whole[4:5, 0:1])
    clip = jnp.minimum(1.0, clip_limit / norm)
    stats = total
    for row, number in ((2, clip), (3, whole[0:1, 0:1]), (4, weight_ref[0:1, 0:1]), (5, norm)):
        stats = jnp.where(wide_row == row, number, stats)
    stat_ref[...] = stats

    @pl.when(natural)
    def _():
        @pl.loop(0, chunks)
        def _(i):
            @pl.when(plain_next)
            def _():
                state_copy(xout, ROWS, i, up_one).wait_send()

            if packing:

                @pl.when(packs & (i + SLOTS >= chunks))
                def _():
                    shorter(packed_state, prows, i, lambda copy: copy.wait_send())

            @pl.when(section > 0)
            def _():
                cot_copy(ROWS, i, down_one).wait_send()

    if packing:

        @pl.when(jnp.logical_not(natural))
        def _():
            @pl.loop(0, chunks // 2)
            def _(turn):
                j = 2 * turn + core
                cot_do(prows, j, lambda copy: copy.wait_send())

                @pl.when(swapped(j) + SLOTS >= chunks)
                def _():
                    pair_copy(swapped(j)).wait_send()

                @pl.when(section < sections - 2)
                def _():
                    state_copy(xout, prows, j, up_chip).wait_send()

    for step in range(1, groups):
        weight_copy(step).wait_send()
        small_copy(step).wait_send()
    for step in range(1, sections):
        tiny_copy(step).wait_send()
    for p in pieces:
        out_copy(p).wait()
        for step in range(bits):
            reduce_copy(p, step).wait_send()
            gather_copy(p, step).wait_send()


def rollout(packing, sections, groups, inputs, target, lengths, lat_index, land, w_up, w_down, gains):
    columns, feats = inputs.shape
    chunks = columns // ROWS
    prows = ROWS * (sections - 2) // sections + 16
    grid_rows = columns // LANES
    packed_bytes = 4 * SLOTS * prows * feats
    ring = min((SAVE_BYTES - packed_bytes) // (8 * ROWS * feats), chunks)
    bits = groups.bit_length() - 1
    pieces = 4 * feats // PIECE
    hbm = pl.BlockSpec(memory_space=pl.ANY)
    vmem = pl.BlockSpec(memory_space=pltpu.VMEM)
    dma = pltpu.SemaphoreType.DMA
    wide = pltpu.VMEM((columns, feats), f32)
    lows = pltpu.VMEM((4, feats, feats), bf16)
    flat = lambda array: array.reshape(grid_rows, LANES)
    return pl.pallas_call(
        functools.partial(rollout_kernel, sections, groups, packing),
        out_shape=(
            jax.ShapeDtypeStruct((4, feats, feats), f32),
            jax.ShapeDtypeStruct((8, feats), f32),
            jax.ShapeDtypeStruct((1, 1), jnp.int32),
        ),
        in_specs=[hbm] * 8,
        out_specs=(hbm, vmem, vmem),
        scratch_shapes=[
            wide,
            wide,
            wide,
            wide,
            pltpu.VMEM((SLOTS * prows if packing else 8, feats), f32),
            pltpu.VMEM((max(NEAR * ROWS, 4 * prows), feats), f32),
            pltpu.VMEM((2, ring * ROWS, feats), bf16),
            pltpu.VMEM((2, ring * ROWS, feats), bf16),
            pltpu.VMEM((sections, prows, LANES), f32),
            lows,
            lows,
            lows,
            lows,
            pltpu.VMEM((grid_rows, LANES), f32),
            pltpu.VMEM((grid_rows, LANES), f32),
            pltpu.VMEM((2, grid_rows, LANES), f32),
            pltpu.VMEM((8, LANES), f32),
            pltpu.VMEM((8, LANES), f32),
            pltpu.VMEM((8, feats), f32),
            pltpu.VMEM((4, 8, feats), f32),
            pltpu.VMEM((groups, 8, LANES), f32),
            pltpu.VMEM((ROWS, feats), f32),
            pltpu.VMEM((grid_rows, LANES), jnp.int32),
            pltpu.VMEM((grid_rows, LANES), jnp.int32),
            pltpu.VMEM((grid_rows, LANES), jnp.int32),
            pltpu.VMEM((2, 2, feats), f32),
            pltpu.VMEM((8, feats, feats), f32),
            pltpu.VMEM((2, 8, feats), f32),
            pltpu.VMEM((pieces, PIECE, feats), f32),
            pltpu.VMEM((groups, 8, feats), f32),
            pltpu.VMEM((sections, 8, LANES), f32),
            dma((chunks,)),
            dma((chunks,)),
            dma((chunks,)),
            dma((chunks,)),
            dma((chunks,)),
            dma((chunks,)),
            dma((groups,)),
            dma((groups,)),
            dma((pieces * bits,)),
            dma((pieces * bits,)),
            dma((pieces * bits,)),
            dma((pieces * bits,)),
            dma((groups,)),
            dma((groups,)),
            dma((sections,)),
            dma((sections,)),
            dma((pieces,)),
            dma((6,)),
            dma((10,)),
            dma((10,)),
            dma((chunks,)),
            dma((chunks,)),
        ],
        compiler_params=pltpu.CompilerParams(
            collective_id=0 if packing else 1,
            has_side_effects=True,
            vmem_limit_bytes=63 * 1024 * 1024,
        ),
        name="rollout_packed" if packing else "rollout_all",
    )(
        inputs,
        target,
        flat(lengths),
        flat(lat_index),
        flat(land),
        w_up,
        w_down,
        gains,
    )


def adam_step(weights_old, gradient, moment_one, moment_two, decay_rate):
    moment_one = beta_one * moment_one + (1.0 - beta_one) * gradient
    moment_two = beta_two * moment_two + (1.0 - beta_two) * gradient * gradient
    second_hat = moment_two * (1.0 / (1.0 - beta_two**STEP))
    root = second_hat * lax.rsqrt(second_hat)
    pace = moment_one * (learn_rate / (1.0 - beta_one**STEP))
    step = pace * pl.reciprocal(root + adam_eps)
    new_weights = weights_old * (1.0 - learn_rate * decay_rate) - step
    return (new_weights, moment_one, moment_two)


def update_kernel(
    grads_ref,
    stat_hbm,
    w_up,
    w_down,
    gains,
    m_up,
    m_down,
    m_gains,
    v_up,
    v_down,
    v_gains,
    loss_out,
    total_out,
    norm_out,
    new_up,
    new_down,
    new_gains,
    new_m_up,
    new_m_down,
    new_m_gains,
    new_v_up,
    new_v_down,
    new_v_gains,
    held,
    stat_ref,
    gain_ref,
    in_sem,
    out_sem,
    small_in,
    small_out,
):
    old = ((grads_ref, grads_ref), (w_up, w_down), (m_up, m_down), (v_up, v_down))
    new = ((new_up, new_down), (new_m_up, new_m_down), (new_v_up, new_v_down))

    def fetch(i, part):
        source = old[part][i // 2].at[i if part == 0 else i % 2]
        return pltpu.make_async_copy(source, held.at[part, i], in_sem.at[part, i])

    def store(i, part):
        return pltpu.make_async_copy(
            held.at[part + 1, i], new[part][i // 2].at[i % 2], out_sem.at[part, i]
        )

    small_fetch = [pltpu.make_async_copy(stat_hbm, stat_ref, small_in.at[3])]
    small_store = []
    for part, (source, out) in enumerate(
        ((gains, new_gains), (m_gains, new_m_gains), (v_gains, new_v_gains))
    ):
        small_fetch.append(pltpu.make_async_copy(source, gain_ref.at[part], small_in.at[part]))
        small_store.append(pltpu.make_async_copy(gain_ref.at[part], out, small_out.at[part]))
    for copy in small_fetch:
        copy.start()
    for i in range(4):
        for part in range(4):
            fetch(i, part).start()
    for copy in small_fetch:
        copy.wait()
    clip = stat_ref[2:3, 0:1]
    for row, out in ((3, loss_out), (4, total_out), (5, norm_out)):
        out[...] = stat_ref[row : row + 1, 0:1]
    fresh = adam_step(gain_ref[0], stat_ref[0:2] * clip, gain_ref[1], gain_ref[2], 0.0)
    for part in range(3):
        gain_ref[part] = fresh[part]
        small_store[part].start()
    for i in range(4):
        for part in range(4):
            fetch(i, part).wait()
        fresh = adam_step(held[1, i], held[0, i] * clip, held[2, i], held[3, i], weight_decay)
        for part in range(3):
            held[part + 1, i] = fresh[part]
            store(i, part).start()
    for i in range(4):
        for part in range(3):
            store(i, part).wait()
    for copy in small_store:
        copy.wait()


def update(grads, stats, *state):
    hbm = pl.BlockSpec(memory_space=pl.ANY)
    vmem = pl.BlockSpec(memory_space=pltpu.VMEM)
    return pl.pallas_call(
        update_kernel,
        in_specs=[hbm] * 11,
        out_specs=(vmem,) * 3 + (hbm,) * 9,
        out_shape=(jax.ShapeDtypeStruct((1, 1), f32),) * 3
        + tuple(jax.ShapeDtypeStruct(a.shape, f32) for a in state),
        scratch_shapes=[
            pltpu.VMEM((4,) + grads.shape, f32),
            pltpu.VMEM(stats.shape, f32),
            pltpu.VMEM((3,) + state[2].shape, f32),
            pltpu.SemaphoreType.DMA((4, 4)),
            pltpu.SemaphoreType.DMA((3, 4)),
            pltpu.SemaphoreType.DMA((4,)),
            pltpu.SemaphoreType.DMA((3,)),
        ],
        compiler_params=pltpu.CompilerParams(vmem_limit_bytes=63 * 1024 * 1024),
        name="update",
    )(grads, stats, *state)


def per_device(
    inputs,
    targets,
    lengths,
    lat_index,
    land,
    w_up,
    w_down,
    gains,
    m_up,
    m_down,
    m_gains,
    v_up,
    v_down,
    v_gains,
):
    sections, groups = lax.axis_size("section"), lax.axis_size("dp")
    state = tuple(
        a[0] for a in (w_up, w_down, gains, m_up, m_down, m_gains, v_up, v_down, v_gains)
    )
    operands = (inputs, targets[0], lengths, lat_index, land) + state[:3]
    packed = rollout(True, sections, groups, *operands)

    grads, stats, unused = lax.switch(
        packed[2].reshape(()),
        (lambda: packed, lambda: rollout(False, sections, groups, *operands)),
    )
    new = update(grads, stats, *state)
    return tuple(a.reshape(()) for a in new[:3]) + tuple(a[None] for a in new[3:])


def solution(mesh):
    return jax.shard_map(
        per_device,
        mesh=mesh,
        in_specs=(
            P("dp", None),
            P("section", "dp", None),
            P("dp"),
            P("dp"),
            P("dp"),
            P("section", None, None, None),
            P("section", None, None, None),
            P("section", None, None),
            P("section", None, None, None),
            P("section", None, None, None),
            P("section", None, None),
            P("section", None, None, None),
            P("section", None, None, None),
            P("section", None, None),
        ),
        out_specs=(
            P(),
            P(),
            P(),
            P("section", None, None, None),
            P("section", None, None, None),
            P("section", None, None),
            P("section", None, None, None),
            P("section", None, None, None),
            P("section", None, None),
            P("section", None, None, None),
            P("section", None, None, None),
            P("section", None, None),
        ),
        check_vma=False,
    )
```
